32 devices in a mesh: dp: 8 (over z, x), mp: 4 (over y, core).
Axes of the slice: x: 2, y: 2, z: 4, core: 2. Of those that a mesh axis runs over, the one named last changes fastest.
Arguments:
- tokens: bfloat16 [11040, 1024], P(('dp', 'mp')), may hold values from -6 to 6
- cotangent: bfloat16 [11040, 1024], P(('dp', 'mp')), may hold values from -6 to 6
- crop_lengths: int32 [16, 10], P('dp'), may hold values from 37 to 197, as said below
- qkv_weight: float32 [1024, 3, 1024], P('dp', None, 'mp'), may hold values from -0.25 to 0.25
- out_weight: float32 [1024, 1024], P('dp', 'mp'), may hold values from -0.5 to 0.5
- up_weight: float32 [1024, 4096], P('dp', 'mp'), may hold values from -0.1875 to 0.1875
- down_weight: float32 [1024, 4096], P('dp', 'mp'), may hold values from -0.09375 to 0.09375
- vectors: float32 [6, 1024], P(None, ('dp', 'mp')), may hold values from 0.25 to 1.75
- qkv_first: float32 [1024, 3, 1024], P('dp', None, 'mp'), may hold values from -96 to 96
- out_first: float32 [1024, 1024], P('dp', 'mp'), may hold values from -64 to 64
- up_first: float32 [1024, 4096], P('dp', 'mp'), may hold values from -40 to 40
- down_first: float32 [1024, 4096], P('dp', 'mp'), may hold values from -64 to 64
- vector_first: float32 [6, 1024], P(None, ('dp', 'mp')), may hold values from -64 to 64
- qkv_second: float32 [1024, 3, 1024], P('dp', None, 'mp'), may hold values from 22.08 to 88.32
- out_second: float32 [1024, 1024], P('dp', 'mp'), may hold values from 11.04 to 44.16
- up_second: float32 [1024, 4096], P('dp', 'mp'), may hold values from 3.312 to 13.248
- down_second: float32 [1024, 4096], P('dp', 'mp'), may hold values from 11.04 to 44.16
- vector_second: float32 [6, 1024], P(None, ('dp', 'mp')), may hold values from 11.04 to 44.16
Outputs:
- output: bfloat16 [11040, 1024], P(('dp', 'mp'))
- input_grad: bfloat16 [11040, 1024], P(('dp', 'mp'))
- qkv_new: float32 [1024, 3, 1024], P('dp', None, 'mp')
- qkv_first_new: float32 [1024, 3, 1024], P('dp', None, 'mp')
- qkv_second_new: float32 [1024, 3, 1024], P('dp', None, 'mp')
- out_new: float32 [1024, 1024], P('dp', 'mp')
- out_first_new: float32 [1024, 1024], P('dp', 'mp')
- out_second_new: float32 [1024, 1024], P('dp', 'mp')
- up_new: float32 [1024, 4096], P('dp', 'mp')
- up_first_new: float32 [1024, 4096], P('dp', 'mp')
- up_second_new: float32 [1024, 4096], P('dp', 'mp')
- down_new: float32 [1024, 4096], P('dp', 'mp')
- down_first_new: float32 [1024, 4096], P('dp', 'mp')
- down_second_new: float32 [1024, 4096], P('dp', 'mp')
- vector_new: float32 [6, 1024], P(None, ('dp', 'mp'))
- vector_first_new: float32 [6, 1024], P(None, ('dp', 'mp'))
- vector_second_new: float32 [6, 1024], P(None, ('dp', 'mp'))
The draws below stay inside these ranges and needn't reach their ends.
Inputs may be any that keep to these rules, and one draw needn't show every extreme that they name: `crop_lengths`: each image's 10 crops are two global crops of 197 tokens and the others local crops of 37 tokens, in an order drawn for each image; they sum to 690.
All inputs are finite; a program needn't handle non-finite values.
Results may differ from the reference program's by a relative error of at most 0.018.
The reference program's roundings to bfloat16 on the way count: a program that leaves them out, or rounds other values in their place, can miss the bound.
Values may be sent and summed in bfloat16 or wider, within the bound.
No kernel may reach another device: no remote copies, remote signals or barrier semaphores. Data moves between devices by JAX's collectives and lax.ppermute only.
A program may use at most 128 MiB of HBM per device.

```python
import math
from functools import partial
import jax
import jax.numpy as jnp
from jax import lax

D = 1024
HEADS = 16
HEAD_DIM = 64
FF = 4096
CROPS = 10
GLOBAL_LEN = 197
LOCAL_LEN = 37
STEP = 10
TOK_IMG = 690
IMAGES = 16
TOKENS = 11040
N_MP = 4


def crop_order(image_key):
    return jax.random.permutation(image_key, CROPS)


def draw_crop_lengths(key, part):
    key = jax.random.fold_in(key, 7)
    image_keys = jax.random.split(key, IMAGES)
    orders = jax.vmap(crop_order)(image_keys)
    return jnp.where(orders < 2, GLOBAL_LEN, LOCAL_LEN).astype(jnp.int32)


def levels(own_key, extent, cuts, smallest, largest):
    factor_of, own = 1.0, jax.random.fold_in(own_key, 6)
    for axis_at, blocks in cuts:
        heights = jnp.exp(jax.random.uniform(jax.random.fold_in(own, axis_at), (blocks,), jnp.float32, smallest / len(cuts), largest / len(cuts)))
        factor_of = factor_of * jnp.repeat(heights, extent[axis_at] // blocks).reshape([-1 if axis == axis_at else 1 for axis in range(len(extent))])
    return factor_of


def noise(key, shape, scale, most, cuts=(), held_as=jnp.bfloat16):
    result = jax.random.normal(key, shape, jnp.float32) * scale
    if len(cuts) > 0:
        result = levels(key, shape, cuts, -0.22, 0.18) * result
    return jnp.clip(result, min=-most, max=most).astype(held_as)


def setup_inputs(seed: int = 0) -> dict:
    streams_of = jax.random.split(jax.random.key(seed), 19)
    return {
        "tokens": noise(streams_of[0], (TOKENS, D), 1.0, 6.0, ((0, 32),)),
        "cotangent": noise(streams_of[1], (TOKENS, D), 1.0, 6.0, ((0, 32),)),
        "crop_lengths": draw_crop_lengths(jax.random.fold_in(streams_of[18], 71), 0),
        "qkv_weight": noise(streams_of[3], (D, 3, D), (D // 2) ** -0.5, 0.25, ((0, 8), (2, 4)), jnp.float32),
        "out_weight": noise(streams_of[4], (D, D), (D // 8) ** -0.5, 0.5, ((0, 8), (1, 4)), jnp.float32),
        "up_weight": noise(streams_of[5], (D, FF), D ** -0.5, 0.1875, ((0, 8), (1, 4)), jnp.float32),
        "down_weight": noise(streams_of[6], (D, FF), FF ** -0.5, 0.09375, ((0, 8), (1, 4)), jnp.float32),
        "vectors": jnp.clip(1.0 + 0.15 * jax.random.normal(streams_of[7], (6, D), jnp.float32), 0.25, 1.75),
        "qkv_first": noise(streams_of[8], (D, 3, D), (0.11 * (2 * TOKENS) ** 0.5), 96.0, ((0, 8), (2, 4)), jnp.float32),
        "out_first": noise(streams_of[9], (D, D), (0.11 * TOKENS ** 0.5), 64.0, ((0, 8), (1, 4)), jnp.float32),
        "up_first": noise(streams_of[10], (D, FF), (0.11 * (0.3 * TOKENS) ** 0.5), 40.0, ((0, 8), (1, 4)), jnp.float32),
        "down_first": noise(streams_of[11], (D, FF), (0.11 * TOKENS ** 0.5), 64.0, ((0, 8), (1, 4)), jnp.float32),
        "vector_first": noise(streams_of[12], (6, D), (0.11 * TOKENS ** 0.5), 64.0, ((1, 32),), jnp.float32),
        "qkv_second": jnp.clip(jnp.exp(math.log(88.32) - 1.3862944 * jax.random.uniform(streams_of[13], (D, 3, D), jnp.float32) ** levels(streams_of[13], (D, 3, D), ((0, 8), (2, 4)), -0.2, 0.2)), 22.08, 88.32),
        "out_second": jnp.clip(jnp.exp(math.log(44.16) - 1.3862944 * jax.random.uniform(streams_of[14], (D, D), jnp.float32) ** levels(streams_of[14], (D, D), ((0, 8), (1, 4)), -0.2, 0.2)), 11.04, 44.16),
        "up_second": jnp.clip(jnp.exp(math.log(13.248) - 1.3862944 * jax.random.uniform(streams_of[15], (D, FF), jnp.float32) ** levels(streams_of[15], (D, FF), ((0, 8), (1, 4)), -0.2, 0.2)), 3.312, 13.248),
        "down_second": jnp.clip(jnp.exp(math.log(44.16) - 1.3862944 * jax.random.uniform(streams_of[16], (D, FF), jnp.float32) ** levels(streams_of[16], (D, FF), ((0, 8), (1, 4)), -0.2, 0.2)), 11.04, 44.16),
        "vector_second": jnp.clip(jnp.exp(math.log(44.16) - 1.3862944 * jax.random.uniform(streams_of[17], (6, D), jnp.float32) ** levels(streams_of[17], (6, D), ((1, 32),), -0.2, 0.2)), 11.04, 44.16),
    }


norm_eps = 1e-06
masked_score = -1e+30
beta_first = 0.9
beta_second = 0.999
adam_eps = 1e-08
matrix_rate = 0.1
vector_rate = 1.25
matrix_decay = 0.04

@jax.custom_vjp
def low(v):
    return lax.optimization_barrier(v.astype(jnp.bfloat16)).astype(jnp.float32)

@jax.custom_vjp
def low_back(v):
    return v

def low_keep(v):
    return (low(v), None)

def low_pass(kept, grad):
    return (grad,)

def back_keep(v):
    return (v, None)

def back_low(kept, grad):
    return (low(grad),)
low.defvjp(low_keep, low_pass)
low_back.defvjp(back_keep, back_low)

def normalize(values, norm_gain, norm_shift):
    center = values - lax.optimization_barrier(jnp.mean(values, axis=-1, keepdims=True))
    spread = lax.optimization_barrier(jnp.mean(center * center, axis=-1, keepdims=True))
    return center * lax.rsqrt(spread + norm_eps) * norm_gain + norm_shift

def segment_mask(lengths, length_rows):
    crop_ends = jnp.cumsum(lengths)
    places = jnp.arange(length_rows, dtype=jnp.int32)
    labels = lax.optimization_barrier(jnp.sum((places[:, None] >= crop_ends[None, :]).astype(jnp.int32), axis=1))
    return labels[:, None] == labels[None, :]

def image_attention(operands):
    block_rows, lengths = operands
    queries = block_rows[:, 0]
    key_rows = block_rows[:, 1]
    value_rows = block_rows[:, 2]
    scores = jnp.einsum('qhd,khd->hqk', queries, key_rows, precision=lax.Precision.HIGHEST) * HEAD_DIM ** (-0.5)
    allowed = segment_mask(lengths, TOK_IMG)
    scores = low_back(jnp.where(allowed[None], scores, masked_score))
    prob_full = low(jax.nn.softmax(scores, axis=-1))
    return jnp.einsum('hqk,khd->qhd', prob_full, value_rows, precision=lax.Precision.HIGHEST)

def grouped(row_block, weight, width):
    running_sum = jnp.zeros((row_block.shape[0], weight.shape[0]), jnp.float32)
    for section in range(N_MP):
        group_term = jnp.dot(row_block[:, section * width:(section + 1) * width], weight[:, section * width:(section + 1) * width].T, precision=lax.Precision.HIGHEST)
        running_sum = running_sum + low(group_term)
    return running_sum

def forward(lengths, inputs, qkv_master, out_master, up_master, down_master, vector_master):
    qkv_low = low(qkv_master)
    out_low = low(out_master)
    up_low = low(up_master)
    down_low = low(down_master)
    gain_one, shift_one, gain_two, shift_two, scale_one, scale_two = low(vector_master)
    norm_one = low(normalize(inputs, gain_one, shift_one))
    qkv_rows = jnp.dot(norm_one, qkv_low.reshape(D, 3 * D), precision=lax.Precision.HIGHEST)
    qkv_rows = low_back(low(qkv_rows)).reshape(IMAGES, TOK_IMG, 3, HEADS, HEAD_DIM)
    attended = lax.map(jax.checkpoint(image_attention), (qkv_rows, lengths))
    attended = low_back(low(attended.reshape(TOKENS, D)))
    branch_one = low_back(grouped(attended, out_low, D // N_MP))
    middle = inputs + scale_one * branch_one
    norm_two = low(normalize(middle, gain_two, shift_two))
    hidden_pre = low_back(jnp.dot(norm_two, up_low, precision=lax.Precision.HIGHEST))
    hidden_act = low(jax.nn.gelu(hidden_pre, approximate=False))
    branch_two = low_back(grouped(hidden_act, down_low, FF // N_MP))
    return middle + scale_two * branch_two

def adamw_step(weight, gradient, first_old, second_old, step_rate, decay_rate):
    first_new = beta_first * first_old + (1.0 - beta_first) * gradient
    second_new = beta_second * second_old + (1.0 - beta_second) * gradient * gradient
    first_hat = first_new / (1.0 - beta_first ** STEP)
    second_hat = second_new / (1.0 - beta_second ** STEP)
    weight_new = weight - step_rate * (first_hat / (jnp.sqrt(second_hat) + adam_eps) + decay_rate * weight)
    return (weight_new, first_new, second_new)

def reference(tokens, cotangent, crop_lengths, qkv_weight, out_weight, up_weight, down_weight, vectors, qkv_first, out_first, up_first, down_first, vector_first, qkv_second, out_second, up_second, down_second, vector_second):
    inputs = tokens.astype(jnp.float32)
    output, pullback = jax.vjp(partial(forward, crop_lengths), inputs, qkv_weight, out_weight, up_weight, down_weight, vectors)
    grads = pullback(cotangent.astype(jnp.float32))
    qkv_new, qkv_first_new, qkv_second_new = adamw_step(qkv_weight, grads[1], qkv_first, qkv_second, matrix_rate, matrix_decay)
    out_new, out_first_new, out_second_new = adamw_step(out_weight, grads[2], out_first, out_second, matrix_rate, matrix_decay)
    up_new, up_first_new, up_second_new = adamw_step(up_weight, grads[3], up_first, up_second, matrix_rate, matrix_decay)
    down_new, down_first_new, down_second_new = adamw_step(down_weight, grads[4], down_first, down_second, matrix_rate, matrix_decay)
    vector_new, vector_first_new, vector_second_new = adamw_step(vectors, grads[5], vector_first, vector_second, vector_rate, 0.0)
    return (output.astype(jnp.bfloat16), grads[0].astype(jnp.bfloat16), qkv_new, qkv_first_new, qkv_second_new, out_new, out_first_new, out_second_new, up_new, up_first_new, up_second_new, down_new, down_first_new, down_second_new, vector_new, vector_first_new, vector_second_new)
```

```python
import jax
import jax.numpy as jnp
from jax import lax
from jax.sharding import PartitionSpec as P

HEAD_DIM = 64
STEP = 10
GLOBAL_LEN = 197
LOCAL_LEN = 37
GLOBAL_PAD = 208
LOCAL_TILE = 128
PER_TILE = 3
SLOTS = 2 * GLOBAL_PAD + 3 * LOCAL_TILE

norm_eps = 1e-06
masked_score = -1e30
beta_first = 0.9
beta_second = 0.999
adam_eps = 1e-08
matrix_rate = 0.1
vector_rate = 1.25
matrix_decay = 0.04

F32 = jnp.float32
BF16 = jnp.bfloat16
AXES = ("dp", "mp")


def dot(a, b, dims):
    return lax.dot_general(a, b, (dims, ((), ())), preferred_element_type=F32)


def nn(a, b):
    return dot(a, b, ((1,), (0,)))


def nt(a, b):
    return dot(a, b, ((1,), (1,)))


def tn(a, b):
    return dot(a, b, ((0,), (0,)))


def adamw_step(weight, gradient, first_old, second_old, step_rate, decay_rate):
    first_new = beta_first * first_old + (1.0 - beta_first) * gradient
    second_new = beta_second * second_old + (1.0 - beta_second) * gradient * gradient
    first_hat = first_new / (1.0 - beta_first**STEP)
    second_hat = second_new / (1.0 - beta_second**STEP)
    weight_new = weight - step_rate * (
        first_hat / (jnp.sqrt(second_hat) + adam_eps) + decay_rate * weight
    )
    return (weight_new, first_new, second_new)


class Comm:
    def __init__(self, n_dp, n_mp):
        self.n_dp, self.n_mp = n_dp, n_mp
        self.n = n_dp * n_mp
        self.grid = n_dp == 8 and n_mp == 4

    def perm(self, f):
        out = []
        for d in range(self.n_dp):
            for m in range(self.n_mp):
                td, tm = f(d, m)
                out.append((d * self.n_mp + m, td * self.n_mp + tm))
        return out

    def core(self, v):
        return lax.ppermute(v, AXES, self.perm(lambda d, m: (d, m ^ 1)))

    def y(self, v):
        return lax.ppermute(v, AXES, self.perm(lambda d, m: (d, m ^ 2)))

    def x(self, v):
        return lax.ppermute(v, AXES, self.perm(lambda d, m: (d ^ 1, m)))

    def z(self, v, k):
        return lax.ppermute(v, AXES, self.perm(lambda d, m: ((d + 2 * k) % 8, m)))

    def total(self, v):
        bit = 1
        while bit < self.n:
            v = v + lax.ppermute(v, AXES, [(i, i ^ bit) for i in range(self.n)])
            bit *= 2
        return v

    def order(self):
        d = lax.axis_index("dp")
        if not self.grid:
            return [jnp.int32(r) for r in range(self.n_dp)]
        z, x = d // 2, d % 2
        return [((z + dz) % 4) * 2 + (x ^ dx) for dx in range(2) for dz in range(4)]

    def places(self):
        d = lax.axis_index("dp")
        if not self.grid:
            return [jnp.int32(r) for r in range(self.n_dp)]
        z, x = d // 2, d % 2
        return [((a // 2 - z + 4) % 4) + 4 * ((a % 2) ^ x) for a in range(8)]

    def gather(self, p):
        if not self.grid:
            own = lax.all_gather(p, "dp", axis=0, tiled=True)
            return [own], [self.y(own)]
        rows = p.shape[0]
        x0, y0 = self.x(p), self.y(p)
        s = jnp.concatenate([self.z(p, -1), self.z(p, 2), self.z(p, 1)], axis=0)
        xs, ys = self.x(s), self.y(s)
        d01 = self.y(jnp.concatenate([x0, xs[:rows]], axis=0))
        d23 = self.x(ys[rows:])
        return [p, s, x0, xs], [y0, ys, d01, d23]

    def scatter(self, own, other):
        if not self.grid:
            mine = own + self.y(other.astype(BF16)).astype(F32)
            return lax.psum_scatter(mine, "dp", scatter_dimension=0, tiled=True)
        block = own.shape[0] // 8
        half = 4 * block
        e01 = self.y(other[half : half + 2 * block].astype(BF16))
        e23 = self.x(other[half + 2 * block :].astype(BF16))
        qx = jnp.concatenate(
            [(own[half : half + 2 * block] + e01).astype(BF16), own[half + 2 * block :].astype(BF16)], axis=0
        )
        qy = jnp.concatenate(
            [other[: 2 * block].astype(BF16), (other[2 * block : half] + e23).astype(BF16)], axis=0
        )
        fx, fy = self.x(qx), self.y(qy)
        q = own[:half] + fx + fy
        g1 = self.z(q[block : 2 * block].astype(BF16), 1)
        g2 = self.z(q[2 * block : 3 * block].astype(BF16), 2)
        g3 = self.z(q[3 * block :].astype(BF16), -1)
        return q[:block] + g1 + g2 + g3


def norm_parts(values):
    center = values - jnp.mean(values, axis=-1, keepdims=True)
    spread = jnp.mean(center * center, axis=-1, keepdims=True)
    inverse = lax.rsqrt(spread + norm_eps)
    return center * inverse, inverse


def norm_back(normed, inverse, gain, grad):
    e = gain * grad
    return (
        e - jnp.mean(e, axis=-1, keepdims=True) - normed * jnp.mean(e * normed, axis=-1, keepdims=True)
    ) * inverse


def take_blocks(v, which, block):
    return jnp.concatenate(
        [lax.dynamic_slice_in_dim(v, w * block, block, axis=1) for w in which], axis=1
    )


def pad_rows(v, rows):
    return jnp.pad(v, ((0, rows - v.shape[0]), (0, 0)))


def slots_of(lengths, positions):
    ends = jnp.cumsum(lengths)
    starts = ends - lengths
    is_global = lengths == GLOBAL_LEN
    global_rank = jnp.cumsum(is_global.astype(jnp.int32)) - 1
    local_rank = jnp.cumsum(1 - is_global.astype(jnp.int32)) - 1
    base = jnp.where(
        is_global,
        GLOBAL_PAD * global_rank,
        2 * GLOBAL_PAD + LOCAL_TILE * (local_rank // PER_TILE) + LOCAL_LEN * (local_rank % PER_TILE),
    )
    inside = (positions[:, None] >= starts[None]) & (positions[:, None] < ends[None])
    return jnp.sum(jnp.where(inside, base[None] + positions[:, None] - starts[None], 0), axis=1)


TILES = [(0, GLOBAL_PAD), (GLOBAL_PAD, GLOBAL_PAD)] + [
    (2 * GLOBAL_PAD + LOCAL_TILE * k, LOCAL_TILE) for k in range(3)
]


def tile_mask(size):
    row = lax.broadcasted_iota(jnp.int32, (size, size), 0)
    col = lax.broadcasted_iota(jnp.int32, (size, size), 1)
    if size == GLOBAL_PAD:
        return col < GLOBAL_LEN
    return (row // LOCAL_LEN) == (col // LOCAL_LEN)


def attention_forward(qkv):
    heads = qkv.shape[1] // (3 * HEAD_DIM)
    split = qkv.reshape(SLOTS, 3, heads, HEAD_DIM)
    outs, probs = [], []
    for at, size in TILES:
        part = split[at : at + size]
        scores = jnp.einsum("qhd,khd->hqk", part[:, 0], part[:, 1], preferred_element_type=F32)
        scores = jnp.where(tile_mask(size)[None], scores * 0.125, masked_score)
        prob = jax.nn.softmax(scores, axis=-1)
        probs.append(prob)
        outs.append(
            jnp.einsum("hqk,khd->qhd", prob.astype(BF16), part[:, 2], preferred_element_type=F32).astype(BF16)
        )
    return jnp.concatenate(outs, axis=0).reshape(SLOTS, heads * HEAD_DIM), probs


def attention_backward(qkv, probs, grad):
    heads = qkv.shape[1] // (3 * HEAD_DIM)
    split = qkv.reshape(SLOTS, 3, heads, HEAD_DIM)
    grads = grad.reshape(SLOTS, heads, HEAD_DIM)
    outs = []
    for (at, size), prob in zip(TILES, probs):
        part = split[at : at + size]
        out_grad = grads[at : at + size]
        low = prob.astype(BF16)
        value_grad = jnp.einsum("hqk,qhd->khd", low, out_grad, preferred_element_type=F32)
        prob_grad = jnp.einsum("qhd,khd->hqk", out_grad, part[:, 2], preferred_element_type=F32)
        row_dot = jnp.sum(prob_grad * prob, axis=-1, keepdims=True)
        score_grad = (prob * (prob_grad - row_dot)).astype(BF16)
        query_grad = 0.125 * jnp.einsum("hqk,khd->qhd", score_grad, part[:, 1], preferred_element_type=F32)
        key_grad = 0.125 * jnp.einsum("hqk,qhd->khd", score_grad, part[:, 0], preferred_element_type=F32)
        outs.append(jnp.stack([query_grad, key_grad, value_grad], axis=1).astype(BF16))
    return jnp.concatenate(outs, axis=0).reshape(SLOTS, 3 * heads * HEAD_DIM)


def shards(comm, tokens, cotangent, crop_lengths, qkv_weight, out_weight, up_weight, down_weight, vectors,
           qkv_first, out_first, up_first, down_first, vector_first,
           qkv_second, out_second, up_second, down_second, vector_second):
    rows, width = tokens.shape
    padded = -(-rows // 16) * 16
    block = width // comm.n_dp
    own_index = lax.axis_index("mp")
    image, core = own_index // 2, own_index % 2
    flat_index = lax.axis_index("dp") * comm.n_mp + own_index
    local = qkv_weight.shape[2]
    hidden = up_weight.shape[1]
    order, places = comm.order(), comm.places()
    to_rel = lambda v: take_blocks(v, order, block)
    to_abs = lambda v: take_blocks(v, places, block)

    vector_part = vectors.astype(BF16)
    vector_full = comm.total(
        lax.dynamic_update_slice(
            jnp.zeros((6, width), F32), vector_part.astype(F32), (0, flat_index * vectors.shape[1])
        ).astype(BF16)
    ).astype(F32)
    gain_one, shift_one, gain_two, shift_two, scale_one, scale_two = vector_full
    pack_a = jnp.concatenate([qkv_weight.reshape(-1, 3 * local), out_weight], axis=1).astype(BF16)
    a_own, a_oth = comm.gather(pack_a)
    u_own, u_oth = comm.gather(up_weight.astype(BF16))
    d_own, d_oth = comm.gather(down_weight.astype(BF16))
    cat = lambda blocks: jnp.concatenate(blocks, axis=0)
    a_own, a_oth, u_own, u_oth, d_own, d_oth = map(cat, (a_own, a_oth, u_own, u_oth, d_own, d_oth))

    lengths = lax.dynamic_index_in_dim(crop_lengths, image, 0, keepdims=False)
    lane = jnp.arange(padded, dtype=jnp.int32)
    positions = jnp.concatenate(
        [jnp.where(lane < rows, lane + half * rows, -1) for half in (core, 1 - core)]
    )
    slot = jnp.where(positions >= 0, slots_of(lengths, positions), -1)
    pick = (jnp.arange(SLOTS, dtype=jnp.int32)[:, None] == slot[None, :]).astype(BF16)

    def both(v):
        return jnp.concatenate([v, comm.core(v)], axis=0)

    residual = tokens.astype(F32)
    normed_one, inverse_one = norm_parts(residual)
    norm_one = pad_rows(to_rel((normed_one * gain_one + shift_one).astype(BF16)), padded)
    rows_one = both(norm_one)
    out_grad = cotangent.astype(F32)
    mlp_rows = both(pad_rows(to_rel((out_grad * scale_two).astype(BF16)), padded))

    wide = 3 * local
    qkv = jnp.concatenate([nn(rows_one, a_own[:, :wide]), nn(rows_one, a_oth[:, :wide])], axis=1).astype(BF16)
    heads = local // HEAD_DIM
    interleave = lambda v: v.reshape(-1, 2, 3, local).transpose(0, 2, 1, 3).reshape(-1, 2 * wide)
    back = lambda v: v.reshape(-1, 3, 2, local).transpose(0, 2, 1, 3).reshape(-1, 2 * wide)
    qkv_slots = interleave(nn(pick, qkv).astype(BF16))
    attended_slots, probs = attention_forward(qkv_slots)
    attended = tn(pick, attended_slots).astype(BF16)

    def grouped(left, own, other):
        width_own = left.shape[1] // 2
        return nt(left[:, :width_own], own).astype(BF16).astype(F32) + nt(left[:, width_own:], other).astype(
            BF16
        ).astype(F32)

    def own_sum(partial):
        return to_abs(partial[:rows] + comm.core(partial[padded:].astype(BF16))[:rows].astype(F32))

    branch_one = own_sum(grouped(attended, a_own[:, wide:], a_oth[:, wide:]))
    middle = residual + scale_one * branch_one
    normed_two, inverse_two = norm_parts(middle)
    rows_two = both(pad_rows(to_rel((normed_two * gain_two + shift_two).astype(BF16)), padded))

    hidden_pre = jnp.concatenate([nn(rows_two, u_own), nn(rows_two, u_oth)], axis=1)
    cdf = 0.5 * (1.0 + lax.erf(hidden_pre * (0.5**0.5)))
    hidden_act = (hidden_pre * cdf).astype(BF16)
    slope = cdf + hidden_pre * jnp.exp(-0.5 * hidden_pre * hidden_pre) * 0.3989422804014327
    branch_two = own_sum(grouped(hidden_act, d_own, d_oth))
    output = (middle + scale_two * branch_two).astype(BF16)
    grad_scale_two = jnp.sum(out_grad * branch_two, axis=0)
    down_share = comm.scatter(tn(mlp_rows, hidden_act[:, :hidden]), tn(mlp_rows, hidden_act[:, hidden:]))
    act_grad = jnp.concatenate([nn(mlp_rows, d_own), nn(mlp_rows, d_oth)], axis=1)
    pre_grad = (act_grad * slope).astype(BF16)
    up_share = comm.scatter(tn(rows_two, pre_grad[:, :hidden]), tn(rows_two, pre_grad[:, hidden:]))
    norm_two_grad = own_sum(nt(pre_grad[:, :hidden], u_own) + nt(pre_grad[:, hidden:], u_oth))
    middle_grad = out_grad + norm_back(normed_two, inverse_two, gain_two, norm_two_grad)
    grad_gain_two = jnp.sum(norm_two_grad * normed_two, axis=0)
    grad_shift_two = jnp.sum(norm_two_grad, axis=0)
    grad_scale_one = jnp.sum(middle_grad * branch_one, axis=0)
    attn_rows = both(pad_rows(to_rel((middle_grad * scale_one).astype(BF16)), padded))

    attended_grad = jnp.concatenate(
        [nn(attn_rows, a_own[:, wide:]), nn(attn_rows, a_oth[:, wide:])], axis=1
    ).astype(BF16)
    grad_slots = attention_backward(qkv_slots, probs, nn(pick, attended_grad).astype(BF16))
    qkv_grad = tn(pick, back(grad_slots)).astype(BF16)
    a_share = comm.scatter(
        jnp.concatenate([tn(rows_one, qkv_grad[:, :wide]), tn(attn_rows, attended[:, :local])], axis=1),
        jnp.concatenate([tn(rows_one, qkv_grad[:, wide:]), tn(attn_rows, attended[:, local:])], axis=1),
    )
    norm_one_grad = own_sum(nt(qkv_grad[:, :wide], a_own[:, :wide]) + nt(qkv_grad[:, wide:], a_oth[:, :wide]))
    input_grad = (middle_grad + norm_back(normed_one, inverse_one, gain_one, norm_one_grad)).astype(BF16)
    grad_gain_one = jnp.sum(norm_one_grad * normed_one, axis=0)
    grad_shift_one = jnp.sum(norm_one_grad, axis=0)

    vector_grad = comm.total(
        jnp.stack([grad_gain_one, grad_shift_one, grad_gain_two, grad_shift_two, grad_scale_one, grad_scale_two])
    )
    vector_share = lax.dynamic_slice_in_dim(
        vector_grad, flat_index * vectors.shape[1], vectors.shape[1], axis=1
    )
    matrix = lambda w, g, m, v: adamw_step(w, g, m, v, matrix_rate, matrix_decay)
    return (
        output,
        input_grad,
        *matrix(qkv_weight, a_share[:, :wide].reshape(qkv_weight.shape), qkv_first, qkv_second),
        *matrix(out_weight, a_share[:, wide:], out_first, out_second),
        *matrix(up_weight, up_share, up_first, up_second),
        *matrix(down_weight, down_share, down_first, down_second),
        *adamw_step(vectors, vector_share, vector_first, vector_second, vector_rate, 0.0),
    )


def solution(mesh):
    comm = Comm(mesh.shape["dp"], mesh.shape["mp"])
    rows = P(("dp", "mp"), None)
    cube = P("dp", None, "mp")
    flat = P("dp", "mp")
    vec = P(None, ("dp", "mp"))
    moments = (cube, flat, flat, flat, vec)
    return jax.shard_map(
        lambda *args: shards(comm, *args),
        mesh=mesh,
        in_specs=(rows, rows, P("dp", None), *moments, *moments, *moments),
        out_specs=(rows, rows, *(spec for spec in moments for _ in range(3))),
        check_vma=False,
    )
```

```python
import functools

import jax
import jax.numpy as jnp
from jax import lax
from jax.experimental import pallas as pl
from jax.experimental.pallas import tpu as pltpu
from jax.sharding import PartitionSpec as P

HEAD_DIM = 64
STEP = 10
GLOBAL_LEN = 197
LOCAL_LEN = 37
GLOBAL_PAD = 208
LOCAL_TILE = 128
PER_TILE = 3
SLOTS = 2 * GLOBAL_PAD + 3 * LOCAL_TILE

norm_eps = 1e-06
masked_score = -1e30
beta_first = 0.9
beta_second = 0.999
adam_eps = 1e-08
matrix_rate = 0.1
vector_rate = 1.25
matrix_decay = 0.04

F32 = jnp.float32
BF16 = jnp.bfloat16
AXES = ("dp", "mp")


def dot(a, b, dims):
    return lax.dot_general(a, b, (dims, ((), ())), preferred_element_type=F32)


def nn(a, b):
    return dot(a, b, ((1,), (0,)))


def nt(a, b):
    return dot(a, b, ((1,), (1,)))


def tn(a, b):
    return dot(a, b, ((0,), (0,)))


def adamw_step(weight, gradient, first_old, second_old, step_rate, decay_rate):
    first_new = beta_first * first_old + (1.0 - beta_first) * gradient
    second_new = beta_second * second_old + (1.0 - beta_second) * gradient * gradient
    first_hat = first_new / (1.0 - beta_first**STEP)
    second_hat = second_new / (1.0 - beta_second**STEP)
    weight_new = weight - step_rate * (
        first_hat / (jnp.sqrt(second_hat) + adam_eps) + decay_rate * weight
    )
    return (weight_new, first_new, second_new)


def after(v, *first):
    return lax.optimization_barrier((v, first))[0]


class Comm:
    def __init__(self, n_dp, n_mp):
        self.n_dp, self.n_mp = n_dp, n_mp
        self.n = n_dp * n_mp
        self.grid = n_dp == 8 and n_mp == 4

    def perm(self, f):
        out = []
        for d in range(self.n_dp):
            for m in range(self.n_mp):
                td, tm = f(d, m)
                out.append((d * self.n_mp + m, td * self.n_mp + tm))
        return out

    def core(self, v):
        return lax.ppermute(v, AXES, self.perm(lambda d, m: (d, m ^ 1)))

    def y(self, v):
        return lax.ppermute(v, AXES, self.perm(lambda d, m: (d, m ^ 2)))

    def x(self, v):
        return lax.ppermute(v, AXES, self.perm(lambda d, m: (d ^ 1, m)))

    def z(self, v, k):
        return lax.ppermute(v, AXES, self.perm(lambda d, m: ((d + 2 * k) % 8, m)))

    def total(self, v):
        bit = 1
        while bit < self.n:
            v = v + lax.ppermute(v, AXES, [(i, i ^ bit) for i in range(self.n)])
            bit *= 2
        return v

    def order(self):
        d = lax.axis_index("dp")
        if not self.grid:
            return [jnp.int32(r) for r in range(self.n_dp)]
        z, x = d // 2, d % 2
        return [((z + dz) % 4) * 2 + (x ^ dx) for dx in range(2) for dz in range(4)]

    def places(self):
        d = lax.axis_index("dp")
        if not self.grid:
            return [jnp.int32(r) for r in range(self.n_dp)]
        z, x = d // 2, d % 2
        return [((a // 2 - z + 4) % 4) + 4 * ((a % 2) ^ x) for a in range(8)]

    def gather_all(self, a, m, vector):
        if not self.grid:
            out = []
            for p in (a, m):
                own = lax.all_gather(p, "dp", axis=0, tiled=True)
                out.append(([own], [self.y(own)]))
            return out[0], out[1], self.total(vector)
        rows = a.shape[0]
        cat = lambda *v: jnp.concatenate(v, axis=0)
        ax0, ay0 = self.x(a), self.y(a)
        az = cat(self.z(a, -1), self.z(a, 2), self.z(a, 1))
        vector = self.total(after(vector, ax0, ay0))
        m_late = after(m, ax0, ay0)
        mx0, my0 = self.x(m_late), self.y(m_late)
        axs, ays = self.x(az), self.y(az)
        m_later = after(m, az)
        mz = cat(self.z(m_later, -1), self.z(m_later, 2), self.z(m_later, 1))
        ady = self.y(cat(ax0, axs[:rows]))
        adx = self.x(ays[rows:])
        mz = after(mz, ady, adx)
        mxs, mys = self.x(mz), self.y(mz)
        mdy = self.y(cat(mx0, mxs[:rows]))
        mdx = self.x(mys[rows:])
        return (
            ([a, az, ax0, axs], [ay0, ays, ady, adx]),
            ([m, mz, mx0, mxs], [my0, mys, mdy, mdx]),
            vector,
        )

    def scatter(self, own, other):
        if not self.grid:
            mine = own + self.y(other.astype(BF16)).astype(F32)
            return lax.psum_scatter(mine, "dp", scatter_dimension=0, tiled=True)
        block = own.shape[0] // 8
        half = 4 * block
        e01 = self.y(other[half : half + 2 * block].astype(BF16))
        e23 = self.x(other[half + 2 * block :].astype(BF16))
        qx = jnp.concatenate(
            [(own[half : half + 2 * block] + e01).astype(BF16), own[half + 2 * block :].astype(BF16)], axis=0
        )
        qy = jnp.concatenate(
            [other[: 2 * block].astype(BF16), (other[2 * block : half] + e23).astype(BF16)], axis=0
        )
        fx, fy = self.x(qx), self.y(qy)
        q = own[:half] + fx + fy
        g1 = self.z(q[block : 2 * block].astype(BF16), 1)
        g2 = self.z(q[2 * block : 3 * block].astype(BF16), 2)
        g3 = self.z(q[3 * block :].astype(BF16), -1)
        return q[:block] + g1 + g2 + g3


def norm_parts(values):
    center = values - jnp.mean(values, axis=-1, keepdims=True)
    spread = jnp.mean(center * center, axis=-1, keepdims=True)
    inverse = lax.rsqrt(spread + norm_eps)
    return center * inverse, inverse


def norm_back(normed, inverse, gain, grad):
    e = gain * grad
    return (
        e - jnp.mean(e, axis=-1, keepdims=True) - normed * jnp.mean(e * normed, axis=-1, keepdims=True)
    ) * inverse


def take_blocks(v, which, block):
    return jnp.concatenate(
        [lax.dynamic_slice_in_dim(v, w * block, block, axis=1) for w in which], axis=1
    )


def pad_rows(v, rows):
    return jnp.pad(v, ((0, rows - v.shape[0]), (0, 0)))


def slots_of(lengths, positions):
    ends = jnp.cumsum(lengths)
    starts = ends - lengths
    is_global = lengths == GLOBAL_LEN
    global_rank = jnp.cumsum(is_global.astype(jnp.int32)) - 1
    local_rank = jnp.cumsum(1 - is_global.astype(jnp.int32)) - 1
    base = jnp.where(
        is_global,
        GLOBAL_PAD * global_rank,
        2 * GLOBAL_PAD + LOCAL_TILE * (local_rank // PER_TILE) + LOCAL_LEN * (local_rank % PER_TILE),
    )
    inside = (positions[:, None] >= starts[None]) & (positions[:, None] < ends[None])
    return jnp.sum(jnp.where(inside, base[None] + positions[:, None] - starts[None], 0), axis=1)


VMEM_LIMIT = 60 * 1024 * 1024


def lanes_of(h, v):
    lane = lax.broadcasted_iota(jnp.int32, v.shape, 1)
    keep = (lane < HEAD_DIM) if h == 0 else (lane >= HEAD_DIM)
    return jnp.where(keep, v, jnp.zeros_like(v))


TILES = [(0, GLOBAL_PAD, 256), (GLOBAL_PAD, GLOBAL_PAD, 256)] + [
    (2 * GLOBAL_PAD + LOCAL_TILE * k, LOCAL_TILE, LOCAL_TILE) for k in range(3)
]


def tile_mask(queries, keys):
    row = lax.broadcasted_iota(jnp.int32, (queries, keys), 0)
    col = lax.broadcasted_iota(jnp.int32, (queries, keys), 1)
    if keys == 256:
        return col < GLOBAL_LEN
    same = None
    for k in range(4):
        lo, hi = k * LOCAL_LEN, (k + 1) * LOCAL_LEN if k < 3 else LOCAL_TILE
        inside = (row >= lo) & (row < hi) & (col >= lo) & (col < hi)
        same = inside if same is None else same | inside
    return same


def fill_pick(pick, slot_row):
    places = lax.broadcasted_iota(jnp.int32, pick.shape, 0)
    pick[...] = jnp.where(places == slot_row[...], 1.0, 0.0).astype(BF16)


def fill_pick_t(pick_t, slot_col):
    places = lax.broadcasted_iota(jnp.int32, pick_t.shape, 1)
    pick_t[...] = jnp.where(places == slot_col[...], 1.0, 0.0).astype(BF16)


def attend_kernel(counts, *refs):
    n = sum(counts)
    rows_own, rows_oth, slot_row, slot_col = refs[:4]
    pieces = refs[4 : 4 + n]
    weights, slots, attended, keep, send, probs_g, probs_l = refs[4 + n : 11 + n]
    pick, pick_t, qkv, att_slots, sems = refs[11 + n :]
    half = rows_own.shape[0]
    wide = qkv.shape[1]
    local = slots.shape[1] // 6
    three = 3 * local
    copies = []
    at = 0
    for g in range(2):
        row = 0
        for _ in range(counts[g]):
            piece = pieces[at]
            copies.append(
                pltpu.make_async_copy(piece, weights.at[g, pl.ds(row, piece.shape[0])], sems.at[at])
            )
            row += piece.shape[0]
            at += 1
    for c in copies:
        c.start()
    fill_pick(pick, slot_row)
    fill_pick_t(pick_t, slot_col)
    for c in copies:
        c.wait()
    for g in range(2):

        def project(n, _, g=g):
            cols = pl.ds(pl.multiple_of(n * wide, wide), wide)
            w = weights[g, :, cols]
            qkv[:half] = nn(rows_own[...], w).astype(BF16)
            qkv[half:] = nn(rows_oth[...], w).astype(BF16)
            out = pl.ds(pl.multiple_of(g * three + n * wide, wide), wide)
            slots[:, out] = nn(pick[...], qkv[...]).astype(BF16)
            return 0

        lax.fori_loop(0, three // wide, project, 0)
    masks = {k: tile_mask(q, k) for _, q, k in TILES}
    pairs = local // 128
    for g in range(2):
        for p in range(pairs):
            base = g * three + p * 128
            for t, (first, queries, keys) in enumerate(TILES):
                q = slots[first : first + queries, base : base + 128]
                k = slots[first : first + keys, base + local : base + local + 128]
                v = slots[first : first + keys, base + 2 * local : base + 2 * local + 128]
                outs = []
                for h in range(2):
                    scores = nt(lanes_of(h, q), k) * 0.125
                    scores = jnp.where(masks[keys], scores, masked_score)
                    e = jnp.exp(scores - jnp.max(scores, axis=1, keepdims=True))
                    prob = e * (1.0 / jnp.sum(e, axis=1, keepdims=True))
                    head = (g * pairs + p) * 2 + h
                    if keys == 256:
                        probs_g[head, t] = prob
                    else:
                        probs_l[head, t - 2] = prob
                    outs.append(nn(prob.astype(BF16), v))
                lane = lax.broadcasted_iota(jnp.int32, outs[0].shape, 1)
                col = g * local + p * 128
                att_slots[first : first + queries, col : col + 128] = jnp.where(
                    lane < HEAD_DIM, outs[0], outs[1]
                ).astype(BF16)
    attended[...] = nn(pick_t[...], att_slots[...]).astype(BF16)

    def back(n, _):
        rows = pl.ds(pl.multiple_of(n * 256, 256), 256)
        total = 0.0
        for g in range(2):
            w = weights[g, rows, three:]
            total = total + nt(attended[:, g * local : (g + 1) * local], w).astype(BF16).astype(F32)
        keep[:, rows] = total[:half]
        send[:, rows] = total[half:].astype(BF16)
        return 0

    lax.fori_loop(0, weights.shape[1] // 256, back, 0)


def vmem():
    return pl.BlockSpec(memory_space=pltpu.VMEM)


def attend(rows_own, rows_oth, slot_row, slot_col, own, oth):
    half, width = rows_own.shape
    cols = own[0].shape[1]
    local = cols // 4
    pieces = [*own, *oth]
    heads = 2 * local // HEAD_DIM
    shape = jax.ShapeDtypeStruct
    wide = local
    return pl.pallas_call(
        functools.partial(attend_kernel, (len(own), len(oth))),
        out_shape=(
            shape((2, width, cols), BF16),
            shape((SLOTS, 6 * local), BF16),
            shape((2 * half, 2 * local), BF16),
            shape((half, width), F32),
            shape((half, width), BF16),
            shape((heads, 2, GLOBAL_PAD, 256), F32),
            shape((heads, 3, LOCAL_TILE, LOCAL_TILE), F32),
        ),
        in_specs=[vmem()] * 4 + [pl.BlockSpec(memory_space=pl.ANY)] * len(pieces),
        out_specs=(vmem(),) * 7,
        scratch_shapes=[
            pltpu.VMEM((SLOTS, 2 * half), BF16),
            pltpu.VMEM((2 * half, SLOTS), BF16),
            pltpu.VMEM((2 * half, wide), BF16),
            pltpu.VMEM((SLOTS, 2 * local), BF16),
            pltpu.SemaphoreType.DMA((len(pieces),)),
        ],
        compiler_params=pltpu.CompilerParams(vmem_limit_bytes=VMEM_LIMIT),
        cost_estimate=pl.CostEstimate(flops=9_000_000_000, bytes_accessed=20_000_000, transcendentals=2_000_000),
        name="attend",
    )(rows_own, rows_oth, slot_row, slot_col, *pieces)


def attend_back_kernel(
    rows_own, rows_oth, slot_row, slot_col, weights, slots, probs_g, probs_l, qkv_grad, keep, send,
    pick, pick_t, att, grads, slot_grads,
):
    half = rows_own.shape[0]
    local = slots.shape[1] // 6
    three = 3 * local
    fill_pick(pick, slot_row)
    fill_pick_t(pick_t, slot_col)
    for g in range(2):
        w = weights[g, :, three:]
        att[:half, g * local : (g + 1) * local] = nn(rows_own[...], w).astype(BF16)
        att[half:, g * local : (g + 1) * local] = nn(rows_oth[...], w).astype(BF16)
    grads[...] = nn(pick[...], att[...]).astype(BF16)
    pairs = local // 128
    for g in range(2):
        for p in range(pairs):
            base = g * three + p * 128
            for t, (first, queries, keys) in enumerate(TILES):
                q = slots[first : first + queries, base : base + 128]
                k = slots[first : first + keys, base + local : base + local + 128]
                v = slots[first : first + keys, base + 2 * local : base + 2 * local + 128]
                d = grads[first : first + queries, g * local + p * 128 : g * local + (p + 1) * 128]
                dqs, dks, dvs = [], [], []
                for h in range(2):
                    head = (g * pairs + p) * 2 + h
                    prob = probs_g[head, t] if keys == 256 else probs_l[head, t - 2]
                    dp = nt(lanes_of(h, d), v)
                    ds = (prob * (dp - jnp.sum(dp * prob, axis=1, keepdims=True))).astype(BF16)
                    dvs.append(tn(prob.astype(BF16), d))
                    dqs.append(nn(ds, k))
                    dks.append(tn(ds, q))
                for j, (two, factor) in enumerate(((dqs, 0.125), (dks, 0.125), (dvs, 1.0))):
                    lane = lax.broadcasted_iota(jnp.int32, two[0].shape, 1)
                    both = jnp.where(lane < HEAD_DIM, two[0], two[1])
                    if factor != 1.0:
                        both = both * factor
                    slot_grads[first : first + queries, base + j * local : base + j * local + 128] = both[
                        :queries
                    ].astype(BF16)

    def unsort(n, _):
        cols = pl.ds(pl.multiple_of(n * local, local), local)
        qkv_grad[:, cols] = nn(pick_t[...], slot_grads[:, cols]).astype(BF16)
        return 0

    lax.fori_loop(0, 6, unsort, 0)

    def back(n, _):
        rows = pl.ds(pl.multiple_of(n * 256, 256), 256)
        total = nt(qkv_grad[:, :three], weights[0, rows, :three]) + nt(qkv_grad[:, three:], weights[1, rows, :three])
        keep[:, rows] = total[:half]
        send[:, rows] = total[half:].astype(BF16)
        return 0

    lax.fori_loop(0, weights.shape[1] // 256, back, 0)


def attend_back(rows_own, rows_oth, slot_row, slot_col, weights, slots, probs_g, probs_l):
    half, width = rows_own.shape
    local = slots.shape[1] // 6
    shape = jax.ShapeDtypeStruct
    return pl.pallas_call(
        attend_back_kernel,
        out_shape=(
            shape((2 * half, 6 * local), BF16),
            shape((half, width), F32),
            shape((half, width), BF16),
        ),
        in_specs=[vmem()] * 8,
        out_specs=(vmem(),) * 3,
        scratch_shapes=[
            pltpu.VMEM((SLOTS, 2 * half), BF16),
            pltpu.VMEM((2 * half, SLOTS), BF16),
            pltpu.VMEM((2 * half, 2 * local), BF16),
            pltpu.VMEM((SLOTS, 2 * local), BF16),
            pltpu.VMEM((SLOTS, 6 * local), BF16),
        ],
        compiler_params=pltpu.CompilerParams(vmem_limit_bytes=VMEM_LIMIT),
        cost_estimate=pl.CostEstimate(flops=12_000_000_000, bytes_accessed=20_000_000, transcendentals=0),
        name="attend_back",
    )(rows_own, rows_oth, slot_row, slot_col, weights, slots, probs_g, probs_l)


def shards(comm, tokens, cotangent, crop_lengths, qkv_weight, out_weight, up_weight, down_weight, vectors,
           qkv_first, out_first, up_first, down_first, vector_first,
           qkv_second, out_second, up_second, down_second, vector_second):
    rows, width = tokens.shape
    padded = -(-rows // 16) * 16
    block = width // comm.n_dp
    own_index = lax.axis_index("mp")
    image, core = own_index // 2, own_index % 2
    flat_index = lax.axis_index("dp") * comm.n_mp + own_index
    local = qkv_weight.shape[2]
    hidden = up_weight.shape[1]
    order, places = comm.order(), comm.places()
    to_rel = lambda v: take_blocks(v, order, block)
    to_abs = lambda v: take_blocks(v, places, block)

    pack_a = jnp.concatenate([qkv_weight.reshape(-1, 3 * local), out_weight], axis=1).astype(BF16)
    pack_m = jnp.concatenate([up_weight, down_weight], axis=1).astype(BF16)
    vector_full = lax.dynamic_update_slice(
        jnp.zeros((6, width), F32), vectors.astype(BF16).astype(F32), (0, flat_index * vectors.shape[1])
    ).astype(BF16)
    (a_own, a_oth), (m_own, m_oth), vector_full = comm.gather_all(pack_a, pack_m, vector_full)
    gain_one, shift_one, gain_two, shift_two, scale_one, scale_two = vector_full.astype(F32)
    cat = lambda blocks: jnp.concatenate(blocks, axis=0)
    m_own, m_oth = cat(m_own), cat(m_oth)
    u_own, d_own = m_own[:, :hidden], m_own[:, hidden:]
    u_oth, d_oth = m_oth[:, :hidden], m_oth[:, hidden:]

    lengths = lax.dynamic_index_in_dim(crop_lengths, image, 0, keepdims=False)
    lane = jnp.arange(padded, dtype=jnp.int32)
    positions = jnp.concatenate(
        [jnp.where(lane < rows, lane + half * rows, -1) for half in (core, 1 - core)]
    )
    slot = jnp.where(positions >= 0, slots_of(lengths, positions), -1)
    slot_row, slot_col = slot[None, :], slot[:, None]

    def both(v):
        return jnp.concatenate([v, comm.core(v)], axis=0)

    residual = tokens.astype(F32)
    normed_one, inverse_one = norm_parts(residual)
    norm_one = pad_rows(to_rel((normed_one * gain_one + shift_one).astype(BF16)), padded)
    norm_one_other = comm.core(norm_one)
    rows_one = jnp.concatenate([norm_one, norm_one_other], axis=0)
    out_grad = cotangent.astype(F32)
    mlp_rows = both(pad_rows(to_rel((out_grad * scale_two).astype(BF16)), padded))

    wide = 3 * local
    weights_a, slots, attended, keep, send, probs_g, probs_l = attend(
        norm_one, norm_one_other, slot_row, slot_col, a_own, a_oth
    )

    def joined(keep, send):
        return to_abs(keep[:rows] + comm.core(send)[:rows].astype(F32))

    def own_sum(partial):
        return joined(partial[:padded], partial[padded:].astype(BF16))

    def grouped(left, own, other):
        width_own = left.shape[1] // 2
        return nt(left[:, :width_own], own).astype(BF16).astype(F32) + nt(left[:, width_own:], other).astype(
            BF16
        ).astype(F32)

    branch_one = joined(keep, send)
    middle = residual + scale_one * branch_one
    normed_two, inverse_two = norm_parts(middle)
    rows_two = both(pad_rows(to_rel((normed_two * gain_two + shift_two).astype(BF16)), padded))

    hidden_pre = jnp.concatenate([nn(rows_two, u_own), nn(rows_two, u_oth)], axis=1)
    cdf = 0.5 * (1.0 + lax.erf(hidden_pre * (0.5**0.5)))
    hidden_act = (hidden_pre * cdf).astype(BF16)
    slope = cdf + hidden_pre * jnp.exp(-0.5 * hidden_pre * hidden_pre) * 0.3989422804014327
    branch_two = own_sum(grouped(hidden_act, d_own, d_oth))
    output = (middle + scale_two * branch_two).astype(BF16)
    grad_scale_two = jnp.sum(out_grad * branch_two, axis=0)
    down_share = comm.scatter(tn(mlp_rows, hidden_act[:, :hidden]), tn(mlp_rows, hidden_act[:, hidden:]))
    act_grad = jnp.concatenate([nn(mlp_rows, d_own), nn(mlp_rows, d_oth)], axis=1)
    pre_grad = (act_grad * slope).astype(BF16)
    up_share = comm.scatter(tn(rows_two, pre_grad[:, :hidden]), tn(rows_two, pre_grad[:, hidden:]))
    norm_two_grad = own_sum(nt(pre_grad[:, :hidden], u_own) + nt(pre_grad[:, hidden:], u_oth))
    middle_grad = out_grad + norm_back(normed_two, inverse_two, gain_two, norm_two_grad)
    grad_gain_two = jnp.sum(norm_two_grad * normed_two, axis=0)
    grad_shift_two = jnp.sum(norm_two_grad, axis=0)
    grad_scale_one = jnp.sum(middle_grad * branch_one, axis=0)
    attn_own = pad_rows(to_rel((middle_grad * scale_one).astype(BF16)), padded)
    attn_other = comm.core(attn_own)
    attn_rows = jnp.concatenate([attn_own, attn_other], axis=0)

    qkv_grad, keep, send = attend_back(
        attn_own, attn_other, slot_row, slot_col, weights_a, slots, probs_g, probs_l
    )
    a_share = comm.scatter(
        jnp.concatenate([tn(rows_one, qkv_grad[:, :wide]), tn(attn_rows, attended[:, :local])], axis=1),
        jnp.concatenate([tn(rows_one, qkv_grad[:, wide:]), tn(attn_rows, attended[:, local:])], axis=1),
    )
    norm_one_grad = joined(keep, send)
    input_grad = (middle_grad + norm_back(normed_one, inverse_one, gain_one, norm_one_grad)).astype(BF16)
    grad_gain_one = jnp.sum(norm_one_grad * normed_one, axis=0)
    grad_shift_one = jnp.sum(norm_one_grad, axis=0)

    vector_grad = comm.total(
        jnp.stack([grad_gain_one, grad_shift_one, grad_gain_two, grad_shift_two, grad_scale_one, grad_scale_two])
    )
    vector_share = lax.dynamic_slice_in_dim(
        vector_grad, flat_index * vectors.shape[1], vectors.shape[1], axis=1
    )
    matrix = lambda w, g, m, v: adamw_step(w, g, m, v, matrix_rate, matrix_decay)
    return (
        output,
        input_grad,
        *matrix(qkv_weight, a_share[:, :wide].reshape(qkv_weight.shape), qkv_first, qkv_second),
        *matrix(out_weight, a_share[:, wide:], out_first, out_second),
        *matrix(up_weight, up_share, up_first, up_second),
        *matrix(down_weight, down_share, down_first, down_second),
        *adamw_step(vectors, vector_share, vector_first, vector_second, vector_rate, 0.0),
    )


def solution(mesh):
    comm = Comm(mesh.shape["dp"], mesh.shape["mp"])
    rows = P(("dp", "mp"), None)
    cube = P("dp", None, "mp")
    flat = P("dp", "mp")
    vec = P(None, ("dp", "mp"))
    moments = (cube, flat, flat, flat, vec)
    return jax.shard_map(
        lambda *args: shards(comm, *args),
        mesh=mesh,
        in_specs=(rows, rows, P("dp", None), *moments, *moments, *moments),
        out_specs=(rows, rows, *(spec for spec in moments for _ in range(3))),
        check_vma=False,
    )
```

```python
import functools

import jax
import jax.numpy as jnp
from jax import lax
from jax.experimental import pallas as pl
from jax.experimental.pallas import tpu as pltpu
from jax.sharding import PartitionSpec as P

HEAD_DIM = 64
STEP = 10
GLOBAL_LEN = 197
LOCAL_LEN = 37
GLOBAL_PAD = 208
LOCAL_TILE = 128
PER_TILE = 3
SLOTS = 2 * GLOBAL_PAD + 3 * LOCAL_TILE

norm_eps = 1e-06
masked_score = -1e30
beta_first = 0.9
beta_second = 0.999
adam_eps = 1e-08
matrix_rate = 0.1
vector_rate = 1.25
matrix_decay = 0.04

F32 = jnp.float32
BF16 = jnp.bfloat16
AXES = ("dp", "mp")


def dot(a, b, dims):
    return lax.dot_general(a, b, (dims, ((), ())), preferred_element_type=F32)


def nn(a, b):
    return dot(a, b, ((1,), (0,)))


def nt(a, b):
    return dot(a, b, ((1,), (1,)))


def tn(a, b):
    return dot(a, b, ((0,), (0,)))


def adamw_step(weight, gradient, first_old, second_old, step_rate, decay_rate):
    first_new = beta_first * first_old + (1.0 - beta_first) * gradient
    second_new = beta_second * second_old + (1.0 - beta_second) * gradient * gradient
    first_hat = first_new / (1.0 - beta_first**STEP)
    second_hat = second_new / (1.0 - beta_second**STEP)
    weight_new = weight - step_rate * (
        first_hat / (jnp.sqrt(second_hat) + adam_eps) + decay_rate * weight
    )
    return (weight_new, first_new, second_new)


def after(v, *first):
    return lax.optimization_barrier((v, first))[0]


class Comm:
    def __init__(self, n_dp, n_mp):
        self.n_dp, self.n_mp = n_dp, n_mp
        self.n = n_dp * n_mp
        self.grid = n_dp == 8 and n_mp == 4

    def perm(self, f):
        out = []
        for d in range(self.n_dp):
            for m in range(self.n_mp):
                td, tm = f(d, m)
                out.append((d * self.n_mp + m, td * self.n_mp + tm))
        return out

    def core(self, v):
        return lax.ppermute(v, AXES, self.perm(lambda d, m: (d, m ^ 1)))

    def y(self, v):
        return lax.ppermute(v, AXES, self.perm(lambda d, m: (d, m ^ 2)))

    def x(self, v):
        return lax.ppermute(v, AXES, self.perm(lambda d, m: (d ^ 1, m)))

    def z(self, v, k):
        return lax.ppermute(v, AXES, self.perm(lambda d, m: (d ^ (2 * k), m)))

    def total(self, v, bits=None):
        for bit in bits or [1 << k for k in range(self.n.bit_length() - 1)]:
            v = v + lax.ppermute(v, AXES, [(i, i ^ bit) for i in range(self.n)])
        return v

    def order(self):
        d = lax.axis_index("dp")
        if not self.grid:
            return [jnp.int32(r) for r in range(self.n_dp)]
        z, x = d // 2, d % 2
        return [(z ^ dz) * 2 + (x ^ dx) for dx in range(2) for dz in range(4)]

    def places(self):
        d = lax.axis_index("dp")
        if not self.grid:
            return [jnp.int32(r) for r in range(self.n_dp)]
        z, x = d // 2, d % 2
        return [((a // 2) ^ z) + 4 * ((a % 2) ^ x) for a in range(8)]

    def gather_first(self, a, u, d, vector):
        if not self.grid:
            a, u, d = (lax.all_gather(p, "dp", axis=0, tiled=True) for p in (a, u, d))
            return ([a], [self.y(a)]), u, d, self.total(vector)
        rows, cols = u.shape
        cat = lambda *v: jnp.concatenate(v, axis=0)
        ax0, ay0 = self.x(a), self.y(a)
        az = tuple(self.z(a, k) for k in (1, 2, 3))
        vector = self.total(after(vector, ax0, ay0))
        ud = jnp.concatenate([u, d], axis=1)
        udx0 = self.x(after(ud, ax0))
        ud1 = self.z(after(ud, vector, *az), 1)
        az = after(cat(*az), udx0)
        axs, ays = self.x(az), self.y(az)
        ady, adx = self.y(after(cat(ax0, axs[:rows]), ays, ud1)), self.x(after(ays[rows:], axs, ud1))
        u1, d1 = ud1[:, :cols], ud1[:, cols:]
        u23 = self.z(after(cat(u, u1), axs, ays), 2)
        return ([a, az, ax0, axs], [ay0, ays, ady, adx]), (u, u1, u23, udx0[:, :cols]), (d, d1, udx0[:, cols:]), vector

    def gather_rest(self, u, d, first):
        if not self.grid:
            return [u], [d]
        cat = lambda *v: jnp.concatenate(v, axis=0)
        (u, u1, u23, ux0), (d, d1, dx0) = u, d
        uxs = self.x(after(cat(u1, u23), first))
        d23 = self.z(after(cat(d, d1), first), 2)
        dxs = self.x(after(cat(d1, d23), uxs))
        return [u, u1, u23, ux0, uxs], [d, d1, d23, dx0, dxs]

    def scatter_diagonal(self, part, rows):
        if not self.grid:
            return (self.y(part(1, 0, rows).astype(BF16)),)
        half = rows // 2
        middle = half + rows // 4
        return self.y(part(1, half, middle).astype(BF16)), self.x(part(1, middle, rows).astype(BF16))

    def scatter_sides(self, part, rows, diagonal):
        if not self.grid:
            return diagonal
        e01, e23 = diagonal
        half, two = rows // 2, rows // 4
        cat = lambda *v: jnp.concatenate(v, axis=0)
        fx = self.x(cat((part(0, half, half + two) + e01).astype(BF16), part(0, half + two, rows).astype(BF16)))
        fy = self.y(cat(part(1, 0, two).astype(BF16), (part(1, two, half) + e23).astype(BF16)))
        return fx, fy

    def scatter_x(self, part, rows):
        if not self.grid:
            return (), None
        sent = part(0, rows // 2, rows).astype(BF16)
        return (self.x(sent),), sent

    def scatter_two(self, part, rows, sides, *first):
        if not self.grid:
            mine = sum(sides, part(0, 0, rows))
            return None, lambda *_: lax.psum_scatter(mine, "dp", scatter_dimension=0, tiled=True)
        block = rows // 8
        q = sum(after(sides, *first) if first else sides, part(0, 0, 4 * block))

        def rest(got, *first):
            both = q[: 2 * block] + after(got, *first)
            return both[:block] + self.z(both[block:].astype(BF16), 1)

        return self.z(q[2 * block :].astype(BF16), 2), rest

    def scatter_z(self, part, rows, sides, *first):
        if not self.grid:
            mine = sum(sides, part(0, 0, rows))
            return lax.psum_scatter(mine, "dp", scatter_dimension=0, tiled=True)
        block = rows // 8
        q = sum(sides, part(0, 0, 4 * block))
        sent = [q[k * block : (k + 1) * block].astype(BF16) for k in (1, 2, 3)]
        return sum((self.z(v, k) for v, k in zip(sent, (1, 2, 3))), q[:block])


def norm_parts(values):
    center = values - jnp.mean(values, axis=-1, keepdims=True)
    spread = jnp.mean(center * center, axis=-1, keepdims=True)
    inverse = lax.rsqrt(spread + norm_eps)
    return center * inverse, inverse


def norm_back(normed, inverse, gain, grad):
    e = gain * grad
    return (
        e - jnp.mean(e, axis=-1, keepdims=True) - normed * jnp.mean(e * normed, axis=-1, keepdims=True)
    ) * inverse


def take_blocks(v, which, block):
    return jnp.concatenate(
        [lax.dynamic_slice_in_dim(v, w * block, block, axis=1) for w in which], axis=1
    )


def pad_rows(v, rows):
    return jnp.pad(v, ((0, rows - v.shape[0]), (0, 0)))


def slots_of(lengths, positions):
    ends = jnp.cumsum(lengths)
    starts = ends - lengths
    is_global = lengths == GLOBAL_LEN
    global_rank = jnp.cumsum(is_global.astype(jnp.int32)) - 1
    local_rank = jnp.cumsum(1 - is_global.astype(jnp.int32)) - 1
    base = jnp.where(
        is_global,
        GLOBAL_PAD * global_rank,
        2 * GLOBAL_PAD + LOCAL_TILE * (local_rank // PER_TILE) + LOCAL_LEN * (local_rank % PER_TILE),
    )
    inside = (positions[:, None] >= starts[None]) & (positions[:, None] < ends[None])
    return jnp.sum(jnp.where(inside, base[None] + positions[:, None] - starts[None], 0), axis=1)


VMEM_LIMIT = 48 * 1024 * 1024


def lanes_of(h, v):
    lane = lax.broadcasted_iota(jnp.int32, v.shape, 1)
    keep = (lane < HEAD_DIM) if h == 0 else (lane >= HEAD_DIM)
    return jnp.where(keep, v, jnp.zeros_like(v))


def two_heads(first, second):
    lane = lax.broadcasted_iota(jnp.int32, first.shape, 1)
    return jnp.where(lane < HEAD_DIM, first, second)


GLOBAL_TILES = [(0, GLOBAL_PAD, 256), (GLOBAL_PAD, GLOBAL_PAD, 256)]
LOCAL_TILES = [(2 * GLOBAL_PAD + LOCAL_TILE * k, LOCAL_TILE, LOCAL_TILE) for k in range(3)]


def tile_mask(queries, keys):
    row = lax.broadcasted_iota(jnp.int32, (queries, keys), 0)
    col = lax.broadcasted_iota(jnp.int32, (queries, keys), 1)
    if keys == 256:
        return col < GLOBAL_LEN
    same = None
    for k in range(4):
        lo, hi = k * LOCAL_LEN, (k + 1) * LOCAL_LEN if k < 3 else LOCAL_TILE
        inside = (row >= lo) & (row < hi) & (col >= lo) & (col < hi)
        same = inside if same is None else same | inside
    return same


def fill_picks(pick, pick_t, slot_row):
    places = lax.broadcasted_iota(jnp.int32, pick.shape, 0)
    row = slot_row[...]
    pick[...] = jnp.where(places == row, 1.0, 0.0).astype(BF16)
    col = jnp.transpose(jnp.broadcast_to(row.astype(F32), (8, row.shape[1])))[:, :1].astype(jnp.int32)
    places = lax.broadcasted_iota(jnp.int32, pick_t.shape, 1)
    pick_t[...] = jnp.where(places == col, 1.0, 0.0).astype(BF16)


def vmem():
    return pl.BlockSpec(memory_space=pltpu.VMEM)


def anywhere():
    return pl.BlockSpec(memory_space=pl.ANY)


def attend_kernel(counts, *refs):
    n = sum(counts)
    rows_own, rows_oth, slot_row = refs[:3]
    pieces = refs[3 : 3 + n]
    weights_out, slots_out, attended, keep, send, probs_g_out, probs_l_out = refs[3 + n : 10 + n]
    pick, pick_t, qkv, att_slots, weights, slots, probs_g, probs_l, sems, out_sems = refs[10 + n :]
    half = rows_own.shape[0]
    wide = qkv.shape[1]
    local = slots.shape[1] // 6
    three = 3 * local
    copies = [[], []]
    at = 0
    for g in range(2):
        row = 0
        for _ in range(counts[g]):
            piece = pieces[at]
            copies[g].append(
                pltpu.make_async_copy(piece, weights.at[g, pl.ds(row, piece.shape[0])], sems.at[at])
            )
            row += piece.shape[0]
            at += 1
    for c in copies[0] + copies[1]:
        c.start()
    fill_picks(pick, pick_t, slot_row)
    outs = []

    def put(src, dst):
        c = pltpu.make_async_copy(src, dst, out_sems.at[len(outs)])
        c.start()
        outs.append(c)

    for g in range(2):
        for c in copies[g]:
            c.wait()
        put(weights.at[g], weights_out.at[g])

        def project(n, _, g=g):
            cols = pl.ds(pl.multiple_of(n * wide, wide), wide)
            w = weights[g, :, cols]
            qkv[:half] = nn(rows_own[...], w).astype(BF16)
            qkv[half:] = nn(rows_oth[...], w).astype(BF16)
            out = pl.ds(pl.multiple_of(g * three + n * wide, wide), wide)
            slots[:, out] = nn(pick[...], qkv[...]).astype(BF16)
            return 0

        lax.fori_loop(0, three // wide, project, 0)
    put(slots, slots_out)
    pairs = local // 128
    for tiles, probs in ((GLOBAL_TILES, probs_g), (LOCAL_TILES, probs_l)):
        mask = tile_mask(*tiles[0][1:])
        for g in range(2):
            for p in range(pairs):
                base = g * three + p * 128
                units = [(t, first, queries, keys, h) for t, (first, queries, keys) in enumerate(tiles) for h in range(2)]
                scores = [
                    nt(
                        lanes_of(h, slots[first : first + queries, base : base + 128]),
                        slots[first : first + keys, base + local : base + local + 128],
                    )
                    for t, first, queries, keys, h in units
                ]
                scores = [jnp.where(mask, s * 0.125, masked_score) for s in scores]
                tops = [jnp.max(s, axis=1, keepdims=True) for s in scores]
                es = [jnp.exp(s - top) for s, top in zip(scores, tops)]
                sums = [1.0 / jnp.sum(e, axis=1, keepdims=True) for e in es]
                lows = []
                for (t, first, queries, keys, h), e, s in zip(units, es, sums):
                    prob = e * s
                    probs[(g * pairs + p) * 2 + h, t] = prob
                    lows.append(prob.astype(BF16))
                mixed = [
                    nn(low, slots[first : first + keys, base + 2 * local : base + 2 * local + 128])
                    for (t, first, queries, keys, h), low in zip(units, lows)
                ]
                for t, (first, queries, keys) in enumerate(tiles):
                    col = g * local + p * 128
                    att_slots[first : first + queries, col : col + 128] = two_heads(
                        mixed[2 * t], mixed[2 * t + 1]
                    ).astype(BF16)
        put(probs, probs_g_out if probs is probs_g else probs_l_out)
    attended[...] = nn(pick_t[...], att_slots[...]).astype(BF16)

    def back(n, _):
        rows = pl.ds(pl.multiple_of(n * 256, 256), 256)
        total = 0.0
        for g in range(2):
            w = weights[g, rows, three:]
            total = total + nt(attended[:, g * local : (g + 1) * local], w).astype(BF16).astype(F32)
        keep[:, rows] = total[:half]
        send[:, rows] = total[half:].astype(BF16)
        return 0

    lax.fori_loop(0, weights.shape[1] // 256, back, 0)
    for c in outs:
        c.wait()


def attend(rows_own, rows_oth, slot_row, own, oth):
    half, width = rows_own.shape
    cols = own[0].shape[1]
    local = cols // 4
    pieces = [*own, *oth]
    heads = 2 * local // HEAD_DIM
    shape = jax.ShapeDtypeStruct
    probs = ((heads, 2, GLOBAL_PAD, 256), (heads, 3, LOCAL_TILE, LOCAL_TILE))
    return pl.pallas_call(
        functools.partial(attend_kernel, (len(own), len(oth))),
        out_shape=(
            shape((2, width, cols), BF16),
            shape((SLOTS, 6 * local), BF16),
            shape((2 * half, 2 * local), BF16),
            shape((half, width), F32),
            shape((half, width), BF16),
            shape(probs[0], F32),
            shape(probs[1], F32),
        ),
        in_specs=[vmem()] * 3 + [anywhere()] * len(pieces),
        out_specs=(anywhere(), anywhere(), vmem(), vmem(), vmem(), anywhere(), anywhere()),
        scratch_shapes=[
            pltpu.VMEM((SLOTS, 2 * half), BF16),
            pltpu.VMEM((2 * half, SLOTS), BF16),
            pltpu.VMEM((2 * half, local), BF16),
            pltpu.VMEM((SLOTS, 2 * local), BF16),
            pltpu.VMEM((2, width, cols), BF16),
            pltpu.VMEM((SLOTS, 6 * local), BF16),
            pltpu.VMEM(probs[0], F32),
            pltpu.VMEM(probs[1], F32),
            pltpu.SemaphoreType.DMA((len(pieces),)),
            pltpu.SemaphoreType.DMA((5,)),
        ],
        compiler_params=pltpu.CompilerParams(vmem_limit_bytes=VMEM_LIMIT),
        cost_estimate=pl.CostEstimate(flops=1000, bytes_accessed=1000, transcendentals=0),
        name="attend",
    )(rows_own, rows_oth, slot_row, *pieces)


def attend_back_kernel(
    rows_own, rows_oth, slot_row, weights_in, slots_in, probs_g_in, probs_l_in, qkv_grad_out, keep, send,
    pick, pick_t, att, grads, slot_grads, weights, slots, probs_g, probs_l, qkv_grad, sems, out_sems,
):
    half = rows_own.shape[0]
    local = slots.shape[1] // 6
    three = 3 * local
    gets = [
        pltpu.make_async_copy(src, dst, sems.at[i])
        for i, (src, dst) in enumerate(
            (
                (weights_in.at[:, :, pl.ds(three, local)], weights.at[:, :, pl.ds(three, local)]),
                (slots_in, slots),
                (probs_g_in, probs_g),
                (probs_l_in, probs_l),
                (weights_in.at[:, :, pl.ds(0, three)], weights.at[:, :, pl.ds(0, three)]),
            )
        )
    ]
    for c in gets:
        c.start()
    fill_picks(pick, pick_t, slot_row)
    gets[0].wait()
    for g in range(2):
        w = weights[g, :, three:]
        att[:half, g * local : (g + 1) * local] = nn(rows_own[...], w).astype(BF16)
        att[half:, g * local : (g + 1) * local] = nn(rows_oth[...], w).astype(BF16)
    grads[...] = nn(pick[...], att[...]).astype(BF16)
    gets[1].wait()
    pairs = local // 128
    for tiles, probs, get in ((GLOBAL_TILES, probs_g, gets[2]), (LOCAL_TILES, probs_l, gets[3])):
        get.wait()
        for g in range(2):
            for p in range(pairs):
                base = g * three + p * 128
                col = g * local + p * 128
                units = [(t, first, queries, keys, h) for t, (first, queries, keys) in enumerate(tiles) for h in range(2)]

                def part(j, first, size):
                    return slots[first : first + size, base + j * local : base + j * local + 128]

                outs = [grads[first : first + queries, col : col + 128] for t, first, queries, keys, h in units]
                prob = [probs[(g * pairs + p) * 2 + h, t] for t, first, queries, keys, h in units]
                dps = [
                    nt(lanes_of(h, d), part(2, first, keys)) for (t, first, queries, keys, h), d in zip(units, outs)
                ]
                dvs = [tn(pr.astype(BF16), d) for pr, d in zip(prob, outs)]
                dots = [jnp.sum(dp * pr, axis=1, keepdims=True) for dp, pr in zip(dps, prob)]
                dss = [(pr * (dp - dot_)).astype(BF16) for pr, dp, dot_ in zip(prob, dps, dots)]
                dqs = [nn(ds, part(1, first, keys)) for (t, first, queries, keys, h), ds in zip(units, dss)]
                dks = [tn(ds, part(0, first, queries)) for (t, first, queries, keys, h), ds in zip(units, dss)]
                for t, (first, queries, keys) in enumerate(tiles):
                    for j, (two, factor) in enumerate(((dqs, 0.125), (dks, 0.125), (dvs, 1.0))):
                        both = two_heads(two[2 * t], two[2 * t + 1])
                        if factor != 1.0:
                            both = both * factor
                        slot_grads[first : first + queries, base + j * local : base + j * local + 128] = both[
                            :queries
                        ].astype(BF16)

    def unsort(n, _):
        cols = pl.ds(pl.multiple_of(n * local, local), local)
        qkv_grad[:, cols] = nn(pick_t[...], slot_grads[:, cols]).astype(BF16)
        return 0

    lax.fori_loop(0, 6, unsort, 0)
    put = pltpu.make_async_copy(qkv_grad, qkv_grad_out, out_sems.at[0])
    put.start()
    gets[4].wait()

    def back(n, _):
        rows = pl.ds(pl.multiple_of(n * 256, 256), 256)
        total = nt(qkv_grad[:, :three], weights[0, rows, :three]) + nt(qkv_grad[:, three:], weights[1, rows, :three])
        keep[:, rows] = total[:half]
        send[:, rows] = total[half:].astype(BF16)
        return 0

    lax.fori_loop(0, weights.shape[1] // 256, back, 0)
    put.wait()


def attend_back(rows_own, rows_oth, slot_row, weights, slots, probs_g, probs_l):
    half, width = rows_own.shape
    local = slots.shape[1] // 6
    shape = jax.ShapeDtypeStruct
    return pl.pallas_call(
        attend_back_kernel,
        out_shape=(
            shape((2 * half, 6 * local), BF16),
            shape((half, width), F32),
            shape((half, width), BF16),
        ),
        in_specs=[vmem()] * 3 + [anywhere()] * 4,
        out_specs=(anywhere(), vmem(), vmem()),
        scratch_shapes=[
            pltpu.VMEM((SLOTS, 2 * half), BF16),
            pltpu.VMEM((2 * half, SLOTS), BF16),
            pltpu.VMEM((2 * half, 2 * local), BF16),
            pltpu.VMEM((SLOTS, 2 * local), BF16),
            pltpu.VMEM((SLOTS, 6 * local), BF16),
            pltpu.VMEM(weights.shape, BF16),
            pltpu.VMEM(slots.shape, BF16),
            pltpu.VMEM(probs_g.shape, F32),
            pltpu.VMEM(probs_l.shape, F32),
            pltpu.VMEM((2 * half, 6 * local), BF16),
            pltpu.SemaphoreType.DMA((5,)),
            pltpu.SemaphoreType.DMA((1,)),
        ],
        compiler_params=pltpu.CompilerParams(vmem_limit_bytes=VMEM_LIMIT),
        cost_estimate=pl.CostEstimate(flops=1000, bytes_accessed=1000, transcendentals=0),
        name="attend_back",
    )(rows_own, rows_oth, slot_row, weights, slots, probs_g, probs_l)


def shards(comm, tokens, cotangent, crop_lengths, qkv_weight, out_weight, up_weight, down_weight, vectors,
           qkv_first, out_first, up_first, down_first, vector_first,
           qkv_second, out_second, up_second, down_second, vector_second):
    rows, width = tokens.shape
    padded = -(-rows // 16) * 16
    block = width // comm.n_dp
    own_index = lax.axis_index("mp")
    image, core = own_index // 2, own_index % 2
    flat_index = lax.axis_index("dp") * comm.n_mp + own_index
    local = qkv_weight.shape[2]
    hidden = up_weight.shape[1]
    order, places = comm.order(), comm.places()
    to_rel = lambda v: take_blocks(v, order, block)
    to_abs = lambda v: take_blocks(v, places, block)

    pack_a = jnp.concatenate([qkv_weight.reshape(-1, 3 * local), out_weight], axis=1).astype(BF16)
    vector_full = lax.dynamic_update_slice(
        jnp.zeros((6, width), F32), vectors.astype(BF16).astype(F32), (0, flat_index * vectors.shape[1])
    ).astype(BF16)
    (a_own, a_oth), up_part, down_part, vector_full = comm.gather_first(
        pack_a, up_weight.astype(BF16), down_weight.astype(BF16), vector_full
    )
    gain_one, shift_one, gain_two, shift_two, scale_one, scale_two = vector_full.astype(F32)
    cat = lambda blocks: jnp.concatenate(blocks, axis=0)
    lengths = lax.dynamic_index_in_dim(crop_lengths, image, 0, keepdims=False)
    lane = jnp.arange(padded, dtype=jnp.int32)
    positions = jnp.concatenate(
        [jnp.where(lane < rows, lane + half * rows, -1) for half in (core, 1 - core)]
    )
    slot = jnp.where(positions >= 0, slots_of(lengths, positions), -1)
    slot_row = slot[None, :]

    residual = tokens.astype(F32)
    normed_one, inverse_one = norm_parts(residual)
    norm_one = pad_rows(to_rel((normed_one * gain_one + shift_one).astype(BF16)), padded)
    norm_one_other = comm.core(norm_one)
    rows_one = cat([norm_one, norm_one_other])
    out_grad = cotangent.astype(F32)
    own_y = cat([pad_rows(cotangent, padded), pad_rows(comm.y(after(cotangent, a_oth[0])), padded)])
    both_y = cat([own_y, comm.core(own_y)])
    mlp_all = to_rel((both_y.astype(F32) * scale_two).astype(BF16))
    mlp_near, mlp_far = (
        cat([mlp_all[at : at + padded], mlp_all[at + 2 * padded : at + 3 * padded]]) for at in (0, padded)
    )

    wide = 3 * local
    weights_a, slots, attended, keep, send, probs_g, probs_l = attend(
        norm_one, norm_one_other, slot_row, a_own, a_oth
    )

    def joined(keep, send):
        return to_abs(keep[:rows] + comm.core(send)[:rows].astype(F32))

    def spread(near, far, *first):
        got = comm.core(cat([near[padded:].astype(BF16), far[padded:].astype(BF16)]))
        sent = (far[:padded].astype(F32) + got[padded:]).astype(BF16)
        from_y = comm.y(after(sent, *first))
        mine = near[:padded].astype(F32) + got[:padded]
        return mine, sent, from_y

    if comm.grid:
        send = after(send, up_part[2])
    up_blocks, down_blocks = comm.gather_rest(up_part, down_part, send)
    up_full, down_full = cat(up_blocks), cat(down_blocks)
    branch_one = joined(keep, send)
    middle = residual + scale_one * branch_one
    normed_two, inverse_two = norm_parts(middle)
    norm_two = pad_rows(to_rel((normed_two * gain_two + shift_two).astype(BF16)), padded)
    norm_two_y = comm.y(norm_two)
    two_near = cat([norm_two, comm.core(norm_two)])
    two_far = cat([norm_two_y, comm.core(norm_two_y)])
    if comm.grid:
        two_far = after(two_far, up_blocks[4])

    def activate(hidden_pre):
        cdf = 0.5 * (1.0 + lax.erf(hidden_pre * (0.5**0.5)))
        slope = cdf + hidden_pre * jnp.exp(-0.5 * hidden_pre * hidden_pre) * 0.3989422804014327
        return (hidden_pre * cdf).astype(BF16), slope

    act_near, slope_near = activate(nn(two_near, up_full))
    act_far, slope_far = activate(nn(two_far, up_full))
    down_part = lambda g, first, last: tn(mlp_near[:, first:last], act_near) + tn(mlp_far[:, first:last], act_far)
    down_sums, sent = comm.scatter_x(down_part, width)
    back_far, back_near = (mlp_far, mlp_near) if sent is None else after((mlp_far, mlp_near), sent)
    pre_far = (nn(back_far, down_full) * slope_far).astype(BF16)
    pre_near = (nn(back_near, down_full) * slope_near).astype(BF16)
    mine, sent_y, from_y = spread(nt(pre_near, up_full), nt(pre_far, up_full))
    norm_two_grad = to_abs((mine + from_y)[:rows])
    up_part = lambda g, first, last: tn(two_near[:, first:last], pre_near) + tn(two_far[:, first:last], pre_far)
    up_sums, sent = comm.scatter_x(up_part, width)
    middle_grad = out_grad + norm_back(normed_two, inverse_two, gain_two, norm_two_grad)
    grad_gain_two = jnp.sum(norm_two_grad * normed_two, axis=0)
    grad_shift_two = jnp.sum(norm_two_grad, axis=0)
    grad_scale_one = jnp.sum(middle_grad * branch_one, axis=0)
    attn_own = pad_rows(to_rel((middle_grad * scale_one).astype(BF16)), padded)
    attn_other = comm.core(attn_own)
    attn_rows = cat([attn_own, attn_other])
    branch_near, branch_far = after((act_near, act_far), sent_y)
    branch_mine, _, branch_y = spread(
        nt(branch_near, down_full).astype(BF16), nt(branch_far, down_full).astype(BF16), from_y
    )

    qkv_grad, keep, send = attend_back(
        attn_own, attn_other, slot_row, weights_a, slots, probs_g, probs_l
    )
    branch_two = to_abs((branch_mine + after(branch_y, send))[:rows])
    output = (middle + scale_two * branch_two).astype(BF16)
    grad_scale_two = jnp.sum(out_grad * branch_two, axis=0)

    def a_part(g, first, last):
        qkv_cols, out_cols = slice(g * wide, (g + 1) * wide), slice(g * local, (g + 1) * local)
        return jnp.concatenate(
            [tn(rows_one[:, first:last], qkv_grad[:, qkv_cols]), tn(attn_rows[:, first:last], attended[:, out_cols])],
            axis=1,
        )

    down_got, down_rest = comm.scatter_two(down_part, width, down_sums)
    up_got, up_rest = comm.scatter_two(up_part, width, up_sums, send)
    down_share, up_share = down_rest(down_got, send), up_rest(up_got, send)
    a_sums = comm.scatter_diagonal(a_part, width)
    norm_one_grad = joined(keep, send)
    input_grad = (middle_grad + norm_back(normed_one, inverse_one, gain_one, norm_one_grad)).astype(BF16)
    grad_gain_one = jnp.sum(norm_one_grad * normed_one, axis=0)
    grad_shift_one = jnp.sum(norm_one_grad, axis=0)

    vector_grad = jnp.stack(
        [grad_gain_one, grad_shift_one, grad_gain_two, grad_shift_two, grad_scale_one, grad_scale_two]
    )
    bits = [1 << k for k in range(comm.n.bit_length() - 1)]
    if comm.grid:
        a_sums = after(a_sums, vector_grad, down_got)
    vector_grad = comm.total(after(vector_grad, *a_sums), (*bits[3:], bits[0]))
    a_sums = comm.scatter_sides(a_part, width, a_sums)
    if comm.grid:
        a_sums = after(a_sums, vector_grad)
    vector_grad = comm.total(after(vector_grad, *a_sums), bits[1:3])
    a_share = comm.scatter_z(a_part, width, a_sums)
    vector_share = lax.dynamic_slice_in_dim(
        vector_grad, flat_index * vectors.shape[1], vectors.shape[1], axis=1
    )
    matrix = lambda w, g, m, v: adamw_step(w, g, m, v, matrix_rate, matrix_decay)
    qkv_parts = [
        matrix(qkv_weight[:, k], a_share[:, k * local : (k + 1) * local], qkv_first[:, k], qkv_second[:, k])
        for k in range(3)
    ]
    return (
        output,
        input_grad,
        *(jnp.stack(v, axis=1) for v in zip(*qkv_parts)),
        *matrix(out_weight, a_share[:, wide:], out_first, out_second),
        *matrix(up_weight, up_share, up_first, up_second),
        *matrix(down_weight, down_share, down_first, down_second),
        *adamw_step(vectors, vector_share, vector_first, vector_second, vector_rate, 0.0),
    )


def solution(mesh):
    comm = Comm(mesh.shape["dp"], mesh.shape["mp"])
    rows = P(("dp", "mp"), None)
    cube = P("dp", None, "mp")
    flat = P("dp", "mp")
    vec = P(None, ("dp", "mp"))
    moments = (cube, flat, flat, flat, vec)
    return jax.shard_map(
        lambda *args: shards(comm, *args),
        mesh=mesh,
        in_specs=(rows, rows, P("dp", None), *moments, *moments, *moments),
        out_specs=(rows, rows, *(spec for spec in moments for _ in range(3))),
        check_vma=False,
    )
```

```python
import functools

import jax
import jax.numpy as jnp
from jax import lax
from jax.experimental import pallas as pl
from jax.experimental.pallas import tpu as pltpu
from jax.sharding import PartitionSpec as P

HEAD_DIM = 64
STEP = 10
GLOBAL_LEN = 197
LOCAL_LEN = 37
GLOBAL_PAD = 208
LOCAL_TILE = 128
PER_TILE = 3
SLOTS = 2 * GLOBAL_PAD + 3 * LOCAL_TILE

norm_eps = 1e-06
masked_score = -1e30
beta_first = 0.9
beta_second = 0.999
adam_eps = 1e-08
matrix_rate = 0.1
vector_rate = 1.25
matrix_decay = 0.04

F32 = jnp.float32
BF16 = jnp.bfloat16
AXES = ("dp", "mp")


def dot(a, b, dims):
    return lax.dot_general(a, b, (dims, ((), ())), preferred_element_type=F32)


def nn(a, b):
    return dot(a, b, ((1,), (0,)))


def nt(a, b):
    return dot(a, b, ((1,), (1,)))


def tn(a, b):
    return dot(a, b, ((0,), (0,)))


def adamw_step(weight, gradient, first_old, second_old, step_rate, decay_rate):
    first_new = beta_first * first_old + (1.0 - beta_first) * gradient
    second_new = beta_second * second_old + (1.0 - beta_second) * gradient * gradient
    first_hat = first_new / (1.0 - beta_first**STEP)
    second_hat = second_new / (1.0 - beta_second**STEP)
    weight_new = weight - step_rate * (
        first_hat / (jnp.sqrt(second_hat) + adam_eps) + decay_rate * weight
    )
    return (weight_new, first_new, second_new)


def after(v, *first):
    return lax.optimization_barrier((v, first))[0]


class Comm:
    def __init__(self, n_dp, n_mp):
        self.n_dp, self.n_mp = n_dp, n_mp
        self.n = n_dp * n_mp
        self.grid = n_dp == 8 and n_mp == 4

    def perm(self, f):
        out = []
        for d in range(self.n_dp):
            for m in range(self.n_mp):
                td, tm = f(d, m)
                out.append((d * self.n_mp + m, td * self.n_mp + tm))
        return out

    def core(self, v):
        return lax.ppermute(v, AXES, self.perm(lambda d, m: (d, m ^ 1)))

    def y(self, v):
        return lax.ppermute(v, AXES, self.perm(lambda d, m: (d, m ^ 2)))

    def x(self, v):
        return lax.ppermute(v, AXES, self.perm(lambda d, m: (d ^ 1, m)))

    def z(self, v, k):
        return lax.ppermute(v, AXES, self.perm(lambda d, m: (d ^ (2 * k), m)))

    def total(self, v, bits=None):
        for bit in bits or [1 << k for k in range(self.n.bit_length() - 1)]:
            v = v + lax.ppermute(v, AXES, [(i, i ^ bit) for i in range(self.n)])
        return v

    def order(self):
        d = lax.axis_index("dp")
        if not self.grid:
            return [jnp.int32(r) for r in range(self.n_dp)]
        z, x = d // 2, d % 2
        return [(z ^ dz) * 2 + (x ^ dx) for dx in range(2) for dz in range(4)]

    def places(self):
        d = lax.axis_index("dp")
        if not self.grid:
            return [jnp.int32(r) for r in range(self.n_dp)]
        z, x = d // 2, d % 2
        return [((a // 2) ^ z) + 4 * ((a % 2) ^ x) for a in range(8)]

    def gather_first(self, a, u, d, vector):
        if not self.grid:
            a, u, d = (lax.all_gather(p, "dp", axis=0, tiled=True) for p in (a, u, d))
            return ([a], [self.y(a)]), u, d, self.total(vector)
        rows, cols = u.shape
        cat = lambda *v: jnp.concatenate(v, axis=0)
        ax0, ay0 = self.x(a), self.y(a)
        az = tuple(self.z(a, k) for k in (1, 2, 3))
        vector = self.total(after(vector, ax0, ay0))
        ud = jnp.concatenate([u, d], axis=1)
        ud1 = self.z(after(ud, vector, *az), 1)
        az = cat(*az)
        axs, ays = self.x(az), self.y(az)
        ady, adx = self.y(after(cat(ax0, axs[:rows]), ays, ud1)), self.x(after(ays[rows:], axs, ud1))
        udx0 = self.x(after(ud, adx))
        u1, d1 = ud1[:, :cols], ud1[:, cols:]
        u23 = self.z(after(cat(u, u1), axs, ays), 2)
        return ([a, az, ax0, axs], [ay0, ays, ady, adx]), (u, u1, u23, udx0), (d, d1), vector

    def gather_rest(self, u, d, first):
        if not self.grid:
            return [u], [d]
        cat = lambda *v: jnp.concatenate(v, axis=0)
        (u, u1, u23, udx0), (d, d1) = u, d
        ux0, dx0 = udx0[:, : u.shape[1]], udx0[:, u.shape[1] :]
        uxs = self.x(after(cat(u1, u23), first))
        d23 = self.z(after(cat(d, d1), first), 2)
        dxs = self.x(after(cat(d1, d23), uxs))
        return [u, u1, u23, ux0, uxs], [d, d1, d23, dx0, dxs]

    def scatter_diagonal(self, part, rows):
        if not self.grid:
            return (self.y(part(1, 0, rows).astype(BF16)),), ()
        half = rows // 2
        middle = half + rows // 4
        sent = part(1, half, middle).astype(BF16), part(1, middle, rows).astype(BF16)
        return (self.y(sent[0]), self.x(sent[1])), sent

    def scatter_sides(self, part, rows, diagonal):
        if not self.grid:
            return diagonal
        e01, e23 = diagonal
        half, two = rows // 2, rows // 4
        cat = lambda *v: jnp.concatenate(v, axis=0)
        fx = self.x(cat((part(0, half, half + two) + e01).astype(BF16), part(0, half + two, rows).astype(BF16)))
        fy = self.y(cat(part(1, 0, two).astype(BF16), (part(1, two, half) + e23).astype(BF16)))
        return fx, fy

    def scatter_x(self, part, rows, *first):
        if not self.grid:
            return (), None
        sent = part(0, rows // 2, rows).astype(BF16)
        return (self.x(after(sent, *first)),), sent

    def scatter_two(self, part, rows, sides, *first):
        if not self.grid:
            mine = sum(sides, part(0, 0, rows))
            return None, lambda *_: lax.psum_scatter(mine, "dp", scatter_dimension=0, tiled=True)
        block = rows // 8
        q = sum(after(sides, *first) if first else sides, part(0, 0, 4 * block))

        def rest(got, *first):
            both = q[: 2 * block] + after(got, *first)
            return both[:block] + self.z(both[block:].astype(BF16), 1)

        return self.z(q[2 * block :].astype(BF16), 2), rest

    def scatter_z(self, part, rows, sides, *first):
        if not self.grid:
            mine = sum(sides, part(0, 0, rows))
            return lax.psum_scatter(mine, "dp", scatter_dimension=0, tiled=True)
        block = rows // 8
        q = sum(sides, part(0, 0, 4 * block))
        sent = [q[k * block : (k + 1) * block].astype(BF16) for k in (1, 2, 3)]
        return sum((self.z(v, k) for v, k in zip(sent, (1, 2, 3))), q[:block])


def norm_parts(values):
    center = values - jnp.mean(values, axis=-1, keepdims=True)
    spread = jnp.mean(center * center, axis=-1, keepdims=True)
    inverse = lax.rsqrt(spread + norm_eps)
    return center * inverse, inverse


def norm_back(normed, inverse, gain, grad):
    e = gain * grad
    return (
        e - jnp.mean(e, axis=-1, keepdims=True) - normed * jnp.mean(e * normed, axis=-1, keepdims=True)
    ) * inverse


def take_blocks(v, which, block):
    return jnp.concatenate(
        [lax.dynamic_slice_in_dim(v, w * block, block, axis=1) for w in which], axis=1
    )


def pad_rows(v, rows):
    return jnp.pad(v, ((0, rows - v.shape[0]), (0, 0)))


def slots_of(lengths, positions):
    ends = jnp.cumsum(lengths)
    starts = ends - lengths
    is_global = lengths == GLOBAL_LEN
    global_rank = jnp.cumsum(is_global.astype(jnp.int32)) - 1
    local_rank = jnp.cumsum(1 - is_global.astype(jnp.int32)) - 1
    base = jnp.where(
        is_global,
        GLOBAL_PAD * global_rank,
        2 * GLOBAL_PAD + LOCAL_TILE * (local_rank // PER_TILE) + LOCAL_LEN * (local_rank % PER_TILE),
    )
    inside = (positions[:, None] >= starts[None]) & (positions[:, None] < ends[None])
    return jnp.sum(jnp.where(inside, base[None] + positions[:, None] - starts[None], 0), axis=1)


VMEM_LIMIT = 48 * 1024 * 1024


def lanes_of(h, v):
    lane = lax.broadcasted_iota(jnp.int32, v.shape, 1)
    keep = (lane < HEAD_DIM) if h == 0 else (lane >= HEAD_DIM)
    return jnp.where(keep, v, jnp.zeros_like(v))


def two_heads(first, second):
    lane = lax.broadcasted_iota(jnp.int32, first.shape, 1)
    return jnp.where(lane < HEAD_DIM, first, second)


GLOBAL_TILES = [(0, GLOBAL_PAD, 256), (GLOBAL_PAD, GLOBAL_PAD, 256)]
LOCAL_TILES = [(2 * GLOBAL_PAD + LOCAL_TILE * k, LOCAL_TILE, LOCAL_TILE) for k in range(3)]


def tile_mask(queries, keys):
    row = lax.broadcasted_iota(jnp.int32, (queries, keys), 0)
    col = lax.broadcasted_iota(jnp.int32, (queries, keys), 1)
    if keys == 256:
        return col < GLOBAL_LEN
    same = None
    for k in range(4):
        lo, hi = k * LOCAL_LEN, (k + 1) * LOCAL_LEN if k < 3 else LOCAL_TILE
        inside = (row >= lo) & (row < hi) & (col >= lo) & (col < hi)
        same = inside if same is None else same | inside
    return same


def fill_picks(pick, pick_t, slot_row):
    places = lax.broadcasted_iota(jnp.int32, pick.shape, 0)
    row = slot_row[...]
    pick[...] = jnp.where(places == row, 1.0, 0.0).astype(BF16)
    col = jnp.transpose(jnp.broadcast_to(row.astype(F32), (8, row.shape[1])))[:, :1].astype(jnp.int32)
    places = lax.broadcasted_iota(jnp.int32, pick_t.shape, 1)
    pick_t[...] = jnp.where(places == col, 1.0, 0.0).astype(BF16)


def vmem():
    return pl.BlockSpec(memory_space=pltpu.VMEM)


def anywhere():
    return pl.BlockSpec(memory_space=pl.ANY)


def attend_kernel(counts, *refs):
    n = sum(counts)
    rows_own, rows_oth, slot_row = refs[:3]
    pieces = refs[3 : 3 + n]
    weights_out, slots_out, attended, keep, send, probs_g_out, probs_l_out = refs[3 + n : 10 + n]
    pick, pick_t, qkv, att_slots, weights, slots, probs_g, probs_l, sems, out_sems = refs[10 + n :]
    half = rows_own.shape[0]
    wide = qkv.shape[1]
    local = slots.shape[1] // 6
    three = 3 * local
    copies = [[], []]
    at = 0
    for g in range(2):
        row = 0
        for _ in range(counts[g]):
            piece = pieces[at]
            copies[g].append(
                pltpu.make_async_copy(piece, weights.at[g, pl.ds(row, piece.shape[0])], sems.at[at])
            )
            row += piece.shape[0]
            at += 1
    for c in copies[0] + copies[1]:
        c.start()
    fill_picks(pick, pick_t, slot_row)
    outs = []

    def put(src, dst):
        c = pltpu.make_async_copy(src, dst, out_sems.at[len(outs)])
        c.start()
        outs.append(c)

    for g in range(2):
        for c in copies[g]:
            c.wait()
        put(weights.at[g], weights_out.at[g])

        def project(n, _, g=g):
            cols = pl.ds(pl.multiple_of(n * wide, wide), wide)
            w = weights[g, :, cols]
            qkv[:half] = nn(rows_own[...], w).astype(BF16)
            qkv[half:] = nn(rows_oth[...], w).astype(BF16)
            out = pl.ds(pl.multiple_of(g * three + n * wide, wide), wide)
            slots[:, out] = nn(pick[...], qkv[...]).astype(BF16)
            return 0

        lax.fori_loop(0, three // wide, project, 0)
    put(slots, slots_out)
    pairs = local // 128
    for tiles, probs in ((GLOBAL_TILES, probs_g), (LOCAL_TILES, probs_l)):
        mask = tile_mask(*tiles[0][1:])
        for g in range(2):
            for p in range(pairs):
                base = g * three + p * 128
                units = [(t, first, queries, keys, h) for t, (first, queries, keys) in enumerate(tiles) for h in range(2)]
                scores = [
                    nt(
                        lanes_of(h, slots[first : first + queries, base : base + 128]),
                        slots[first : first + keys, base + local : base + local + 128],
                    )
                    for t, first, queries, keys, h in units
                ]
                scores = [jnp.where(mask, s * 0.125, masked_score) for s in scores]
                tops = [jnp.max(s, axis=1, keepdims=True) for s in scores]
                es = [jnp.exp(s - top) for s, top in zip(scores, tops)]
                sums = [1.0 / jnp.sum(e, axis=1, keepdims=True) for e in es]
                lows = []
                for (t, first, queries, keys, h), e, s in zip(units, es, sums):
                    prob = e * s
                    probs[(g * pairs + p) * 2 + h, t] = prob
                    lows.append(prob.astype(BF16))
                mixed = [
                    nn(low, slots[first : first + keys, base + 2 * local : base + 2 * local + 128])
                    for (t, first, queries, keys, h), low in zip(units, lows)
                ]
                for t, (first, queries, keys) in enumerate(tiles):
                    col = g * local + p * 128
                    att_slots[first : first + queries, col : col + 128] = two_heads(
                        mixed[2 * t], mixed[2 * t + 1]
                    ).astype(BF16)
        put(probs, probs_g_out if probs is probs_g else probs_l_out)
    attended[...] = nn(pick_t[...], att_slots[...]).astype(BF16)

    def back(n, _):
        rows = pl.ds(pl.multiple_of(n * 256, 256), 256)
        total = 0.0
        for g in range(2):
            w = weights[g, rows, three:]
            total = total + nt(attended[:, g * local : (g + 1) * local], w).astype(BF16).astype(F32)
        keep[:, rows] = total[:half]
        send[:, rows] = total[half:].astype(BF16)
        return 0

    lax.fori_loop(0, weights.shape[1] // 256, back, 0)
    for c in outs:
        c.wait()


def attend(rows_own, rows_oth, slot_row, own, oth):
    half, width = rows_own.shape
    cols = own[0].shape[1]
    local = cols // 4
    pieces = [*own, *oth]
    heads = 2 * local // HEAD_DIM
    shape = jax.ShapeDtypeStruct
    probs = ((heads, 2, GLOBAL_PAD, 256), (heads, 3, LOCAL_TILE, LOCAL_TILE))
    return pl.pallas_call(
        functools.partial(attend_kernel, (len(own), len(oth))),
        out_shape=(
            shape((2, width, cols), BF16),
            shape((SLOTS, 6 * local), BF16),
            shape((2 * half, 2 * local), BF16),
            shape((half, width), F32),
            shape((half, width), BF16),
            shape(probs[0], F32),
            shape(probs[1], F32),
        ),
        in_specs=[vmem()] * 3 + [anywhere()] * len(pieces),
        out_specs=(anywhere(), anywhere(), vmem(), vmem(), vmem(), anywhere(), anywhere()),
        scratch_shapes=[
            pltpu.VMEM((SLOTS, 2 * half), BF16),
            pltpu.VMEM((2 * half, SLOTS), BF16),
            pltpu.VMEM((2 * half, local), BF16),
            pltpu.VMEM((SLOTS, 2 * local), BF16),
            pltpu.VMEM((2, width, cols), BF16),
            pltpu.VMEM((SLOTS, 6 * local), BF16),
            pltpu.VMEM(probs[0], F32),
            pltpu.VMEM(probs[1], F32),
            pltpu.SemaphoreType.DMA((len(pieces),)),
            pltpu.SemaphoreType.DMA((5,)),
        ],
        compiler_params=pltpu.CompilerParams(vmem_limit_bytes=VMEM_LIMIT),
        cost_estimate=pl.CostEstimate(flops=1000, bytes_accessed=1000, transcendentals=0),
        name="attend",
    )(rows_own, rows_oth, slot_row, *pieces)


def attend_back_kernel(
    rows_own, rows_oth, slot_row, weights_in, slots_in, probs_g_in, probs_l_in, qkv_grad_out, keep, send,
    pick, pick_t, att, grads, slot_grads, weights, slots, probs_g, probs_l, qkv_grad, sems, out_sems,
):
    half = rows_own.shape[0]
    local = slots.shape[1] // 6
    three = 3 * local
    gets = [
        pltpu.make_async_copy(src, dst, sems.at[i])
        for i, (src, dst) in enumerate(
            (
                (weights_in.at[:, :, pl.ds(three, local)], weights.at[:, :, pl.ds(three, local)]),
                (slots_in, slots),
                (probs_g_in, probs_g),
                (probs_l_in, probs_l),
                (weights_in.at[:, :, pl.ds(0, three)], weights.at[:, :, pl.ds(0, three)]),
            )
        )
    ]
    for c in gets:
        c.start()
    fill_picks(pick, pick_t, slot_row)
    gets[0].wait()
    for g in range(2):
        w = weights[g, :, three:]
        att[:half, g * local : (g + 1) * local] = nn(rows_own[...], w).astype(BF16)
        att[half:, g * local : (g + 1) * local] = nn(rows_oth[...], w).astype(BF16)
    grads[...] = nn(pick[...], att[...]).astype(BF16)
    gets[1].wait()
    pairs = local // 128
    for tiles, probs, get in ((GLOBAL_TILES, probs_g, gets[2]), (LOCAL_TILES, probs_l, gets[3])):
        get.wait()
        for g in range(2):
            for p in range(pairs):
                base = g * three + p * 128
                col = g * local + p * 128
                units = [(t, first, queries, keys, h) for t, (first, queries, keys) in enumerate(tiles) for h in range(2)]

                def part(j, first, size):
                    return slots[first : first + size, base + j * local : base + j * local + 128]

                outs = [grads[first : first + queries, col : col + 128] for t, first, queries, keys, h in units]
                prob = [probs[(g * pairs + p) * 2 + h, t] for t, first, queries, keys, h in units]
                dps = [
                    nt(lanes_of(h, d), part(2, first, keys)) for (t, first, queries, keys, h), d in zip(units, outs)
                ]
                dvs = [tn(pr.astype(BF16), d) for pr, d in zip(prob, outs)]
                dots = [jnp.sum(dp * pr, axis=1, keepdims=True) for dp, pr in zip(dps, prob)]
                dss = [(pr * (dp - dot_)).astype(BF16) for pr, dp, dot_ in zip(prob, dps, dots)]
                dqs = [nn(ds, part(1, first, keys)) for (t, first, queries, keys, h), ds in zip(units, dss)]
                dks = [tn(ds, part(0, first, queries)) for (t, first, queries, keys, h), ds in zip(units, dss)]
                for t, (first, queries, keys) in enumerate(tiles):
                    for j, (two, factor) in enumerate(((dqs, 0.125), (dks, 0.125), (dvs, 1.0))):
                        both = two_heads(two[2 * t], two[2 * t + 1])
                        if factor != 1.0:
                            both = both * factor
                        slot_grads[first : first + queries, base + j * local : base + j * local + 128] = both[
                            :queries
                        ].astype(BF16)

    def unsort(n, _):
        cols = pl.ds(pl.multiple_of(n * local, local), local)
        qkv_grad[:, cols] = nn(pick_t[...], slot_grads[:, cols]).astype(BF16)
        return 0

    lax.fori_loop(0, 6, unsort, 0)
    put = pltpu.make_async_copy(qkv_grad, qkv_grad_out, out_sems.at[0])
    put.start()
    gets[4].wait()

    def back(n, _):
        rows = pl.ds(pl.multiple_of(n * 256, 256), 256)
        total = nt(qkv_grad[:, :three], weights[0, rows, :three]) + nt(qkv_grad[:, three:], weights[1, rows, :three])
        keep[:, rows] = total[:half]
        send[:, rows] = total[half:].astype(BF16)
        return 0

    lax.fori_loop(0, weights.shape[1] // 256, back, 0)
    put.wait()


def attend_back(rows_own, rows_oth, slot_row, weights, slots, probs_g, probs_l):
    half, width = rows_own.shape
    local = slots.shape[1] // 6
    shape = jax.ShapeDtypeStruct
    return pl.pallas_call(
        attend_back_kernel,
        out_shape=(
            shape((2 * half, 6 * local), BF16),
            shape((half, width), F32),
            shape((half, width), BF16),
        ),
        in_specs=[vmem()] * 3 + [anywhere()] * 4,
        out_specs=(anywhere(), vmem(), vmem()),
        scratch_shapes=[
            pltpu.VMEM((SLOTS, 2 * half), BF16),
            pltpu.VMEM((2 * half, SLOTS), BF16),
            pltpu.VMEM((2 * half, 2 * local), BF16),
            pltpu.VMEM((SLOTS, 2 * local), BF16),
            pltpu.VMEM((SLOTS, 6 * local), BF16),
            pltpu.VMEM(weights.shape, BF16),
            pltpu.VMEM(slots.shape, BF16),
            pltpu.VMEM(probs_g.shape, F32),
            pltpu.VMEM(probs_l.shape, F32),
            pltpu.VMEM((2 * half, 6 * local), BF16),
            pltpu.SemaphoreType.DMA((5,)),
            pltpu.SemaphoreType.DMA((1,)),
        ],
        compiler_params=pltpu.CompilerParams(vmem_limit_bytes=VMEM_LIMIT),
        cost_estimate=pl.CostEstimate(flops=1000, bytes_accessed=1000, transcendentals=0),
        name="attend_back",
    )(rows_own, rows_oth, slot_row, weights, slots, probs_g, probs_l)


def shards(comm, tokens, cotangent, crop_lengths, qkv_weight, out_weight, up_weight, down_weight, vectors,
           qkv_first, out_first, up_first, down_first, vector_first,
           qkv_second, out_second, up_second, down_second, vector_second):
    rows, width = tokens.shape
    padded = -(-rows // 16) * 16
    block = width // comm.n_dp
    own_index = lax.axis_index("mp")
    image, core = own_index // 2, own_index % 2
    flat_index = lax.axis_index("dp") * comm.n_mp + own_index
    local = qkv_weight.shape[2]
    hidden = up_weight.shape[1]
    order, places = comm.order(), comm.places()
    to_rel = lambda v: take_blocks(v, order, block)
    to_abs = lambda v: take_blocks(v, places, block)

    pack_a = jnp.concatenate([qkv_weight.reshape(-1, 3 * local), out_weight], axis=1).astype(BF16)
    vector_full = lax.dynamic_update_slice(
        jnp.zeros((6, width), F32), vectors.astype(BF16).astype(F32), (0, flat_index * vectors.shape[1])
    ).astype(BF16)
    (a_own, a_oth), up_part, down_part, vector_full = comm.gather_first(
        pack_a, up_weight.astype(BF16), down_weight.astype(BF16), vector_full
    )
    gain_one, shift_one, gain_two, shift_two, scale_one, scale_two = vector_full.astype(F32)
    cat = lambda blocks: jnp.concatenate(blocks, axis=0)
    lengths = lax.dynamic_index_in_dim(crop_lengths, image, 0, keepdims=False)
    lane = jnp.arange(padded, dtype=jnp.int32)
    positions = jnp.concatenate(
        [jnp.where(lane < rows, lane + half * rows, -1) for half in (core, 1 - core)]
    )
    slot = jnp.where(positions >= 0, slots_of(lengths, positions), -1)
    slot_row = slot[None, :]

    residual = tokens.astype(F32)
    normed_one, inverse_one = norm_parts(residual)
    norm_one = pad_rows(to_rel((normed_one * gain_one + shift_one).astype(BF16)), padded)
    norm_one_other = comm.core(norm_one)
    rows_one = cat([norm_one, norm_one_other])
    out_grad = cotangent.astype(F32)
    cot_y = comm.y(after(cotangent, *a_oth[-2:]))
    cot_mine = cat([pad_rows(cotangent, padded), pad_rows(cot_y, padded)])
    mlp_mine, mlp_mate = (
        to_rel((v.astype(F32) * scale_two).astype(BF16)) for v in (cot_mine, comm.core(cot_mine))
    )

    wide = 3 * local
    weights_a, slots, attended, keep, send, probs_g, probs_l = attend(
        norm_one, norm_one_other, slot_row, a_own, a_oth
    )

    def joined(keep, send):
        return to_abs(keep[:rows] + comm.core(send)[:rows].astype(F32))

    def spread(mine, mate, *first):
        total = mine + comm.core(mate.astype(BF16))
        sent = total[padded:].astype(BF16)
        return total[:padded], sent, comm.y(after(sent, *first))

    if comm.grid:
        send = after(send, *up_part[2:])
    up_blocks, down_blocks = comm.gather_rest(up_part, down_part, send)
    up_full = cat(up_blocks)
    branch_one = joined(keep, send)
    middle = residual + scale_one * branch_one
    normed_two, inverse_two = norm_parts(middle)
    norm_two = pad_rows(to_rel((normed_two * gain_two + shift_two).astype(BF16)), padded)
    norm_two_y = comm.y(norm_two)
    two_mine = cat([norm_two, norm_two_y])
    two_mate = comm.core(two_mine)
    if comm.grid:
        two_mate = after(two_mate, up_blocks[4])

    def activate(hidden_pre):
        cdf = 0.5 * (1.0 + lax.erf(hidden_pre * (0.5**0.5)))
        slope = cdf + hidden_pre * jnp.exp(-0.5 * hidden_pre * hidden_pre) * 0.3989422804014327
        return (hidden_pre * cdf).astype(BF16), slope

    act_mine, slope_mine = activate(nn(two_mine, up_full))
    act_mate, slope_mate = activate(nn(two_mate, up_full))
    down_part = lambda g, first, last: tn(mlp_mine[:, first:last], act_mine) + tn(mlp_mate[:, first:last], act_mate)
    down_full = cat(down_blocks)
    pre_mate = (nn(mlp_mate, down_full) * slope_mate).astype(BF16)
    pre_mine = (nn(mlp_mine, down_full) * slope_mine).astype(BF16)
    down_sums, sent = comm.scatter_x(down_part, width, pre_mine, pre_mate)
    mine, sent_y, from_y = spread(nt(pre_mine, up_full), nt(pre_mate, up_full))
    norm_two_grad = to_abs((mine + from_y)[:rows])
    pre_mine, pre_mate = after((pre_mine, pre_mate), sent_y)
    up_part = lambda g, first, last: tn(two_mine[:, first:last], pre_mine) + tn(two_mate[:, first:last], pre_mate)
    up_sums, sent = comm.scatter_x(up_part, width)
    middle_grad = out_grad + norm_back(normed_two, inverse_two, gain_two, norm_two_grad)
    grad_gain_two = jnp.sum(norm_two_grad * normed_two, axis=0)
    grad_shift_two = jnp.sum(norm_two_grad, axis=0)
    grad_scale_one = jnp.sum(middle_grad * branch_one, axis=0)
    attn_own = pad_rows(to_rel((middle_grad * scale_one).astype(BF16)), padded)
    attn_other = comm.core(attn_own)
    attn_rows = cat([attn_own, attn_other])
    branch_own, branch_mate = after((act_mine, act_mate), sent_y)
    branch_mine, _, branch_y = spread(
        nt(branch_own, down_full).astype(BF16).astype(F32), nt(branch_mate, down_full), from_y
    )

    qkv_grad, keep, send = attend_back(
        attn_own, attn_other, slot_row, weights_a, slots, probs_g, probs_l
    )
    branch_two = to_abs((branch_mine + after(branch_y, send))[:rows])
    output = (middle + scale_two * branch_two).astype(BF16)
    grad_scale_two = jnp.sum(out_grad * branch_two, axis=0)

    def a_part(g, first, last):
        qkv_cols, out_cols = slice(g * wide, (g + 1) * wide), slice(g * local, (g + 1) * local)
        return jnp.concatenate(
            [tn(rows_one[:, first:last], qkv_grad[:, qkv_cols]), tn(attn_rows[:, first:last], attended[:, out_cols])],
            axis=1,
        )

    a_sums, first = comm.scatter_diagonal(a_part, width)
    down_got, down_rest = comm.scatter_two(down_part, width, down_sums, from_y)
    late_mine, late_mate = after((pre_mine, pre_mate), send)
    up_late = lambda g, first, last: tn(two_mine[:, first:last], late_mine) + tn(two_mate[:, first:last], late_mate)
    up_got, up_rest = comm.scatter_two(up_late, width, up_sums, *first)
    down_share = down_rest(down_got, *first)
    norm_one_grad = joined(keep, send)
    input_grad = (middle_grad + norm_back(normed_one, inverse_one, gain_one, norm_one_grad)).astype(BF16)
    grad_gain_one = jnp.sum(norm_one_grad * normed_one, axis=0)
    grad_shift_one = jnp.sum(norm_one_grad, axis=0)

    vector_grad = jnp.stack(
        [grad_gain_one, grad_shift_one, grad_gain_two, grad_shift_two, grad_scale_one, grad_scale_two]
    )
    bits = [1 << k for k in range(comm.n.bit_length() - 1)]
    vector_grad = comm.total(after(vector_grad, *a_sums), (*bits[3:], bits[0]))
    a_sums = comm.scatter_sides(a_part, width, a_sums)
    if comm.grid:
        a_sums, up_got = lax.optimization_barrier((a_sums, up_got))
    up_share = up_rest(up_got)
    vector_grad = comm.total(after(vector_grad, *a_sums), bits[1:3])
    a_share = comm.scatter_z(a_part, width, a_sums)
    vector_share = lax.dynamic_slice_in_dim(
        vector_grad, flat_index * vectors.shape[1], vectors.shape[1], axis=1
    )
    matrix = lambda w, g, m, v: adamw_step(w, g, m, v, matrix_rate, matrix_decay)
    qkv_parts = [
        matrix(qkv_weight[:, k], a_share[:, k * local : (k + 1) * local], qkv_first[:, k], qkv_second[:, k])
        for k in range(3)
    ]
    return (
        output,
        input_grad,
        *(jnp.stack(v, axis=1) for v in zip(*qkv_parts)),
        *matrix(out_weight, a_share[:, wide:], out_first, out_second),
        *matrix(up_weight, up_share, up_first, up_second),
        *matrix(down_weight, down_share, down_first, down_second),
        *adamw_step(vectors, vector_share, vector_first, vector_second, vector_rate, 0.0),
    )


def solution(mesh):
    comm = Comm(mesh.shape["dp"], mesh.shape["mp"])
    rows = P(("dp", "mp"), None)
    cube = P("dp", None, "mp")
    flat = P("dp", "mp")
    vec = P(None, ("dp", "mp"))
    moments = (cube, flat, flat, flat, vec)
    return jax.shard_map(
        lambda *args: shards(comm, *args),
        mesh=mesh,
        in_specs=(rows, rows, P("dp", None), *moments, *moments, *moments),
        out_specs=(rows, rows, *(spec for spec in moments for _ in range(3))),
        check_vma=False,
    )
```

```python
import functools

import jax
import jax.numpy as jnp
from jax import lax
from jax.experimental import pallas as pl
from jax.experimental.pallas import tpu as pltpu
from jax.sharding import PartitionSpec as P

HEAD_DIM = 64
STEP = 10
GLOBAL_LEN = 197
LOCAL_LEN = 37
GLOBAL_PAD = 208
LOCAL_TILE = 128
PER_TILE = 3
SLOTS = 2 * GLOBAL_PAD + 3 * LOCAL_TILE

norm_eps = 1e-06
masked_score = -1e30
beta_first = 0.9
beta_second = 0.999
adam_eps = 1e-08
matrix_rate = 0.1
vector_rate = 1.25
matrix_decay = 0.04

F32 = jnp.float32
BF16 = jnp.bfloat16
AXES = ("dp", "mp")


def dot(a, b, dims):
    return lax.dot_general(a, b, (dims, ((), ())), preferred_element_type=F32)


def nn(a, b):
    return dot(a, b, ((1,), (0,)))


def nt(a, b):
    return dot(a, b, ((1,), (1,)))


def tn(a, b):
    return dot(a, b, ((0,), (0,)))


def adamw_step(weight, gradient, first_old, second_old, step_rate, decay_rate):
    first_new = beta_first * first_old + (1.0 - beta_first) * gradient
    second_new = beta_second * second_old + (1.0 - beta_second) * gradient * gradient
    first_hat = first_new / (1.0 - beta_first**STEP)
    second_hat = second_new / (1.0 - beta_second**STEP)
    weight_new = weight - step_rate * (
        first_hat / (jnp.sqrt(second_hat) + adam_eps) + decay_rate * weight
    )
    return (weight_new, first_new, second_new)


def after(v, *first):
    return lax.optimization_barrier((v, first))[0]


class Comm:
    def __init__(self, n_dp, n_mp):
        self.n_dp, self.n_mp = n_dp, n_mp
        self.n = n_dp * n_mp
        self.grid = n_dp == 8 and n_mp == 4

    def perm(self, f):
        out = []
        for d in range(self.n_dp):
            for m in range(self.n_mp):
                td, tm = f(d, m)
                out.append((d * self.n_mp + m, td * self.n_mp + tm))
        return out

    def core(self, v):
        return lax.ppermute(v, AXES, self.perm(lambda d, m: (d, m ^ 1)))

    def y(self, v):
        return lax.ppermute(v, AXES, self.perm(lambda d, m: (d, m ^ 2)))

    def x(self, v):
        return lax.ppermute(v, AXES, self.perm(lambda d, m: (d ^ 1, m)))

    def z(self, v, k):
        return lax.ppermute(v, AXES, self.perm(lambda d, m: (d ^ (2 * k), m)))

    def total(self, v, bits=None):
        for bit in bits or [1 << k for k in range(self.n.bit_length() - 1)]:
            v = v + lax.ppermute(v, AXES, [(i, i ^ bit) for i in range(self.n)])
        return v

    def order(self):
        d = lax.axis_index("dp")
        if not self.grid:
            return [jnp.int32(r) for r in range(self.n_dp)]
        z, x = d // 2, d % 2
        return [(z ^ dz) * 2 + (x ^ dx) for dx in range(2) for dz in range(4)]

    def places(self):
        d = lax.axis_index("dp")
        if not self.grid:
            return [jnp.int32(r) for r in range(self.n_dp)]
        z, x = d // 2, d % 2
        return [((a // 2) ^ z) + 4 * ((a % 2) ^ x) for a in range(8)]

    def gather_first(self, a, u, d, vector):
        if not self.grid:
            a, u, d = (lax.all_gather(p, "dp", axis=0, tiled=True) for p in (a, u, d))
            return ([a], [self.y(a)]), u, d, self.total(vector)
        rows, cols = u.shape
        cat = lambda *v: jnp.concatenate(v, axis=0)
        ax0, ay0 = self.x(a), self.y(a)
        az = tuple(self.z(a, k) for k in (1, 2, 3))
        vector = self.total(after(vector, ax0, ay0))
        ud = jnp.concatenate([u, d], axis=1)
        ud1 = self.z(after(ud, vector, *az), 1)
        az = cat(*az)
        axs, ays = self.x(az), self.y(az)
        ady, adx = self.y(after(cat(ax0, axs[:rows]), ays, ud1)), self.x(after(ays[rows:], axs, ud1))
        udx0 = self.x(after(ud, adx))
        u1, d1 = ud1[:, :cols], ud1[:, cols:]
        u23 = self.z(after(cat(u, u1), axs, ays), 2)
        return ([a, az, ax0, axs], [ay0, ays, ady, adx]), (u, u1, u23, udx0), (d, d1), vector

    def gather_rest(self, u, d, first):
        if not self.grid:
            return [u], [d]
        cat = lambda *v: jnp.concatenate(v, axis=0)
        (u, u1, u23, udx0), (d, d1) = u, d
        ux0, dx0 = udx0[:, : u.shape[1]], udx0[:, u.shape[1] :]
        uxs = self.x(after(cat(u1, u23), first))
        d23 = self.z(after(cat(d, d1), first), 2)
        dxs = self.x(after(cat(d1, d23), uxs))
        return [u, u1, u23, ux0, uxs], [d, d1, d23, dx0, dxs]

    def scatter_diagonal(self, part, rows):
        if not self.grid:
            return (self.y(part(1, 0, rows).astype(BF16)),), ()
        half = rows // 2
        middle = half + rows // 4
        sent = part(1, half, middle).astype(BF16), part(1, middle, rows).astype(BF16)
        return (self.y(sent[0]), self.x(sent[1])), sent

    def scatter_sides(self, part, rows, diagonal):
        if not self.grid:
            return diagonal, ()
        e01, e23 = diagonal
        half, two = rows // 2, rows // 4
        cat = lambda *v: jnp.concatenate(v, axis=0)
        to_x = cat((part(0, half, half + two) + e01).astype(BF16), part(0, half + two, rows).astype(BF16))
        to_y = cat(part(1, 0, two).astype(BF16), (part(1, two, half) + e23).astype(BF16))
        return (self.x(to_x), self.y(to_y)), (to_x, to_y)

    def scatter_x(self, part, rows, *first):
        if not self.grid:
            return (), None
        sent = part(0, rows // 2, rows).astype(BF16)
        return (self.x(after(sent, *first)),), sent

    def scatter_two(self, part, rows, sides, *first):
        if not self.grid:
            mine = sum(sides, part(0, 0, rows))
            return None, lambda *_: lax.psum_scatter(mine, "dp", scatter_dimension=0, tiled=True)
        block = rows // 8
        q = sum(after(sides, *first) if first else sides, part(0, 0, 4 * block))

        def rest(got, *first):
            both = q[: 2 * block] + after(got, *first)
            return both[:block] + self.z(both[block:].astype(BF16), 1)

        return self.z(q[2 * block :].astype(BF16), 2), rest

    def fold(self, v, send):
        half = v.shape[0] // 2
        return v[:half] + send(v[half:].astype(BF16))

    def scatter_z(self, part, rows, sides, *first):
        if not self.grid:
            mine = sum(sides, part(0, 0, rows))
            return lax.psum_scatter(mine, "dp", scatter_dimension=0, tiled=True)
        block = rows // 8
        q = sum(sides, part(0, 0, 4 * block))
        sent = [q[k * block : (k + 1) * block].astype(BF16) for k in (1, 2, 3)]
        return sum((self.z(v, k) for v, k in zip(sent, (1, 2, 3))), q[:block])


def norm_parts(values):
    center = values - jnp.mean(values, axis=-1, keepdims=True)
    spread = jnp.mean(center * center, axis=-1, keepdims=True)
    inverse = lax.rsqrt(spread + norm_eps)
    return center * inverse, inverse


def norm_back(normed, inverse, gain, grad):
    e = gain * grad
    return (
        e - jnp.mean(e, axis=-1, keepdims=True) - normed * jnp.mean(e * normed, axis=-1, keepdims=True)
    ) * inverse


def take_blocks(v, which, block):
    return jnp.concatenate(
        [lax.dynamic_slice_in_dim(v, w * block, block, axis=1) for w in which], axis=1
    )


def pad_rows(v, rows):
    return jnp.pad(v, ((0, rows - v.shape[0]), (0, 0)))


def slots_of(lengths, positions):
    ends = jnp.cumsum(lengths)
    starts = ends - lengths
    is_global = lengths == GLOBAL_LEN
    global_rank = jnp.cumsum(is_global.astype(jnp.int32)) - 1
    local_rank = jnp.cumsum(1 - is_global.astype(jnp.int32)) - 1
    base = jnp.where(
        is_global,
        GLOBAL_PAD * global_rank,
        2 * GLOBAL_PAD + LOCAL_TILE * (local_rank // PER_TILE) + LOCAL_LEN * (local_rank % PER_TILE),
    )
    inside = (positions[:, None] >= starts[None]) & (positions[:, None] < ends[None])
    return jnp.sum(jnp.where(inside, base[None] + positions[:, None] - starts[None], 0), axis=1)


VMEM_LIMIT = 48 * 1024 * 1024


def lanes_of(h, v):
    lane = lax.broadcasted_iota(jnp.int32, v.shape, 1)
    keep = (lane < HEAD_DIM) if h == 0 else (lane >= HEAD_DIM)
    return jnp.where(keep, v, jnp.zeros_like(v))


def two_heads(first, second):
    lane = lax.broadcasted_iota(jnp.int32, first.shape, 1)
    return jnp.where(lane < HEAD_DIM, first, second)


GLOBAL_TILES = [(0, GLOBAL_PAD, 256), (GLOBAL_PAD, GLOBAL_PAD, 256)]
LOCAL_TILES = [(2 * GLOBAL_PAD + LOCAL_TILE * k, LOCAL_TILE, LOCAL_TILE) for k in range(3)]


def tile_mask(queries, keys):
    row = lax.broadcasted_iota(jnp.int32, (queries, keys), 0)
    col = lax.broadcasted_iota(jnp.int32, (queries, keys), 1)
    if keys == 256:
        return col < GLOBAL_LEN
    same = None
    for k in range(4):
        lo, hi = k * LOCAL_LEN, (k + 1) * LOCAL_LEN if k < 3 else LOCAL_TILE
        inside = (row >= lo) & (row < hi) & (col >= lo) & (col < hi)
        same = inside if same is None else same | inside
    return same


def fill_picks(pick, pick_t, slot_row):
    places = lax.broadcasted_iota(jnp.int32, pick.shape, 0)
    row = slot_row[...]
    pick[...] = jnp.where(places == row, 1.0, 0.0).astype(BF16)
    col = jnp.transpose(jnp.broadcast_to(row.astype(F32), (8, row.shape[1])))[:, :1].astype(jnp.int32)
    places = lax.broadcasted_iota(jnp.int32, pick_t.shape, 1)
    pick_t[...] = jnp.where(places == col, 1.0, 0.0).astype(BF16)


def vmem():
    return pl.BlockSpec(memory_space=pltpu.VMEM)


def anywhere():
    return pl.BlockSpec(memory_space=pl.ANY)


def attend_kernel(counts, *refs):
    n = sum(counts)
    rows_own, rows_oth, slot_row = refs[:3]
    pieces = refs[3 : 3 + n]
    weights_out, slots_out, attended, keep, send, probs_g_out, probs_l_out = refs[3 + n : 10 + n]
    pick, pick_t, qkv, att_slots, weights, slots, probs_g, probs_l, sems, out_sems = refs[10 + n :]
    half = rows_own.shape[0]
    wide = qkv.shape[1]
    local = slots.shape[1] // 6
    three = 3 * local
    copies = [[], []]
    at = 0
    for g in range(2):
        row = 0
        for _ in range(counts[g]):
            piece = pieces[at]
            copies[g].append(
                pltpu.make_async_copy(piece, weights.at[g, pl.ds(row, piece.shape[0])], sems.at[at])
            )
            row += piece.shape[0]
            at += 1
    for c in copies[0] + copies[1]:
        c.start()
    fill_picks(pick, pick_t, slot_row)
    outs = []

    def put(src, dst):
        c = pltpu.make_async_copy(src, dst, out_sems.at[len(outs)])
        c.start()
        outs.append(c)

    for g in range(2):
        for c in copies[g]:
            c.wait()
        put(weights.at[g], weights_out.at[g])

        def project(n, _, g=g):
            cols = pl.ds(pl.multiple_of(n * wide, wide), wide)
            w = weights[g, :, cols]
            qkv[:half] = nn(rows_own[...], w).astype(BF16)
            qkv[half:] = nn(rows_oth[...], w).astype(BF16)
            out = pl.ds(pl.multiple_of(g * three + n * wide, wide), wide)
            slots[:, out] = nn(pick[...], qkv[...]).astype(BF16)
            return 0

        lax.fori_loop(0, three // wide, project, 0)
    put(slots, slots_out)
    pairs = local // 128
    for tiles, probs in ((GLOBAL_TILES, probs_g), (LOCAL_TILES, probs_l)):
        mask = tile_mask(*tiles[0][1:])
        for g in range(2):
            for p in range(pairs):
                base = g * three + p * 128
                units = [(t, first, queries, keys, h) for t, (first, queries, keys) in enumerate(tiles) for h in range(2)]
                scores = [
                    nt(
                        lanes_of(h, slots[first : first + queries, base : base + 128]),
                        slots[first : first + keys, base + local : base + local + 128],
                    )
                    for t, first, queries, keys, h in units
                ]
                scores = [jnp.where(mask, s * 0.125, masked_score) for s in scores]
                tops = [jnp.max(s, axis=1, keepdims=True) for s in scores]
                es = [jnp.exp(s - top) for s, top in zip(scores, tops)]
                sums = [1.0 / jnp.sum(e, axis=1, keepdims=True) for e in es]
                lows = []
                for (t, first, queries, keys, h), e, s in zip(units, es, sums):
                    prob = e * s
                    probs[(g * pairs + p) * 2 + h, t] = prob
                    lows.append(prob.astype(BF16))
                mixed = [
                    nn(low, slots[first : first + keys, base + 2 * local : base + 2 * local + 128])
                    for (t, first, queries, keys, h), low in zip(units, lows)
                ]
                for t, (first, queries, keys) in enumerate(tiles):
                    col = g * local + p * 128
                    att_slots[first : first + queries, col : col + 128] = two_heads(
                        mixed[2 * t], mixed[2 * t + 1]
                    ).astype(BF16)
        put(probs, probs_g_out if probs is probs_g else probs_l_out)
    attended[...] = nn(pick_t[...], att_slots[...]).astype(BF16)

    def back(n, _):
        rows = pl.ds(pl.multiple_of(n * 256, 256), 256)
        total = 0.0
        for g in range(2):
            w = weights[g, rows, three:]
            total = total + nt(attended[:, g * local : (g + 1) * local], w).astype(BF16).astype(F32)
        keep[:, rows] = total[:half]
        send[:, rows] = total[half:].astype(BF16)
        return 0

    lax.fori_loop(0, weights.shape[1] // 256, back, 0)
    for c in outs:
        c.wait()


def attend(rows_own, rows_oth, slot_row, own, oth):
    half, width = rows_own.shape
    cols = own[0].shape[1]
    local = cols // 4
    pieces = [*own, *oth]
    heads = 2 * local // HEAD_DIM
    shape = jax.ShapeDtypeStruct
    probs = ((heads, 2, GLOBAL_PAD, 256), (heads, 3, LOCAL_TILE, LOCAL_TILE))
    return pl.pallas_call(
        functools.partial(attend_kernel, (len(own), len(oth))),
        out_shape=(
            shape((2, width, cols), BF16),
            shape((SLOTS, 6 * local), BF16),
            shape((2 * half, 2 * local), BF16),
            shape((half, width), F32),
            shape((half, width), BF16),
            shape(probs[0], F32),
            shape(probs[1], F32),
        ),
        in_specs=[vmem()] * 3 + [anywhere()] * len(pieces),
        out_specs=(anywhere(), anywhere(), vmem(), vmem(), vmem(), anywhere(), anywhere()),
        scratch_shapes=[
            pltpu.VMEM((SLOTS, 2 * half), BF16),
            pltpu.VMEM((2 * half, SLOTS), BF16),
            pltpu.VMEM((2 * half, local), BF16),
            pltpu.VMEM((SLOTS, 2 * local), BF16),
            pltpu.VMEM((2, width, cols), BF16),
            pltpu.VMEM((SLOTS, 6 * local), BF16),
            pltpu.VMEM(probs[0], F32),
            pltpu.VMEM(probs[1], F32),
            pltpu.SemaphoreType.DMA((len(pieces),)),
            pltpu.SemaphoreType.DMA((5,)),
        ],
        compiler_params=pltpu.CompilerParams(vmem_limit_bytes=VMEM_LIMIT),
        cost_estimate=pl.CostEstimate(flops=1000, bytes_accessed=1000, transcendentals=0),
        name="attend",
    )(rows_own, rows_oth, slot_row, *pieces)


def attend_back_kernel(
    rows_own, rows_oth, slot_row, weights_in, slots_in, probs_g_in, probs_l_in, qkv_grad_out, keep, send,
    pick, pick_t, att, grads, slot_grads, weights, slots, probs_g, probs_l, qkv_grad, sems, out_sems,
):
    half = rows_own.shape[0]
    local = slots.shape[1] // 6
    three = 3 * local
    gets = [
        pltpu.make_async_copy(src, dst, sems.at[i])
        for i, (src, dst) in enumerate(
            (
                (weights_in.at[:, :, pl.ds(three, local)], weights.at[:, :, pl.ds(three, local)]),
                (slots_in, slots),
                (probs_g_in, probs_g),
                (probs_l_in, probs_l),
                (weights_in.at[:, :, pl.ds(0, three)], weights.at[:, :, pl.ds(0, three)]),
            )
        )
    ]
    for c in gets:
        c.start()
    fill_picks(pick, pick_t, slot_row)
    gets[0].wait()
    for g in range(2):
        w = weights[g, :, three:]
        att[:half, g * local : (g + 1) * local] = nn(rows_own[...], w).astype(BF16)
        att[half:, g * local : (g + 1) * local] = nn(rows_oth[...], w).astype(BF16)
    grads[...] = nn(pick[...], att[...]).astype(BF16)
    gets[1].wait()
    pairs = local // 128
    for tiles, probs, get in ((GLOBAL_TILES, probs_g, gets[2]), (LOCAL_TILES, probs_l, gets[3])):
        get.wait()
        for g in range(2):
            for p in range(pairs):
                base = g * three + p * 128
                col = g * local + p * 128
                units = [(t, first, queries, keys, h) for t, (first, queries, keys) in enumerate(tiles) for h in range(2)]

                def part(j, first, size):
                    return slots[first : first + size, base + j * local : base + j * local + 128]

                outs = [grads[first : first + queries, col : col + 128] for t, first, queries, keys, h in units]
                prob = [probs[(g * pairs + p) * 2 + h, t] for t, first, queries, keys, h in units]
                dps = [
                    nt(lanes_of(h, d), part(2, first, keys)) for (t, first, queries, keys, h), d in zip(units, outs)
                ]
                dvs = [tn(pr.astype(BF16), d) for pr, d in zip(prob, outs)]
                dots = [jnp.sum(dp * pr, axis=1, keepdims=True) for dp, pr in zip(dps, prob)]
                dss = [(pr * (dp - dot_)).astype(BF16) for pr, dp, dot_ in zip(prob, dps, dots)]
                dqs = [nn(ds, part(1, first, keys)) for (t, first, queries, keys, h), ds in zip(units, dss)]
                dks = [tn(ds, part(0, first, queries)) for (t, first, queries, keys, h), ds in zip(units, dss)]
                for t, (first, queries, keys) in enumerate(tiles):
                    for j, (two, factor) in enumerate(((dqs, 0.125), (dks, 0.125), (dvs, 1.0))):
                        both = two_heads(two[2 * t], two[2 * t + 1])
                        if factor != 1.0:
                            both = both * factor
                        slot_grads[first : first + queries, base + j * local : base + j * local + 128] = both[
                            :queries
                        ].astype(BF16)

    def unsort(n, _):
        cols = pl.ds(pl.multiple_of(n * local, local), local)
        qkv_grad[:, cols] = nn(pick_t[...], slot_grads[:, cols]).astype(BF16)
        return 0

    lax.fori_loop(0, 6, unsort, 0)
    put = pltpu.make_async_copy(qkv_grad, qkv_grad_out, out_sems.at[0])
    put.start()
    gets[4].wait()

    def back(n, _):
        rows = pl.ds(pl.multiple_of(n * 256, 256), 256)
        total = nt(qkv_grad[:, :three], weights[0, rows, :three]) + nt(qkv_grad[:, three:], weights[1, rows, :three])
        keep[:, rows] = total[:half]
        send[:, rows] = total[half:].astype(BF16)
        return 0

    lax.fori_loop(0, weights.shape[1] // 256, back, 0)
    put.wait()


def attend_back(rows_own, rows_oth, slot_row, weights, slots, probs_g, probs_l):
    half, width = rows_own.shape
    local = slots.shape[1] // 6
    shape = jax.ShapeDtypeStruct
    return pl.pallas_call(
        attend_back_kernel,
        out_shape=(
            shape((2 * half, 6 * local), BF16),
            shape((half, width), F32),
            shape((half, width), BF16),
        ),
        in_specs=[vmem()] * 3 + [anywhere()] * 4,
        out_specs=(anywhere(), vmem(), vmem()),
        scratch_shapes=[
            pltpu.VMEM((SLOTS, 2 * half), BF16),
            pltpu.VMEM((2 * half, SLOTS), BF16),
            pltpu.VMEM((2 * half, 2 * local), BF16),
            pltpu.VMEM((SLOTS, 2 * local), BF16),
            pltpu.VMEM((SLOTS, 6 * local), BF16),
            pltpu.VMEM(weights.shape, BF16),
            pltpu.VMEM(slots.shape, BF16),
            pltpu.VMEM(probs_g.shape, F32),
            pltpu.VMEM(probs_l.shape, F32),
            pltpu.VMEM((2 * half, 6 * local), BF16),
            pltpu.SemaphoreType.DMA((5,)),
            pltpu.SemaphoreType.DMA((1,)),
        ],
        compiler_params=pltpu.CompilerParams(vmem_limit_bytes=VMEM_LIMIT),
        cost_estimate=pl.CostEstimate(flops=1000, bytes_accessed=1000, transcendentals=0),
        name="attend_back",
    )(rows_own, rows_oth, slot_row, weights, slots, probs_g, probs_l)


def shards(comm, tokens, cotangent, crop_lengths, qkv_weight, out_weight, up_weight, down_weight, vectors,
           qkv_first, out_first, up_first, down_first, vector_first,
           qkv_second, out_second, up_second, down_second, vector_second):
    rows, width = tokens.shape
    padded = -(-rows // 16) * 16
    block = width // comm.n_dp
    own_index = lax.axis_index("mp")
    image, core = own_index // 2, own_index % 2
    flat_index = lax.axis_index("dp") * comm.n_mp + own_index
    local = qkv_weight.shape[2]
    hidden = up_weight.shape[1]
    order, places = comm.order(), comm.places()
    to_rel = lambda v: take_blocks(v, order, block)
    to_abs = lambda v: take_blocks(v, places, block)

    pack_a = jnp.concatenate([qkv_weight.reshape(-1, 3 * local), out_weight], axis=1).astype(BF16)
    vector_full = lax.dynamic_update_slice(
        jnp.zeros((6, width), F32), vectors.astype(BF16).astype(F32), (0, flat_index * vectors.shape[1])
    ).astype(BF16)
    (a_own, a_oth), up_part, down_part, vector_full = comm.gather_first(
        pack_a, up_weight.astype(BF16), down_weight.astype(BF16), vector_full
    )
    gain_one, shift_one, gain_two, shift_two, scale_one, scale_two = vector_full.astype(F32)
    cat = lambda blocks: jnp.concatenate(blocks, axis=0)
    lengths = lax.dynamic_index_in_dim(crop_lengths, image, 0, keepdims=False)
    lane = jnp.arange(padded, dtype=jnp.int32)
    positions = jnp.concatenate(
        [jnp.where(lane < rows, lane + half * rows, -1) for half in (core, 1 - core)]
    )
    slot = jnp.where(positions >= 0, slots_of(lengths, positions), -1)
    slot_row = slot[None, :]

    residual = tokens.astype(F32)
    normed_one, inverse_one = norm_parts(residual)
    norm_one = pad_rows(to_rel((normed_one * gain_one + shift_one).astype(BF16)), padded)
    norm_one_other = comm.core(norm_one)
    rows_one = cat([norm_one, norm_one_other])
    out_grad = cotangent.astype(F32)
    cot_y = comm.y(after(cotangent, *a_oth[-2:]))
    wide = 3 * local
    weights_a, slots, attended, keep, send, probs_g, probs_l = attend(
        norm_one, norm_one_other, slot_row, a_own, a_oth
    )

    def joined(keep, send):
        return to_abs(keep[:rows] + comm.core(send)[:rows].astype(F32))

    def spread(mine, mate, *first):
        total = mine + comm.core(mate.astype(BF16))
        sent = total[padded:].astype(BF16)
        return total[:padded], sent, comm.y(after(sent, *first))

    if comm.grid:
        send = after(send, *up_part[2:])
    up_blocks, down_blocks = comm.gather_rest(up_part, down_part, send)
    up_full = cat(up_blocks)
    branch_one = joined(keep, send)
    middle = residual + scale_one * branch_one
    normed_two, inverse_two = norm_parts(middle)
    norm_two = pad_rows(to_rel((normed_two * gain_two + shift_two).astype(BF16)), padded)
    norm_two_y = comm.y(norm_two)
    cot_mine = cat([pad_rows(cotangent, padded), pad_rows(cot_y, padded)])
    cot_mine = after(cot_mine, norm_two)
    mlp_mine, mlp_mate = (
        to_rel((v.astype(F32) * scale_two).astype(BF16)) for v in (cot_mine, comm.core(cot_mine))
    )

    two_mine = cat([norm_two, norm_two_y])
    two_mate = comm.core(two_mine)
    if comm.grid:
        two_mate = after(two_mate, up_blocks[4])

    def activate(hidden_pre):
        cdf = 0.5 * (1.0 + lax.erf(hidden_pre * (0.5**0.5)))
        slope = cdf + hidden_pre * jnp.exp(-0.5 * hidden_pre * hidden_pre) * 0.3989422804014327
        return (hidden_pre * cdf).astype(BF16), slope

    act_mine, slope_mine = activate(nn(two_mine, up_full))
    act_mate, slope_mate = activate(nn(two_mate, up_full))
    down_part = lambda g, first, last: tn(mlp_mine[:, first:last], act_mine) + tn(mlp_mate[:, first:last], act_mate)
    if comm.grid:
        down_last, act_mine, act_mate, slope_mine, slope_mate = lax.optimization_barrier(
            (down_blocks[-1], act_mine, act_mate, slope_mine, slope_mate)
        )
        down_blocks = [*down_blocks[:-1], down_last]
    down_full = cat(down_blocks)
    pre_mate = (nn(mlp_mate, down_full) * slope_mate).astype(BF16)
    pre_mine = (nn(mlp_mine, down_full) * slope_mine).astype(BF16)
    down_sums, sent = comm.scatter_x(down_part, width, pre_mine, pre_mate)
    mine, sent_y, from_y = spread(nt(pre_mine, up_full), nt(pre_mate, up_full))
    norm_two_grad = to_abs((mine + from_y)[:rows])
    pre_mine, pre_mate = after((pre_mine, pre_mate), sent_y)
    up_part = lambda g, first, last: tn(two_mine[:, first:last], pre_mine) + tn(two_mate[:, first:last], pre_mate)
    up_sums, sent = comm.scatter_x(up_part, width)
    middle_grad = out_grad + norm_back(normed_two, inverse_two, gain_two, norm_two_grad)
    grad_gain_two = jnp.sum(norm_two_grad * normed_two, axis=0)
    grad_shift_two = jnp.sum(norm_two_grad, axis=0)
    grad_scale_one = jnp.sum(middle_grad * branch_one, axis=0)
    attn_own = pad_rows(to_rel((middle_grad * scale_one).astype(BF16)), padded)
    attn_other = comm.core(attn_own)
    attn_rows = cat([attn_own, attn_other])
    branch_own, branch_mate = after((act_mine, act_mate), sent_y)
    branch_mine, _, branch_y = spread(
        nt(branch_own, down_full).astype(BF16).astype(F32), nt(branch_mate, down_full), from_y
    )

    def out_part(g, first, last):
        return tn(attn_rows[:, first:last], attended[:, g * local : (g + 1) * local])

    out_y = comm.y(out_part(1, 0, width).astype(BF16))

    qkv_grad, keep, send = attend_back(
        attn_own, attn_other, slot_row, weights_a, slots, probs_g, probs_l
    )
    branch_two = to_abs((branch_mine + after(branch_y, send))[:rows])
    output = (middle + scale_two * branch_two).astype(BF16)
    grad_scale_two = jnp.sum(out_grad * branch_two, axis=0)

    def qkv_part(g, first, last):
        return tn(rows_one[:, first:last], qkv_grad[:, g * wide : (g + 1) * wide])

    a_sums, first = comm.scatter_diagonal(qkv_part, width)
    down_got, down_rest = comm.scatter_two(down_part, width, down_sums, from_y)
    late_mine, late_mate = after((pre_mine, pre_mate), send)
    up_late = lambda g, first, last: tn(two_mine[:, first:last], late_mine) + tn(two_mate[:, first:last], late_mate)
    up_got, up_rest = comm.scatter_two(up_late, width, up_sums, *first)
    down_share = down_rest(down_got, *first)
    norm_one_grad = joined(keep, send)
    input_grad = (middle_grad + norm_back(normed_one, inverse_one, gain_one, norm_one_grad)).astype(BF16)
    grad_gain_one = jnp.sum(norm_one_grad * normed_one, axis=0)
    grad_shift_one = jnp.sum(norm_one_grad, axis=0)

    vector_grad = jnp.stack(
        [grad_gain_one, grad_shift_one, grad_gain_two, grad_shift_two, grad_scale_one, grad_scale_two]
    )
    bits = [1 << k for k in range(comm.n.bit_length() - 1)]
    vector_grad = comm.total(after(vector_grad, *a_sums), (*bits[3:], bits[0]))
    a_sums, sides = comm.scatter_sides(qkv_part, width, a_sums)
    out_sum = out_part(0, 0, width) + after(out_y, *sides)
    if comm.grid:
        out_sum = comm.fold(out_sum, comm.x)
    else:
        out_sum = lax.psum_scatter(out_sum, "dp", scatter_dimension=0, tiled=True)
    if comm.grid:
        a_sums, up_got, out_sum = lax.optimization_barrier((a_sums, up_got, out_sum))
        out_sum = comm.fold(comm.fold(out_sum, lambda v: comm.z(v, 2)), lambda v: comm.z(v, 1))
    up_share = up_rest(up_got)
    vector_grad = comm.total(after(vector_grad, *a_sums), bits[1:3])
    a_share = comm.scatter_z(qkv_part, width, a_sums)
    vector_share = lax.dynamic_slice_in_dim(
        vector_grad, flat_index * vectors.shape[1], vectors.shape[1], axis=1
    )
    matrix = lambda w, g, m, v: adamw_step(w, g, m, v, matrix_rate, matrix_decay)
    qkv_parts = [
        matrix(qkv_weight[:, k], a_share[:, k * local : (k + 1) * local], qkv_first[:, k], qkv_second[:, k])
        for k in range(3)
    ]
    return (
        output,
        input_grad,
        *(jnp.stack(v, axis=1) for v in zip(*qkv_parts)),
        *matrix(out_weight, out_sum, out_first, out_second),
        *matrix(up_weight, up_share, up_first, up_second),
        *matrix(down_weight, down_share, down_first, down_second),
        *adamw_step(vectors, vector_share, vector_first, vector_second, vector_rate, 0.0),
    )


def solution(mesh):
    comm = Comm(mesh.shape["dp"], mesh.shape["mp"])
    rows = P(("dp", "mp"), None)
    cube = P("dp", None, "mp")
    flat = P("dp", "mp")
    vec = P(None, ("dp", "mp"))
    moments = (cube, flat, flat, flat, vec)
    return jax.shard_map(
        lambda *args: shards(comm, *args),
        mesh=mesh,
        in_specs=(rows, rows, P("dp", None), *moments, *moments, *moments),
        out_specs=(rows, rows, *(spec for spec in moments for _ in range(3))),
        check_vma=False,
    )
```

```python
import functools

import jax
import jax.numpy as jnp
from jax import lax
from jax.experimental import pallas as pl
from jax.experimental.pallas import tpu as pltpu
from jax.sharding import PartitionSpec as P

HEAD_DIM = 64
STEP = 10
GLOBAL_LEN = 197
LOCAL_LEN = 37
GLOBAL_PAD = 208
LOCAL_TILE = 128
PER_TILE = 3
SLOTS = 2 * GLOBAL_PAD + 3 * LOCAL_TILE

norm_eps = 1e-06
masked_score = -1e30
beta_first = 0.9
beta_second = 0.999
adam_eps = 1e-08
matrix_rate = 0.1
vector_rate = 1.25
matrix_decay = 0.04

F32 = jnp.float32
BF16 = jnp.bfloat16
AXES = ("dp", "mp")


def dot(a, b, dims):
    return lax.dot_general(a, b, (dims, ((), ())), preferred_element_type=F32)


def nn(a, b):
    return dot(a, b, ((1,), (0,)))


def nt(a, b):
    return dot(a, b, ((1,), (1,)))


def tn(a, b):
    return dot(a, b, ((0,), (0,)))


def adamw_step(weight, gradient, first_old, second_old, step_rate, decay_rate):
    first_new = beta_first * first_old + (1.0 - beta_first) * gradient
    second_new = beta_second * second_old + (1.0 - beta_second) * gradient * gradient
    first_hat = first_new / (1.0 - beta_first**STEP)
    second_hat = second_new / (1.0 - beta_second**STEP)
    weight_new = weight - step_rate * (
        first_hat / (jnp.sqrt(second_hat) + adam_eps) + decay_rate * weight
    )
    return (weight_new, first_new, second_new)


def after(v, *first):
    return lax.optimization_barrier((v, first))[0]


class Comm:
    def __init__(self, n_dp, n_mp):
        self.n_dp, self.n_mp = n_dp, n_mp
        self.n = n_dp * n_mp
        self.grid = n_dp == 8 and n_mp == 4

    def perm(self, f):
        out = []
        for d in range(self.n_dp):
            for m in range(self.n_mp):
                td, tm = f(d, m)
                out.append((d * self.n_mp + m, td * self.n_mp + tm))
        return out

    def core(self, v):
        return lax.ppermute(v, AXES, self.perm(lambda d, m: (d, m ^ 1)))

    def y(self, v):
        return lax.ppermute(v, AXES, self.perm(lambda d, m: (d, m ^ 2)))

    def x(self, v):
        return lax.ppermute(v, AXES, self.perm(lambda d, m: (d ^ 1, m)))

    def z(self, v, k):
        return lax.ppermute(v, AXES, self.perm(lambda d, m: (d ^ (2 * k), m)))

    def total(self, v, bits=None):
        for bit in bits or [1 << k for k in range(self.n.bit_length() - 1)]:
            v = v + lax.ppermute(v, AXES, [(i, i ^ bit) for i in range(self.n)])
        return v

    def order(self):
        d = lax.axis_index("dp")
        if not self.grid:
            return [jnp.int32(r) for r in range(self.n_dp)]
        z, x = d // 2, d % 2
        return [(z ^ dz) * 2 + (x ^ dx) for dx in range(2) for dz in range(4)]

    def places(self):
        d = lax.axis_index("dp")
        if not self.grid:
            return [jnp.int32(r) for r in range(self.n_dp)]
        z, x = d // 2, d % 2
        return [((a // 2) ^ z) + 4 * ((a % 2) ^ x) for a in range(8)]

    def gather_first(self, a, u, d, vector):
        if not self.grid:
            a, u, d = (lax.all_gather(p, "dp", axis=0, tiled=True) for p in (a, u, d))
            return ([a], [self.y(a)]), u, d, self.total(vector)
        rows, cols = u.shape
        cat = lambda *v: jnp.concatenate(v, axis=0)
        ax0, ay0 = self.x(a), self.y(a)
        az = tuple(self.z(a, k) for k in (1, 2, 3))
        vector = self.total(after(vector, ax0, ay0))
        ud = jnp.concatenate([u, d], axis=1)
        ud1 = self.z(after(ud, vector, *az), 1)
        az = cat(*az)
        axs, ays = self.x(az), self.y(az)
        ady, adx = self.y(after(cat(ax0, axs[:rows]), ays, ud1)), self.x(after(ays[rows:], axs, ud1))
        udx0 = self.x(after(ud, adx))
        u1, d1 = ud1[:, :cols], ud1[:, cols:]
        u23 = self.z(after(cat(u, u1), axs, ays), 2)
        return ([a, az, ax0, axs], [ay0, ays, ady, adx]), (u, u1, u23, udx0), (d, d1), vector

    def gather_rest(self, u, d, first):
        if not self.grid:
            return [u], [d]
        cat = lambda *v: jnp.concatenate(v, axis=0)
        (u, u1, u23, udx0), (d, d1) = u, d
        ux0, dx0 = udx0[:, : u.shape[1]], udx0[:, u.shape[1] :]
        uxs = self.x(after(cat(u1, u23), first))
        d23 = self.z(cat(d, d1), 2)
        dxs = self.x(after(cat(d1, d23), uxs))
        return [u, u1, u23, ux0, uxs], [d, d1, d23, dx0, dxs]

    def scatter_diagonal(self, part, rows):
        if not self.grid:
            return (self.y(part(1, 0, rows).astype(BF16)),), ()
        half = rows // 2
        middle = half + rows // 4
        sent = part(1, half, middle).astype(BF16), part(1, middle, rows).astype(BF16)
        return (self.y(sent[0]), self.x(sent[1])), sent

    def scatter_sides(self, part, rows, diagonal):
        if not self.grid:
            return diagonal, ()
        e01, e23 = diagonal
        half, two = rows // 2, rows // 4
        cat = lambda *v: jnp.concatenate(v, axis=0)
        to_x = cat((part(0, half, half + two) + e01).astype(BF16), part(0, half + two, rows).astype(BF16))
        to_y = cat(part(1, 0, two).astype(BF16), (part(1, two, half) + e23).astype(BF16))
        return (self.x(to_x), self.y(to_y)), (to_x, to_y)

    def scatter_x(self, part, rows, *first):
        if not self.grid:
            return (), None
        sent = part(0, rows // 2, rows).astype(BF16)
        return (self.x(after(sent, *first)),), sent

    def scatter_two(self, part, rows, sides, *first):
        if not self.grid:
            mine = sum(sides, part(0, 0, rows))
            return None, lambda *_: lax.psum_scatter(mine, "dp", scatter_dimension=0, tiled=True)
        block = rows // 8
        q = sum(after(sides, *first) if first else sides, part(0, 0, 4 * block))

        def rest(got, *first):
            both = q[: 2 * block] + after(got, *first)
            return both[:block] + self.z(both[block:].astype(BF16), 1)

        return self.z(q[2 * block :].astype(BF16), 2), rest

    def fold(self, v, send):
        half = v.shape[0] // 2
        return v[:half] + send(v[half:].astype(BF16))

    def scatter_z(self, part, rows, sides, *first):
        if not self.grid:
            mine = sum(sides, part(0, 0, rows))
            return lax.psum_scatter(mine, "dp", scatter_dimension=0, tiled=True)
        block = rows // 8
        q = sum(sides, part(0, 0, 4 * block))
        sent = [q[k * block : (k + 1) * block].astype(BF16) for k in (1, 2, 3)]
        return sum((self.z(v, k) for v, k in zip(sent, (1, 2, 3))), q[:block])


def norm_parts(values):
    center = values - jnp.mean(values, axis=-1, keepdims=True)
    spread = jnp.mean(center * center, axis=-1, keepdims=True)
    inverse = lax.rsqrt(spread + norm_eps)
    return center * inverse, inverse


def norm_back(normed, inverse, gain, grad):
    e = gain * grad
    return (
        e - jnp.mean(e, axis=-1, keepdims=True) - normed * jnp.mean(e * normed, axis=-1, keepdims=True)
    ) * inverse


def take_blocks(v, which, block):
    return jnp.concatenate(
        [lax.dynamic_slice_in_dim(v, w * block, block, axis=1) for w in which], axis=1
    )


def pad_rows(v, rows):
    return jnp.pad(v, ((0, rows - v.shape[0]), (0, 0)))


def slots_of(lengths, positions):
    ends = jnp.cumsum(lengths)
    starts = ends - lengths
    is_global = lengths == GLOBAL_LEN
    global_rank = jnp.cumsum(is_global.astype(jnp.int32)) - 1
    local_rank = jnp.cumsum(1 - is_global.astype(jnp.int32)) - 1
    base = jnp.where(
        is_global,
        GLOBAL_PAD * global_rank,
        2 * GLOBAL_PAD + LOCAL_TILE * (local_rank // PER_TILE) + LOCAL_LEN * (local_rank % PER_TILE),
    )
    inside = (positions[:, None] >= starts[None]) & (positions[:, None] < ends[None])
    return jnp.sum(jnp.where(inside, base[None] + positions[:, None] - starts[None], 0), axis=1)


VMEM_LIMIT = 48 * 1024 * 1024


def lanes_of(h, v):
    lane = lax.broadcasted_iota(jnp.int32, v.shape, 1)
    keep = (lane < HEAD_DIM) if h == 0 else (lane >= HEAD_DIM)
    return jnp.where(keep, v, jnp.zeros_like(v))


def two_heads(first, second):
    lane = lax.broadcasted_iota(jnp.int32, first.shape, 1)
    return jnp.where(lane < HEAD_DIM, first, second)


GLOBAL_TILES = [(0, GLOBAL_PAD, 256), (GLOBAL_PAD, GLOBAL_PAD, 256)]
LOCAL_TILES = [(2 * GLOBAL_PAD + LOCAL_TILE * k, LOCAL_TILE, LOCAL_TILE) for k in range(3)]


def tile_mask(queries, keys):
    row = lax.broadcasted_iota(jnp.int32, (queries, keys), 0)
    col = lax.broadcasted_iota(jnp.int32, (queries, keys), 1)
    if keys == 256:
        return col < GLOBAL_LEN
    same = None
    for k in range(4):
        lo, hi = k * LOCAL_LEN, (k + 1) * LOCAL_LEN if k < 3 else LOCAL_TILE
        inside = (row >= lo) & (row < hi) & (col >= lo) & (col < hi)
        same = inside if same is None else same | inside
    return same


def fill_picks(pick, pick_t, slot_row):
    places = lax.broadcasted_iota(jnp.int32, pick.shape, 0)
    row = slot_row[...]
    pick[...] = jnp.where(places == row, 1.0, 0.0).astype(BF16)
    col = jnp.transpose(jnp.broadcast_to(row.astype(F32), (8, row.shape[1])))[:, :1].astype(jnp.int32)
    places = lax.broadcasted_iota(jnp.int32, pick_t.shape, 1)
    pick_t[...] = jnp.where(places == col, 1.0, 0.0).astype(BF16)


def vmem():
    return pl.BlockSpec(memory_space=pltpu.VMEM)


def anywhere():
    return pl.BlockSpec(memory_space=pl.ANY)


def attend_kernel(counts, *refs):
    n = sum(counts)
    rows_own, rows_oth, slot_row = refs[:3]
    pieces = refs[3 : 3 + n]
    weights_out, slots_out, attended, keep, send, probs_g_out, probs_l_out = refs[3 + n : 10 + n]
    pick, pick_t, qkv, att_slots, weights, slots, probs_g, probs_l, sems, out_sems = refs[10 + n :]
    half = rows_own.shape[0]
    wide = qkv.shape[1]
    local = slots.shape[1] // 6
    three = 3 * local
    copies = [[], []]
    at = 0
    for g in range(2):
        row = 0
        for _ in range(counts[g]):
            piece = pieces[at]
            copies[g].append(
                pltpu.make_async_copy(piece, weights.at[g, pl.ds(row, piece.shape[0])], sems.at[at])
            )
            row += piece.shape[0]
            at += 1
    for c in copies[0] + copies[1]:
        c.start()
    fill_picks(pick, pick_t, slot_row)
    outs = []

    def put(src, dst):
        c = pltpu.make_async_copy(src, dst, out_sems.at[len(outs)])
        c.start()
        outs.append(c)

    for g in range(2):
        for c in copies[g]:
            c.wait()
        put(weights.at[g], weights_out.at[g])

        def project(n, _, g=g):
            cols = pl.ds(pl.multiple_of(n * wide, wide), wide)
            w = weights[g, :, cols]
            qkv[:half] = nn(rows_own[...], w).astype(BF16)
            qkv[half:] = nn(rows_oth[...], w).astype(BF16)
            out = pl.ds(pl.multiple_of(g * three + n * wide, wide), wide)
            slots[:, out] = nn(pick[...], qkv[...]).astype(BF16)
            return 0

        lax.fori_loop(0, three // wide, project, 0)
    put(slots, slots_out)
    pairs = local // 128
    for tiles, probs in ((GLOBAL_TILES, probs_g), (LOCAL_TILES, probs_l)):
        mask = tile_mask(*tiles[0][1:])
        for g in range(2):
            for p in range(pairs):
                base = g * three + p * 128
                units = [(t, first, queries, keys, h) for t, (first, queries, keys) in enumerate(tiles) for h in range(2)]
                scores = [
                    nt(
                        lanes_of(h, slots[first : first + queries, base : base + 128]),
                        slots[first : first + keys, base + local : base + local + 128],
                    )
                    for t, first, queries, keys, h in units
                ]
                scores = [jnp.where(mask, s * 0.125, masked_score) for s in scores]
                tops = [jnp.max(s, axis=1, keepdims=True) for s in scores]
                es = [jnp.exp(s - top) for s, top in zip(scores, tops)]
                sums = [1.0 / jnp.sum(e, axis=1, keepdims=True) for e in es]
                lows = []
                for (t, first, queries, keys, h), e, s in zip(units, es, sums):
                    prob = e * s
                    probs[(g * pairs + p) * 2 + h, t] = prob
                    lows.append(prob.astype(BF16))
                mixed = [
                    nn(low, slots[first : first + keys, base + 2 * local : base + 2 * local + 128])
                    for (t, first, queries, keys, h), low in zip(units, lows)
                ]
                for t, (first, queries, keys) in enumerate(tiles):
                    col = g * local + p * 128
                    att_slots[first : first + queries, col : col + 128] = two_heads(
                        mixed[2 * t], mixed[2 * t + 1]
                    ).astype(BF16)
        put(probs, probs_g_out if probs is probs_g else probs_l_out)
    attended[...] = nn(pick_t[...], att_slots[...]).astype(BF16)

    def back(n, _):
        rows = pl.ds(pl.multiple_of(n * 256, 256), 256)
        total = 0.0
        for g in range(2):
            w = weights[g, rows, three:]
            total = total + nt(attended[:, g * local : (g + 1) * local], w).astype(BF16).astype(F32)
        keep[:, rows] = total[:half]
        send[:, rows] = total[half:].astype(BF16)
        return 0

    lax.fori_loop(0, weights.shape[1] // 256, back, 0)
    for c in outs:
        c.wait()


def attend(rows_own, rows_oth, slot_row, own, oth):
    half, width = rows_own.shape
    cols = own[0].shape[1]
    local = cols // 4
    pieces = [*own, *oth]
    heads = 2 * local // HEAD_DIM
    shape = jax.ShapeDtypeStruct
    probs = ((heads, 2, GLOBAL_PAD, 256), (heads, 3, LOCAL_TILE, LOCAL_TILE))
    return pl.pallas_call(
        functools.partial(attend_kernel, (len(own), len(oth))),
        out_shape=(
            shape((2, width, cols), BF16),
            shape((SLOTS, 6 * local), BF16),
            shape((2 * half, 2 * local), BF16),
            shape((half, width), F32),
            shape((half, width), BF16),
            shape(probs[0], F32),
            shape(probs[1], F32),
        ),
        in_specs=[vmem()] * 3 + [anywhere()] * len(pieces),
        out_specs=(anywhere(), anywhere(), vmem(), vmem(), vmem(), anywhere(), anywhere()),
        scratch_shapes=[
            pltpu.VMEM((SLOTS, 2 * half), BF16),
            pltpu.VMEM((2 * half, SLOTS), BF16),
            pltpu.VMEM((2 * half, local), BF16),
            pltpu.VMEM((SLOTS, 2 * local), BF16),
            pltpu.VMEM((2, width, cols), BF16),
            pltpu.VMEM((SLOTS, 6 * local), BF16),
            pltpu.VMEM(probs[0], F32),
            pltpu.VMEM(probs[1], F32),
            pltpu.SemaphoreType.DMA((len(pieces),)),
            pltpu.SemaphoreType.DMA((5,)),
        ],
        compiler_params=pltpu.CompilerParams(vmem_limit_bytes=VMEM_LIMIT),
        cost_estimate=pl.CostEstimate(flops=1000, bytes_accessed=1000, transcendentals=0),
        name="attend",
    )(rows_own, rows_oth, slot_row, *pieces)


def attend_back_kernel(
    rows_own, rows_oth, slot_row, weights_in, slots_in, probs_g_in, probs_l_in, qkv_grad_out, keep, send,
    pick, pick_t, att, grads, slot_grads, weights, slots, probs_g, probs_l, qkv_grad, sems, out_sems,
):
    half = rows_own.shape[0]
    local = slots.shape[1] // 6
    three = 3 * local
    gets = [
        pltpu.make_async_copy(src, dst, sems.at[i])
        for i, (src, dst) in enumerate(
            (
                (weights_in.at[:, :, pl.ds(three, local)], weights.at[:, :, pl.ds(three, local)]),
                (slots_in, slots),
                (probs_g_in, probs_g),
                (probs_l_in, probs_l),
                (weights_in.at[:, :, pl.ds(0, three)], weights.at[:, :, pl.ds(0, three)]),
            )
        )
    ]
    for c in gets:
        c.start()
    fill_picks(pick, pick_t, slot_row)
    gets[0].wait()
    for g in range(2):
        w = weights[g, :, three:]
        att[:half, g * local : (g + 1) * local] = nn(rows_own[...], w).astype(BF16)
        att[half:, g * local : (g + 1) * local] = nn(rows_oth[...], w).astype(BF16)
    grads[...] = nn(pick[...], att[...]).astype(BF16)
    gets[1].wait()
    pairs = local // 128
    for tiles, probs, get in ((GLOBAL_TILES, probs_g, gets[2]), (LOCAL_TILES, probs_l, gets[3])):
        get.wait()
        for g in range(2):
            for p in range(pairs):
                base = g * three + p * 128
                col = g * local + p * 128
                units = [(t, first, queries, keys, h) for t, (first, queries, keys) in enumerate(tiles) for h in range(2)]

                def part(j, first, size):
                    return slots[first : first + size, base + j * local : base + j * local + 128]

                outs = [grads[first : first + queries, col : col + 128] for t, first, queries, keys, h in units]
                prob = [probs[(g * pairs + p) * 2 + h, t] for t, first, queries, keys, h in units]
                dps = [
                    nt(lanes_of(h, d), part(2, first, keys)) for (t, first, queries, keys, h), d in zip(units, outs)
                ]
                dvs = [tn(pr.astype(BF16), d) for pr, d in zip(prob, outs)]
                dots = [jnp.sum(dp * pr, axis=1, keepdims=True) for dp, pr in zip(dps, prob)]
                dss = [(pr * (dp - dot_)).astype(BF16) for pr, dp, dot_ in zip(prob, dps, dots)]
                dqs = [nn(ds, part(1, first, keys)) for (t, first, queries, keys, h), ds in zip(units, dss)]
                dks = [tn(ds, part(0, first, queries)) for (t, first, queries, keys, h), ds in zip(units, dss)]
                for t, (first, queries, keys) in enumerate(tiles):
                    for j, (two, factor) in enumerate(((dqs, 0.125), (dks, 0.125), (dvs, 1.0))):
                        both = two_heads(two[2 * t], two[2 * t + 1])
                        if factor != 1.0:
                            both = both * factor
                        slot_grads[first : first + queries, base + j * local : base + j * local + 128] = both[
                            :queries
                        ].astype(BF16)

    def unsort(n, _):
        cols = pl.ds(pl.multiple_of(n * local, local), local)
        qkv_grad[:, cols] = nn(pick_t[...], slot_grads[:, cols]).astype(BF16)
        return 0

    lax.fori_loop(0, 6, unsort, 0)
    put = pltpu.make_async_copy(qkv_grad, qkv_grad_out, out_sems.at[0])
    put.start()
    gets[4].wait()

    def back(n, _):
        rows = pl.ds(pl.multiple_of(n * 256, 256), 256)
        total = nt(qkv_grad[:, :three], weights[0, rows, :three]) + nt(qkv_grad[:, three:], weights[1, rows, :three])
        keep[:, rows] = total[:half]
        send[:, rows] = total[half:].astype(BF16)
        return 0

    lax.fori_loop(0, weights.shape[1] // 256, back, 0)
    put.wait()


def attend_back(rows_own, rows_oth, slot_row, weights, slots, probs_g, probs_l):
    half, width = rows_own.shape
    local = slots.shape[1] // 6
    shape = jax.ShapeDtypeStruct
    return pl.pallas_call(
        attend_back_kernel,
        out_shape=(
            shape((2 * half, 6 * local), BF16),
            shape((half, width), F32),
            shape((half, width), BF16),
        ),
        in_specs=[vmem()] * 3 + [anywhere()] * 4,
        out_specs=(anywhere(), vmem(), vmem()),
        scratch_shapes=[
            pltpu.VMEM((SLOTS, 2 * half), BF16),
            pltpu.VMEM((2 * half, SLOTS), BF16),
            pltpu.VMEM((2 * half, 2 * local), BF16),
            pltpu.VMEM((SLOTS, 2 * local), BF16),
            pltpu.VMEM((SLOTS, 6 * local), BF16),
            pltpu.VMEM(weights.shape, BF16),
            pltpu.VMEM(slots.shape, BF16),
            pltpu.VMEM(probs_g.shape, F32),
            pltpu.VMEM(probs_l.shape, F32),
            pltpu.VMEM((2 * half, 6 * local), BF16),
            pltpu.SemaphoreType.DMA((5,)),
            pltpu.SemaphoreType.DMA((1,)),
        ],
        compiler_params=pltpu.CompilerParams(vmem_limit_bytes=VMEM_LIMIT),
        cost_estimate=pl.CostEstimate(flops=1000, bytes_accessed=1000, transcendentals=0),
        name="attend_back",
    )(rows_own, rows_oth, slot_row, weights, slots, probs_g, probs_l)


def shards(comm, tokens, cotangent, crop_lengths, qkv_weight, out_weight, up_weight, down_weight, vectors,
           qkv_first, out_first, up_first, down_first, vector_first,
           qkv_second, out_second, up_second, down_second, vector_second):
    rows, width = tokens.shape
    padded = -(-rows // 16) * 16
    block = width // comm.n_dp
    own_index = lax.axis_index("mp")
    image, core = own_index // 2, own_index % 2
    flat_index = lax.axis_index("dp") * comm.n_mp + own_index
    local = qkv_weight.shape[2]
    hidden = up_weight.shape[1]
    order, places = comm.order(), comm.places()
    to_rel = lambda v: take_blocks(v, order, block)
    to_abs = lambda v: take_blocks(v, places, block)

    pack_a = jnp.concatenate([qkv_weight.reshape(-1, 3 * local), out_weight], axis=1).astype(BF16)
    vector_full = lax.dynamic_update_slice(
        jnp.zeros((6, width), F32), vectors.astype(BF16).astype(F32), (0, flat_index * vectors.shape[1])
    ).astype(BF16)
    (a_own, a_oth), up_part, down_part, vector_full = comm.gather_first(
        pack_a, up_weight.astype(BF16), down_weight.astype(BF16), vector_full
    )
    gain_one, shift_one, gain_two, shift_two, scale_one, scale_two = vector_full.astype(F32)
    cat = lambda blocks: jnp.concatenate(blocks, axis=0)
    lengths = lax.dynamic_index_in_dim(crop_lengths, image, 0, keepdims=False)
    lane = jnp.arange(padded, dtype=jnp.int32)
    positions = jnp.concatenate(
        [jnp.where(lane < rows, lane + half * rows, -1) for half in (core, 1 - core)]
    )
    slot = jnp.where(positions >= 0, slots_of(lengths, positions), -1)
    slot_row = slot[None, :]

    residual = tokens.astype(F32)
    normed_one, inverse_one = norm_parts(residual)
    norm_one = pad_rows(to_rel((normed_one * gain_one + shift_one).astype(BF16)), padded)
    norm_one_other = comm.core(norm_one)
    rows_one = cat([norm_one, norm_one_other])
    out_grad = cotangent.astype(F32)
    cot_y = comm.y(after(cotangent, *a_oth[-2:]))
    wide = 3 * local
    weights_a, slots, attended, keep, send, probs_g, probs_l = attend(
        norm_one, norm_one_other, slot_row, a_own, a_oth
    )

    def joined(keep, send):
        return to_abs(keep[:rows] + comm.core(send)[:rows].astype(F32))

    def spread(mine, mate, *first):
        total = mine + comm.core(mate.astype(BF16))
        sent = total[padded:].astype(BF16)
        return total[:padded], sent, comm.y(after(sent, *first))

    if comm.grid:
        send = after(send, *up_part[2:])
    up_blocks, down_blocks = comm.gather_rest(up_part, down_part, send)
    up_full = cat(up_blocks)
    branch_one = joined(keep, send)
    middle = residual + scale_one * branch_one
    normed_two, inverse_two = norm_parts(middle)
    norm_two = pad_rows(to_rel((normed_two * gain_two + shift_two).astype(BF16)), padded)
    norm_two_y = comm.y(norm_two)
    cot_mine = cat([pad_rows(cotangent, padded), pad_rows(cot_y, padded)])
    cot_mine = after(cot_mine, norm_two)
    mlp_mine, mlp_mate = (
        to_rel((v.astype(F32) * scale_two).astype(BF16)) for v in (cot_mine, comm.core(cot_mine))
    )

    two_mine = cat([norm_two, norm_two_y])
    two_mate = comm.core(two_mine)
    if comm.grid:
        two_mate = after(two_mate, up_blocks[4])

    def activate(hidden_pre):
        cdf = 0.5 * (1.0 + lax.erf(hidden_pre * (0.5**0.5)))
        slope = cdf + hidden_pre * jnp.exp(-0.5 * hidden_pre * hidden_pre) * 0.3989422804014327
        return (hidden_pre * cdf).astype(BF16), slope

    act_mine, slope_mine = activate(nn(two_mine, up_full))
    act_mate, slope_mate = activate(nn(two_mate, up_full))
    down_part = lambda g, first, last: tn(mlp_mine[:, first:last], act_mine) + tn(mlp_mate[:, first:last], act_mate)
    if comm.grid:
        down_last, act_mine, act_mate, slope_mine, slope_mate = lax.optimization_barrier(
            (down_blocks[-1], act_mine, act_mate, slope_mine, slope_mate)
        )
        down_blocks = [*down_blocks[:-1], down_last]
    down_full = cat(down_blocks)
    pre_mate = (nn(mlp_mate, down_full) * slope_mate).astype(BF16)
    pre_mine = (nn(mlp_mine, down_full) * slope_mine).astype(BF16)
    down_sums, sent = comm.scatter_x(down_part, width, pre_mine, pre_mate)
    mine, sent_y, from_y = spread(nt(pre_mine, up_full), nt(pre_mate, up_full))
    norm_two_grad = to_abs((mine + from_y)[:rows])
    pre_mine, pre_mate = after((pre_mine, pre_mate), sent_y)
    up_part = lambda g, first, last: tn(two_mine[:, first:last], pre_mine) + tn(two_mate[:, first:last], pre_mate)
    up_sums, sent = comm.scatter_x(up_part, width)
    middle_grad = out_grad + norm_back(normed_two, inverse_two, gain_two, norm_two_grad)
    grad_gain_two = jnp.sum(norm_two_grad * normed_two, axis=0)
    grad_shift_two = jnp.sum(norm_two_grad, axis=0)
    grad_scale_one = jnp.sum(middle_grad * branch_one, axis=0)
    attn_own = pad_rows(to_rel((middle_grad * scale_one).astype(BF16)), padded)
    attn_other = comm.core(attn_own)
    attn_rows = cat([attn_own, attn_other])
    branch_own, branch_mate = after((act_mine, act_mate), sent_y)
    branch_mine, _, branch_y = spread(
        nt(branch_own, down_full).astype(BF16).astype(F32), nt(branch_mate, down_full), from_y
    )

    def out_part(g, first, last):
        return tn(attn_rows[:, first:last], attended[:, g * local : (g + 1) * local])

    out_y = comm.y(out_part(1, 0, width).astype(BF16))

    qkv_grad, keep, send = attend_back(
        attn_own, attn_other, slot_row, weights_a, slots, probs_g, probs_l
    )
    branch_two = to_abs((branch_mine + after(branch_y, send))[:rows])
    output = (middle + scale_two * branch_two).astype(BF16)
    grad_scale_two = jnp.sum(out_grad * branch_two, axis=0)

    def qkv_part(g, first, last):
        return tn(rows_one[:, first:last], qkv_grad[:, g * wide : (g + 1) * wide])

    a_sums, first = comm.scatter_diagonal(qkv_part, width)
    down_got, down_rest = comm.scatter_two(down_part, width, down_sums, from_y)
    late_mine, late_mate = after((pre_mine, pre_mate), send)
    up_late = lambda g, first, last: tn(two_mine[:, first:last], late_mine) + tn(two_mate[:, first:last], late_mate)
    up_got, up_rest = comm.scatter_two(up_late, width, up_sums, *first)
    down_share = down_rest(down_got, *first)
    norm_one_grad = joined(keep, send)
    input_grad = (middle_grad + norm_back(normed_one, inverse_one, gain_one, norm_one_grad)).astype(BF16)
    grad_gain_one = jnp.sum(norm_one_grad * normed_one, axis=0)
    grad_shift_one = jnp.sum(norm_one_grad, axis=0)

    vector_grad = jnp.stack(
        [grad_gain_one, grad_shift_one, grad_gain_two, grad_shift_two, grad_scale_one, grad_scale_two]
    )
    bits = [1 << k for k in range(comm.n.bit_length() - 1)]
    vector_grad = comm.total(after(vector_grad, *a_sums), (*bits[3:], bits[0]))
    a_sums, sides = comm.scatter_sides(qkv_part, width, a_sums)
    out_sum = out_part(0, 0, width) + after(out_y, *sides)
    if comm.grid:
        out_sum = comm.fold(out_sum, comm.x)
    else:
        out_sum = lax.psum_scatter(out_sum, "dp", scatter_dimension=0, tiled=True)
    if comm.grid:
        a_sums, up_got, out_sum = lax.optimization_barrier((a_sums, up_got, out_sum))
        out_sum = comm.fold(comm.fold(out_sum, lambda v: comm.z(v, 2)), lambda v: comm.z(v, 1))
    up_share = up_rest(up_got)
    vector_grad = comm.total(after(vector_grad, *a_sums), bits[1:3])
    a_share = comm.scatter_z(qkv_part, width, a_sums)
    vector_share = lax.dynamic_slice_in_dim(
        vector_grad, flat_index * vectors.shape[1], vectors.shape[1], axis=1
    )
    matrix = lambda w, g, m, v: adamw_step(w, g, m, v, matrix_rate, matrix_decay)
    flip = lambda v: jnp.transpose(v, (1, 0, 2))
    up_results = matrix(up_weight, up_share, up_first, up_second)
    if comm.grid:
        a_share, up_results = lax.optimization_barrier((a_share, up_results))
    planes = jnp.stack([a_share[:, k * local : (k + 1) * local] for k in range(3)])
    qkv_results = matrix(flip(qkv_weight), planes, flip(qkv_first), flip(qkv_second))
    return (
        output,
        input_grad,
        *(flip(v) for v in qkv_results),
        *matrix(out_weight, out_sum, out_first, out_second),
        *up_results,
        *matrix(down_weight, down_share, down_first, down_second),
        *adamw_step(vectors, vector_share, vector_first, vector_second, vector_rate, 0.0),
    )


def solution(mesh):
    comm = Comm(mesh.shape["dp"], mesh.shape["mp"])
    rows = P(("dp", "mp"), None)
    cube = P("dp", None, "mp")
    flat = P("dp", "mp")
    vec = P(None, ("dp", "mp"))
    moments = (cube, flat, flat, flat, vec)
    return jax.shard_map(
        lambda *args: shards(comm, *args),
        mesh=mesh,
        in_specs=(rows, rows, P("dp", None), *moments, *moments, *moments),
        out_specs=(rows, rows, *(spec for spec in moments for _ in range(3))),
        check_vma=False,
    )
```

```python
import functools

import jax
import jax.numpy as jnp
from jax import lax
from jax.experimental import pallas as pl
from jax.experimental.pallas import tpu as pltpu
from jax.sharding import PartitionSpec as P

HEAD_DIM = 64
STEP = 10
GLOBAL_LEN = 197
LOCAL_LEN = 37
GLOBAL_PAD = 208
LOCAL_TILE = 128
PER_TILE = 3
SLOTS = 2 * GLOBAL_PAD + 3 * LOCAL_TILE

norm_eps = 1e-06
masked_score = -1e30
beta_first = 0.9
beta_second = 0.999
adam_eps = 1e-08
matrix_rate = 0.1
vector_rate = 1.25
matrix_decay = 0.04

F32 = jnp.float32
BF16 = jnp.bfloat16
AXES = ("dp", "mp")


def dot(a, b, dims):
    return lax.dot_general(a, b, (dims, ((), ())), preferred_element_type=F32)


def nn(a, b):
    return dot(a, b, ((1,), (0,)))


def nt(a, b):
    return dot(a, b, ((1,), (1,)))


def tn(a, b):
    return dot(a, b, ((0,), (0,)))


def adamw_step(weight, gradient, first_old, second_old, step_rate, decay_rate):
    first_new = beta_first * first_old + (1.0 - beta_first) * gradient
    second_new = beta_second * second_old + (1.0 - beta_second) * gradient * gradient
    first_hat = first_new / (1.0 - beta_first**STEP)
    second_hat = second_new / (1.0 - beta_second**STEP)
    weight_new = weight - step_rate * (
        first_hat / (jnp.sqrt(second_hat) + adam_eps) + decay_rate * weight
    )
    return (weight_new, first_new, second_new)


def after(v, *first):
    return lax.optimization_barrier((v, first))[0]


class Comm:
    def __init__(self, n_dp, n_mp):
        self.n_dp, self.n_mp = n_dp, n_mp
        self.n = n_dp * n_mp
        self.grid = n_dp == 8 and n_mp == 4

    def perm(self, f):
        out = []
        for d in range(self.n_dp):
            for m in range(self.n_mp):
                td, tm = f(d, m)
                out.append((d * self.n_mp + m, td * self.n_mp + tm))
        return out

    def core(self, v):
        return lax.ppermute(v, AXES, self.perm(lambda d, m: (d, m ^ 1)))

    def y(self, v):
        return lax.ppermute(v, AXES, self.perm(lambda d, m: (d, m ^ 2)))

    def x(self, v):
        return lax.ppermute(v, AXES, self.perm(lambda d, m: (d ^ 1, m)))

    def z(self, v, k):
        return lax.ppermute(v, AXES, self.perm(lambda d, m: (d ^ (2 * k), m)))

    def total(self, v, bits=None):
        for bit in bits or [1 << k for k in range(self.n.bit_length() - 1)]:
            v = v + lax.ppermute(v, AXES, [(i, i ^ bit) for i in range(self.n)])
        return v

    def order(self):
        d = lax.axis_index("dp")
        if not self.grid:
            return [jnp.int32(r) for r in range(self.n_dp)]
        z, x = d // 2, d % 2
        return [(z ^ dz) * 2 + (x ^ dx) for dx in range(2) for dz in range(4)]

    def places(self):
        d = lax.axis_index("dp")
        if not self.grid:
            return [jnp.int32(r) for r in range(self.n_dp)]
        z, x = d // 2, d % 2
        return [((a // 2) ^ z) + 4 * ((a % 2) ^ x) for a in range(8)]

    def gather_first(self, a, u, d, vector):
        if not self.grid:
            a, u, d = (lax.all_gather(p, "dp", axis=0, tiled=True) for p in (a, u, d))
            return ([a], [self.y(a)]), u, d, self.total(vector)
        rows, cols = u.shape
        cat = lambda *v: jnp.concatenate(v, axis=0)
        ax0, ay0 = self.x(a), self.y(a)
        az = tuple(self.z(a, k) for k in (1, 2, 3))
        vector = self.total(after(vector, ax0, ay0))
        ud = jnp.concatenate([u, d], axis=1)
        ud1 = self.z(after(ud, vector, *az), 1)
        az = cat(*az)
        axs, ays = self.x(az), self.y(az)
        ady, adx = self.y(after(cat(ax0, axs[:rows]), ays, ud1)), self.x(after(ays[rows:], axs, ud1))
        udx0 = self.x(after(ud, adx))
        u1, d1 = ud1[:, :cols], ud1[:, cols:]
        u23 = self.z(after(cat(u, u1), axs, ays), 2)
        return ([a, az, ax0, axs], [ay0, ays, ady, adx]), (u, u1, u23, udx0), (d, d1), vector

    def gather_rest(self, u, d, first):
        if not self.grid:
            return [u], [d]
        cat = lambda *v: jnp.concatenate(v, axis=0)
        (u, u1, u23, udx0), (d, d1) = u, d
        ux0, dx0 = udx0[:, : u.shape[1]], udx0[:, u.shape[1] :]
        uxs = self.x(after(cat(u1, u23), first))
        d23 = self.z(cat(d, d1), 2)
        dxs = self.x(after(cat(d1, d23), uxs))
        return [u, u1, u23, ux0, uxs], [d, d1, d23, dx0, dxs]

    def scatter_diagonal(self, part, rows):
        if not self.grid:
            return (self.y(part(1, 0, rows).astype(BF16)),), ()
        half = rows // 2
        middle = half + rows // 4
        sent = part(1, half, middle).astype(BF16), part(1, middle, rows).astype(BF16)
        return (self.y(sent[0]), self.x(sent[1])), sent

    def scatter_sides(self, part, rows, diagonal):
        if not self.grid:
            return diagonal, ()
        e01, e23 = diagonal
        half, two = rows // 2, rows // 4
        cat = lambda *v: jnp.concatenate(v, axis=0)
        to_x = cat((part(0, half, half + two) + e01).astype(BF16), part(0, half + two, rows).astype(BF16))
        to_y = cat(part(1, 0, two).astype(BF16), (part(1, two, half) + e23).astype(BF16))
        return (self.x(to_x), self.y(to_y)), (to_x, to_y)

    def scatter_x(self, part, rows, *first):
        if not self.grid:
            return (), None
        sent = part(0, rows // 2, rows).astype(BF16)
        return (self.x(after(sent, *first)),), sent

    def scatter_two(self, part, rows, sides, *first):
        if not self.grid:
            mine = sum(sides, part(0, 0, rows))
            return None, lambda *_: lax.psum_scatter(mine, "dp", scatter_dimension=0, tiled=True)
        block = rows // 8
        q = sum(after(sides, *first) if first else sides, part(0, 0, 4 * block))

        def rest(got, *first):
            both = q[: 2 * block] + after(got, *first)
            return both[:block] + self.z(both[block:].astype(BF16), 1)

        return self.z(q[2 * block :].astype(BF16), 2), rest

    def fold(self, v, send):
        half = v.shape[0] // 2
        return v[:half] + send(v[half:].astype(BF16))

    def scatter_z(self, part, rows, sides, *first):
        if not self.grid:
            mine = sum(sides, part(0, 0, rows))
            return lax.psum_scatter(mine, "dp", scatter_dimension=0, tiled=True)
        block = rows // 8
        q = sum(sides, part(0, 0, 4 * block))
        sent = [q[k * block : (k + 1) * block].astype(BF16) for k in (1, 2, 3)]
        return sum((self.z(v, k) for v, k in zip(sent, (1, 2, 3))), q[:block])


def norm_parts(values):
    center = values - jnp.mean(values, axis=-1, keepdims=True)
    spread = jnp.mean(center * center, axis=-1, keepdims=True)
    inverse = lax.rsqrt(spread + norm_eps)
    return center * inverse, inverse


def norm_back(normed, inverse, gain, grad):
    e = gain * grad
    return (
        e - jnp.mean(e, axis=-1, keepdims=True) - normed * jnp.mean(e * normed, axis=-1, keepdims=True)
    ) * inverse


def take_blocks(v, which, block):
    return jnp.concatenate(
        [lax.dynamic_slice_in_dim(v, w * block, block, axis=1) for w in which], axis=1
    )


def pad_rows(v, rows):
    return jnp.pad(v, ((0, rows - v.shape[0]), (0, 0)))


def slots_of(lengths, positions):
    ends = jnp.cumsum(lengths)
    starts = ends - lengths
    is_global = lengths == GLOBAL_LEN
    global_rank = jnp.cumsum(is_global.astype(jnp.int32)) - 1
    local_rank = jnp.cumsum(1 - is_global.astype(jnp.int32)) - 1
    base = jnp.where(
        is_global,
        GLOBAL_PAD * global_rank,
        2 * GLOBAL_PAD + LOCAL_TILE * (local_rank // PER_TILE) + LOCAL_LEN * (local_rank % PER_TILE),
    )
    inside = (positions[:, None] >= starts[None]) & (positions[:, None] < ends[None])
    return jnp.sum(jnp.where(inside, base[None] + positions[:, None] - starts[None], 0), axis=1)


VMEM_LIMIT = 48 * 1024 * 1024


def lanes_of(h, v):
    lane = lax.broadcasted_iota(jnp.int32, v.shape, 1)
    keep = (lane < HEAD_DIM) if h == 0 else (lane >= HEAD_DIM)
    return jnp.where(keep, v, jnp.zeros_like(v))


def two_heads(first, second):
    lane = lax.broadcasted_iota(jnp.int32, first.shape, 1)
    return jnp.where(lane < HEAD_DIM, first, second)


GLOBAL_TILES = [(0, GLOBAL_PAD, 256), (GLOBAL_PAD, GLOBAL_PAD, 256)]
LOCAL_TILES = [(2 * GLOBAL_PAD + LOCAL_TILE * k, LOCAL_TILE, LOCAL_TILE) for k in range(3)]


def tile_mask(queries, keys):
    row = lax.broadcasted_iota(jnp.int32, (queries, keys), 0)
    col = lax.broadcasted_iota(jnp.int32, (queries, keys), 1)
    if keys == 256:
        return col < GLOBAL_LEN
    same = None
    for k in range(4):
        lo, hi = k * LOCAL_LEN, (k + 1) * LOCAL_LEN if k < 3 else LOCAL_TILE
        inside = (row >= lo) & (row < hi) & (col >= lo) & (col < hi)
        same = inside if same is None else same | inside
    return same


def fill_picks(pick, pick_t, slot_row):
    places = lax.broadcasted_iota(jnp.int32, pick.shape, 0)
    row = slot_row[...]
    pick[...] = jnp.where(places == row, 1.0, 0.0).astype(BF16)
    col = jnp.transpose(jnp.broadcast_to(row.astype(F32), (8, row.shape[1])))[:, :1].astype(jnp.int32)
    places = lax.broadcasted_iota(jnp.int32, pick_t.shape, 1)
    pick_t[...] = jnp.where(places == col, 1.0, 0.0).astype(BF16)


def vmem():
    return pl.BlockSpec(memory_space=pltpu.VMEM)


def anywhere():
    return pl.BlockSpec(memory_space=pl.ANY)


def attend_kernel(counts, *refs):
    n = sum(counts)
    rows_own, rows_oth, slot_row = refs[:3]
    pieces = refs[3 : 3 + n]
    weights_out, slots_out, attended, keep, send, probs_g_out, probs_l_out = refs[3 + n : 10 + n]
    pick, pick_t, qkv, att_slots, weights, slots, probs_g, probs_l, sems, out_sems = refs[10 + n :]
    half = rows_own.shape[0]
    wide = qkv.shape[1]
    local = slots.shape[1] // 6
    three = 3 * local
    copies = [[], []]
    at = 0
    for g in range(2):
        row = 0
        for _ in range(counts[g]):
            piece = pieces[at]
            copies[g].append(
                pltpu.make_async_copy(piece, weights.at[g, pl.ds(row, piece.shape[0])], sems.at[at])
            )
            row += piece.shape[0]
            at += 1
    for c in copies[0] + copies[1]:
        c.start()
    fill_picks(pick, pick_t, slot_row)
    outs = []

    def put(src, dst):
        c = pltpu.make_async_copy(src, dst, out_sems.at[len(outs)])
        c.start()
        outs.append(c)

    for g in range(2):
        for c in copies[g]:
            c.wait()
        put(weights.at[g], weights_out.at[g])

        def project(n, _, g=g):
            cols = pl.ds(pl.multiple_of(n * wide, wide), wide)
            w = weights[g, :, cols]
            qkv[:half] = nn(rows_own[...], w).astype(BF16)
            qkv[half:] = nn(rows_oth[...], w).astype(BF16)
            out = pl.ds(pl.multiple_of(g * three + n * wide, wide), wide)
            slots[:, out] = nn(pick[...], qkv[...]).astype(BF16)
            return 0

        lax.fori_loop(0, three // wide, project, 0)
    put(slots, slots_out)
    pairs = local // 128
    for tiles, probs in ((GLOBAL_TILES, probs_g), (LOCAL_TILES, probs_l)):
        mask = tile_mask(*tiles[0][1:])
        for g in range(2):
            for p in range(pairs):
                base = g * three + p * 128
                units = [(t, first, queries, keys, h) for t, (first, queries, keys) in enumerate(tiles) for h in range(2)]
                scores = [
                    nt(
                        lanes_of(h, slots[first : first + queries, base : base + 128]),
                        slots[first : first + keys, base + local : base + local + 128],
                    )
                    for t, first, queries, keys, h in units
                ]
                scores = [jnp.where(mask, s * 0.125, masked_score) for s in scores]
                tops = [jnp.max(s, axis=1, keepdims=True) for s in scores]
                es = [jnp.exp(s - top) for s, top in zip(scores, tops)]
                sums = [1.0 / jnp.sum(e, axis=1, keepdims=True) for e in es]
                lows = []
                for (t, first, queries, keys, h), e, s in zip(units, es, sums):
                    prob = e * s
                    probs[(g * pairs + p) * 2 + h, t] = prob
                    lows.append(prob.astype(BF16))
                mixed = [
                    nn(low, slots[first : first + keys, base + 2 * local : base + 2 * local + 128])
                    for (t, first, queries, keys, h), low in zip(units, lows)
                ]
                for t, (first, queries, keys) in enumerate(tiles):
                    col = g * local + p * 128
                    att_slots[first : first + queries, col : col + 128] = two_heads(
                        mixed[2 * t], mixed[2 * t + 1]
                    ).astype(BF16)
        put(probs, probs_g_out if probs is probs_g else probs_l_out)
    attended[...] = nn(pick_t[...], att_slots[...]).astype(BF16)

    def back(n, _):
        rows = pl.ds(pl.multiple_of(n * 256, 256), 256)
        total = 0.0
        for g in range(2):
            w = weights[g, rows, three:]
            total = total + nt(attended[:, g * local : (g + 1) * local], w).astype(BF16).astype(F32)
        keep[:, rows] = total[:half]
        send[:, rows] = total[half:].astype(BF16)
        return 0

    lax.fori_loop(0, weights.shape[1] // 256, back, 0)
    for c in outs:
        c.wait()


def attend(rows_own, rows_oth, slot_row, own, oth):
    half, width = rows_own.shape
    cols = own[0].shape[1]
    local = cols // 4
    pieces = [*own, *oth]
    heads = 2 * local // HEAD_DIM
    shape = jax.ShapeDtypeStruct
    probs = ((heads, 2, GLOBAL_PAD, 256), (heads, 3, LOCAL_TILE, LOCAL_TILE))
    return pl.pallas_call(
        functools.partial(attend_kernel, (len(own), len(oth))),
        out_shape=(
            shape((2, width, cols), BF16),
            shape((SLOTS, 6 * local), BF16),
            shape((2 * half, 2 * local), BF16),
            shape((half, width), F32),
            shape((half, width), BF16),
            shape(probs[0], F32),
            shape(probs[1], F32),
        ),
        in_specs=[vmem()] * 3 + [anywhere()] * len(pieces),
        out_specs=(anywhere(), anywhere(), vmem(), vmem(), vmem(), anywhere(), anywhere()),
        scratch_shapes=[
            pltpu.VMEM((SLOTS, 2 * half), BF16),
            pltpu.VMEM((2 * half, SLOTS), BF16),
            pltpu.VMEM((2 * half, local), BF16),
            pltpu.VMEM((SLOTS, 2 * local), BF16),
            pltpu.VMEM((2, width, cols), BF16),
            pltpu.VMEM((SLOTS, 6 * local), BF16),
            pltpu.VMEM(probs[0], F32),
            pltpu.VMEM(probs[1], F32),
            pltpu.SemaphoreType.DMA((len(pieces),)),
            pltpu.SemaphoreType.DMA((5,)),
        ],
        compiler_params=pltpu.CompilerParams(vmem_limit_bytes=VMEM_LIMIT),
        cost_estimate=pl.CostEstimate(flops=1000, bytes_accessed=1000, transcendentals=0),
        name="attend",
    )(rows_own, rows_oth, slot_row, *pieces)


def attend_back_kernel(
    rows_own, rows_oth, slot_row, weights_in, slots_in, probs_g_in, probs_l_in, qkv_grad_out, keep, send,
    pick, pick_t, att, grads, slot_grads, weights, slots, probs_g, probs_l, qkv_grad, sems, out_sems,
):
    half = rows_own.shape[0]
    local = slots.shape[1] // 6
    three = 3 * local
    gets = [
        pltpu.make_async_copy(src, dst, sems.at[i])
        for i, (src, dst) in enumerate(
            (
                (weights_in.at[:, :, pl.ds(three, local)], weights.at[:, :, pl.ds(three, local)]),
                (slots_in, slots),
                (probs_g_in, probs_g),
                (probs_l_in, probs_l),
                (weights_in.at[:, :, pl.ds(0, three)], weights.at[:, :, pl.ds(0, three)]),
            )
        )
    ]
    for c in gets:
        c.start()
    fill_picks(pick, pick_t, slot_row)
    gets[0].wait()
    for g in range(2):
        w = weights[g, :, three:]
        att[:half, g * local : (g + 1) * local] = nn(rows_own[...], w).astype(BF16)
        att[half:, g * local : (g + 1) * local] = nn(rows_oth[...], w).astype(BF16)
    grads[...] = nn(pick[...], att[...]).astype(BF16)
    gets[1].wait()
    pairs = local // 128
    for tiles, probs, get in ((GLOBAL_TILES, probs_g, gets[2]), (LOCAL_TILES, probs_l, gets[3])):
        get.wait()
        for g in range(2):
            for p in range(pairs):
                base = g * three + p * 128
                col = g * local + p * 128
                units = [(t, first, queries, keys, h) for t, (first, queries, keys) in enumerate(tiles) for h in range(2)]

                def part(j, first, size):
                    return slots[first : first + size, base + j * local : base + j * local + 128]

                outs = [grads[first : first + queries, col : col + 128] for t, first, queries, keys, h in units]
                prob = [probs[(g * pairs + p) * 2 + h, t] for t, first, queries, keys, h in units]
                dps = [
                    nt(lanes_of(h, d), part(2, first, keys)) for (t, first, queries, keys, h), d in zip(units, outs)
                ]
                dvs = [tn(pr.astype(BF16), d) for pr, d in zip(prob, outs)]
                dots = [jnp.sum(dp * pr, axis=1, keepdims=True) for dp, pr in zip(dps, prob)]
                dss = [(pr * (dp - dot_)).astype(BF16) for pr, dp, dot_ in zip(prob, dps, dots)]
                dqs = [nn(ds, part(1, first, keys)) for (t, first, queries, keys, h), ds in zip(units, dss)]
                dks = [tn(ds, part(0, first, queries)) for (t, first, queries, keys, h), ds in zip(units, dss)]
                for t, (first, queries, keys) in enumerate(tiles):
                    for j, (two, factor) in enumerate(((dqs, 0.125), (dks, 0.125), (dvs, 1.0))):
                        both = two_heads(two[2 * t], two[2 * t + 1])
                        if factor != 1.0:
                            both = both * factor
                        slot_grads[first : first + queries, base + j * local : base + j * local + 128] = both[
                            :queries
                        ].astype(BF16)

    def unsort(n, _):
        cols = pl.ds(pl.multiple_of(n * local, local), local)
        qkv_grad[:, cols] = nn(pick_t[...], slot_grads[:, cols]).astype(BF16)
        return 0

    lax.fori_loop(0, 6, unsort, 0)
    put = pltpu.make_async_copy(qkv_grad, qkv_grad_out, out_sems.at[0])
    put.start()
    gets[4].wait()

    def back(n, _):
        rows = pl.ds(pl.multiple_of(n * 256, 256), 256)
        total = nt(qkv_grad[:, :three], weights[0, rows, :three]) + nt(qkv_grad[:, three:], weights[1, rows, :three])
        keep[:, rows] = total[:half]
        send[:, rows] = total[half:].astype(BF16)
        return 0

    lax.fori_loop(0, weights.shape[1] // 256, back, 0)
    put.wait()


def attend_back(rows_own, rows_oth, slot_row, weights, slots, probs_g, probs_l):
    half, width = rows_own.shape
    local = slots.shape[1] // 6
    shape = jax.ShapeDtypeStruct
    return pl.pallas_call(
        attend_back_kernel,
        out_shape=(
            shape((2 * half, 6 * local), BF16),
            shape((half, width), F32),
            shape((half, width), BF16),
        ),
        in_specs=[vmem()] * 3 + [anywhere()] * 4,
        out_specs=(anywhere(), vmem(), vmem()),
        scratch_shapes=[
            pltpu.VMEM((SLOTS, 2 * half), BF16),
            pltpu.VMEM((2 * half, SLOTS), BF16),
            pltpu.VMEM((2 * half, 2 * local), BF16),
            pltpu.VMEM((SLOTS, 2 * local), BF16),
            pltpu.VMEM((SLOTS, 6 * local), BF16),
            pltpu.VMEM(weights.shape, BF16),
            pltpu.VMEM(slots.shape, BF16),
            pltpu.VMEM(probs_g.shape, F32),
            pltpu.VMEM(probs_l.shape, F32),
            pltpu.VMEM((2 * half, 6 * local), BF16),
            pltpu.SemaphoreType.DMA((5,)),
            pltpu.SemaphoreType.DMA((1,)),
        ],
        compiler_params=pltpu.CompilerParams(vmem_limit_bytes=VMEM_LIMIT),
        cost_estimate=pl.CostEstimate(flops=1000, bytes_accessed=1000, transcendentals=0),
        name="attend_back",
    )(rows_own, rows_oth, slot_row, weights, slots, probs_g, probs_l)


def shards(comm, tokens, cotangent, crop_lengths, qkv_weight, out_weight, up_weight, down_weight, vectors,
           qkv_first, out_first, up_first, down_first, vector_first,
           qkv_second, out_second, up_second, down_second, vector_second):
    rows, width = tokens.shape
    padded = -(-rows // 16) * 16
    block = width // comm.n_dp
    own_index = lax.axis_index("mp")
    image, core = own_index // 2, own_index % 2
    flat_index = lax.axis_index("dp") * comm.n_mp + own_index
    local = qkv_weight.shape[2]
    hidden = up_weight.shape[1]
    order, places = comm.order(), comm.places()
    to_rel = lambda v: take_blocks(v, order, block)
    to_abs = lambda v: take_blocks(v, places, block)

    pack_a = jnp.concatenate([qkv_weight.reshape(-1, 3 * local), out_weight], axis=1).astype(BF16)
    vector_full = lax.dynamic_update_slice(
        jnp.zeros((6, width), F32), vectors.astype(BF16).astype(F32), (0, flat_index * vectors.shape[1])
    ).astype(BF16)
    (a_own, a_oth), up_part, down_part, vector_full = comm.gather_first(
        pack_a, up_weight.astype(BF16), down_weight.astype(BF16), vector_full
    )
    gain_one, shift_one, gain_two, shift_two, scale_one, scale_two = vector_full.astype(F32)
    cat = lambda blocks: jnp.concatenate(blocks, axis=0)
    lengths = lax.dynamic_index_in_dim(crop_lengths, image, 0, keepdims=False)
    lane = jnp.arange(padded, dtype=jnp.int32)
    positions = jnp.concatenate(
        [jnp.where(lane < rows, lane + half * rows, -1) for half in (core, 1 - core)]
    )
    slot = jnp.where(positions >= 0, slots_of(lengths, positions), -1)
    slot_row = slot[None, :]

    residual = tokens.astype(F32)
    normed_one, inverse_one = norm_parts(residual)
    norm_one = pad_rows(to_rel((normed_one * gain_one + shift_one).astype(BF16)), padded)
    norm_one_other = comm.core(norm_one)
    rows_one = cat([norm_one, norm_one_other])
    out_grad = cotangent.astype(F32)
    cot_y = comm.y(after(cotangent, *a_oth[-2:]))
    wide = 3 * local
    weights_a, slots, attended, keep, send, probs_g, probs_l = attend(
        norm_one, norm_one_other, slot_row, a_own, a_oth
    )

    def joined(keep, send):
        return to_abs(keep[:rows] + comm.core(send)[:rows].astype(F32))

    def spread(mine, mate, *first):
        total = mine + comm.core(mate.astype(BF16))
        sent = total[padded:].astype(BF16)
        return total[:padded], sent, comm.y(after(sent, *first))

    if comm.grid:
        send = after(send, *up_part[2:])
    up_blocks, down_blocks = comm.gather_rest(up_part, down_part, send)
    up_full = cat(up_blocks)
    branch_one = joined(keep, send)
    middle = residual + scale_one * branch_one
    normed_two, inverse_two = norm_parts(middle)
    norm_two = pad_rows(to_rel((normed_two * gain_two + shift_two).astype(BF16)), padded)
    norm_two_y = comm.y(norm_two)
    cot_mine = cat([pad_rows(cotangent, padded), pad_rows(cot_y, padded)])
    cot_mine = after(cot_mine, norm_two)
    mlp_mine, mlp_mate = (
        to_rel((v.astype(F32) * scale_two).astype(BF16)) for v in (cot_mine, comm.core(cot_mine))
    )

    two_mine = cat([norm_two, norm_two_y])
    two_mate = comm.core(two_mine)
    if comm.grid:
        two_mate = after(two_mate, up_blocks[4])

    def activate(hidden_pre):
        cdf = 0.5 * (1.0 + lax.erf(hidden_pre * (0.5**0.5)))
        slope = cdf + hidden_pre * jnp.exp(-0.5 * hidden_pre * hidden_pre) * 0.3989422804014327
        return (hidden_pre * cdf).astype(BF16), slope

    act_mine, slope_mine = activate(nn(two_mine, up_full))
    act_mate, slope_mate = activate(nn(two_mate, up_full))
    down_part = lambda g, first, last: tn(mlp_mine[:, first:last], act_mine) + tn(mlp_mate[:, first:last], act_mate)
    if comm.grid:
        down_last, act_mine, act_mate, slope_mine, slope_mate = lax.optimization_barrier(
            (down_blocks[-1], act_mine, act_mate, slope_mine, slope_mate)
        )
        down_blocks = [*down_blocks[:-1], down_last]
    down_full = cat(down_blocks)
    pre_mate = (nn(mlp_mate, down_full) * slope_mate).astype(BF16)
    pre_mine = (nn(mlp_mine, down_full) * slope_mine).astype(BF16)
    down_sums, sent = comm.scatter_x(down_part, width, pre_mine, pre_mate)
    mine, sent_y, from_y = spread(nt(pre_mine, up_full), nt(pre_mate, up_full))
    norm_two_grad = to_abs((mine + from_y)[:rows])
    pre_mine, pre_mate = after((pre_mine, pre_mate), sent_y)
    up_part = lambda g, first, last: tn(two_mine[:, first:last], pre_mine) + tn(two_mate[:, first:last], pre_mate)
    up_sums, sent = comm.scatter_x(up_part, width)
    middle_grad = out_grad + norm_back(normed_two, inverse_two, gain_two, norm_two_grad)
    grad_gain_two = jnp.sum(norm_two_grad * normed_two, axis=0)
    grad_shift_two = jnp.sum(norm_two_grad, axis=0)
    grad_scale_one = jnp.sum(middle_grad * branch_one, axis=0)
    attn_own = pad_rows(to_rel((middle_grad * scale_one).astype(BF16)), padded)
    attn_other = comm.core(attn_own)
    attn_rows = cat([attn_own, attn_other])
    branch_own, branch_mate = after((act_mine, act_mate), sent_y)
    branch_mine, _, branch_y = spread(
        nt(branch_own, down_full).astype(BF16).astype(F32), nt(branch_mate, down_full), from_y
    )

    def out_part(g, first, last):
        return tn(attn_rows[:, first:last], attended[:, g * local : (g + 1) * local])

    out_y = comm.y(out_part(1, 0, width).astype(BF16))

    qkv_grad, keep, send = attend_back(
        attn_own, attn_other, slot_row, weights_a, slots, probs_g, probs_l
    )
    branch_two = to_abs((branch_mine + after(branch_y, send))[:rows])
    output = (middle + scale_two * branch_two).astype(BF16)
    grad_scale_two = jnp.sum(out_grad * branch_two, axis=0)

    def qkv_part(g, first, last):
        return tn(rows_one[:, first:last], qkv_grad[:, g * wide : (g + 1) * wide])

    a_sums, first = comm.scatter_diagonal(qkv_part, width)
    held_mine, held_mate = after((act_mine, act_mate), from_y)
    down_late = lambda g, first, last: tn(mlp_mine[:, first:last], held_mine) + tn(mlp_mate[:, first:last], held_mate)
    down_got, down_rest = comm.scatter_two(down_late, width, down_sums, from_y)
    late_mine, late_mate = after((pre_mine, pre_mate), send)
    up_late = lambda g, first, last: tn(two_mine[:, first:last], late_mine) + tn(two_mate[:, first:last], late_mate)
    up_got, up_rest = comm.scatter_two(up_late, width, up_sums, *first)
    down_share = down_rest(down_got, *first)
    norm_one_grad = joined(keep, send)
    input_grad = (middle_grad + norm_back(normed_one, inverse_one, gain_one, norm_one_grad)).astype(BF16)
    grad_gain_one = jnp.sum(norm_one_grad * normed_one, axis=0)
    grad_shift_one = jnp.sum(norm_one_grad, axis=0)

    vector_grad = jnp.stack(
        [grad_gain_one, grad_shift_one, grad_gain_two, grad_shift_two, grad_scale_one, grad_scale_two]
    )
    bits = [1 << k for k in range(comm.n.bit_length() - 1)]
    vector_grad = comm.total(after(vector_grad, *a_sums), (*bits[3:], bits[0]))
    a_sums, sides = comm.scatter_sides(qkv_part, width, a_sums)
    out_sum = out_part(0, 0, width) + after(out_y, *sides)
    if comm.grid:
        out_sum = comm.fold(out_sum, comm.x)
    else:
        out_sum = lax.psum_scatter(out_sum, "dp", scatter_dimension=0, tiled=True)
    if comm.grid:
        a_sums, up_got, out_sum = lax.optimization_barrier((a_sums, up_got, out_sum))
        out_sum = comm.fold(comm.fold(out_sum, lambda v: comm.z(v, 2)), lambda v: comm.z(v, 1))
    up_share = up_rest(up_got)
    vector_grad = comm.total(after(vector_grad, *a_sums), bits[1:3])
    a_share = comm.scatter_z(qkv_part, width, a_sums)
    vector_share = lax.dynamic_slice_in_dim(
        vector_grad, flat_index * vectors.shape[1], vectors.shape[1], axis=1
    )
    matrix = lambda w, g, m, v: adamw_step(w, g, m, v, matrix_rate, matrix_decay)
    flip = lambda v: jnp.transpose(v, (1, 0, 2))
    up_results = matrix(up_weight, up_share, up_first, up_second)
    if comm.grid:
        a_share, up_results = lax.optimization_barrier((a_share, up_results))
    planes = jnp.stack([a_share[:, k * local : (k + 1) * local] for k in range(3)])
    qkv_results = matrix(flip(qkv_weight), planes, flip(qkv_first), flip(qkv_second))
    return (
        output,
        input_grad,
        *(flip(v) for v in qkv_results),
        *matrix(out_weight, out_sum, out_first, out_second),
        *up_results,
        *matrix(down_weight, down_share, down_first, down_second),
        *adamw_step(vectors, vector_share, vector_first, vector_second, vector_rate, 0.0),
    )


def solution(mesh):
    comm = Comm(mesh.shape["dp"], mesh.shape["mp"])
    rows = P(("dp", "mp"), None)
    cube = P("dp", None, "mp")
    flat = P("dp", "mp")
    vec = P(None, ("dp", "mp"))
    moments = (cube, flat, flat, flat, vec)
    return jax.shard_map(
        lambda *args: shards(comm, *args),
        mesh=mesh,
        in_specs=(rows, rows, P("dp", None), *moments, *moments, *moments),
        out_specs=(rows, rows, *(spec for spec in moments for _ in range(3))),
        check_vma=False,
    )
```
